32 devices in a mesh: tm: 4 (over z), space: 8 (over y, x, core).
Axes of the slice: x: 2, y: 2, z: 4, core: 2. Of those that a mesh axis runs over, the one named last changes fastest.
Arguments:
- starts: float32 [4, 4, 32, 64, 128], P('tm', None, 'space'), may hold values from -46 to 46
- flags: int32 [32, 64, 128], P('space'), may hold values from 0 to 2
Outputs:
- next_states: float32 [4, 4, 32, 64, 128], P('tm', None, 'space')
The draws below stay inside these ranges and needn't reach their ends.
Inputs may be any that keep to these rules, and one draw needn't show every extreme that they name: `flags`: 0 marks a fluid cell, 1 a wall cell, 2 a free-surface cell.
All inputs are finite; a program needn't handle non-finite values.
Results may differ from the reference program's by a relative error of at most 0.0001.
Values sent between devices are 32-bit elements; how exact they have to be, the bound alone decides.
No kernel may reach another device: no remote copies, remote signals or barrier semaphores. Data moves between devices by JAX's collectives and lax.ppermute only.
A program may use at most 64 MiB of HBM per device.

```python
import math
import jax
import jax.numpy as jnp

NY = 64
NZ = 128
FINE_STEPS = 8
COARSE_STEPS = 2
SLICES = 4
NX = 32


def draw_starts(key, part):
    key = jax.random.fold_in(key, 11)
    jitter_key, level_key, phase_key = jax.random.split(key, 3)
    full_shape = (SLICES, 4, NX, NY, NZ)
    jitter = jnp.clip(jax.random.normal(jitter_key, full_shape, jnp.float32), -4.0, 4.0)
    levels = jax.random.uniform(level_key, (SLICES,), jnp.float32, 15.0, 19.0)
    phases = jax.random.uniform(phase_key, (7, SLICES, 1, 1), jnp.float32, -math.pi, math.pi)
    second_index = jnp.arange(NY, dtype=jnp.float32)[None, :, None]
    third_index = jnp.arange(NZ, dtype=jnp.float32)[None, None, :]
    angle_second = 2.0 * math.pi * second_index / NY
    angle_third = 2.0 * math.pi * third_index / NZ
    pattern = 0.45 * jnp.cos(angle_second + phases[0]) + 0.45 * jnp.cos(angle_third + phases[1])
    pattern = pattern + 0.3 * jnp.cos(angle_second + phases[2]) * jnp.cos(2.0 * angle_third + phases[3])
    pattern = pattern + 0.6 * jnp.cos(0.25 * math.pi * second_index + phases[4]) * jnp.cos(0.25 * math.pi * third_index + phases[5])
    pattern = pattern + 0.3 * jnp.cos(0.5 * math.pi * third_index + phases[6])
    parity = jnp.where(jnp.arange(NX) % 2 == 0, 1.0, -1.0).astype(jnp.float32)
    ripple = levels[:, None, None, None] * parity[None, :, None, None] * pattern[:, None, :, :]
    return jnp.concatenate([jitter[:, :3], (jitter[:, 3] + ripple)[:, None]], axis=1)


def touch_ends(array, stream_key, low, top_value):
    spot = [jax.random.randint(jax.random.fold_in(stream_key, axis), (), 0, length) for axis, length in enumerate(array.shape)]
    main_axis = array.shape.index(max(array.shape))
    neighbour = spot[:main_axis] + [(spot[main_axis] + 1) % array.shape[main_axis]] + spot[main_axis + 1:]
    return array.at[tuple(spot)].set(low).at[tuple(neighbour)].set(top_value)


def setup_inputs(seed: int = 0) -> dict:
    splits = jax.random.split(jax.random.key(seed), 3)
    starts = draw_starts(jax.random.fold_in(splits[2], 71), 0)
    flags = touch_ends(jax.random.randint(splits[1], (NX, NY, NZ), 0, 3), jax.random.fold_in(splits[1], 1), 0, 2).astype(jnp.int32)
    return {"starts": starts, "flags": flags}


fine_dt = 0.12
coarse_dt = 0.48
coupling = 0.5


def offset_cut(values, along, offset):
    bounds = [slice(1, -1)] * 3
    bounds[along] = slice(1 + offset, values.shape[along] - 1 + offset)
    return values[tuple(bounds)]


def central(values, along, spacing):
    return (offset_cut(values, along, 1) - offset_cut(values, along, -1)) / (2.0 * spacing)


def laplace(values, spacings, middle):
    total = jnp.zeros_like(middle)
    for along in range(3):
        total = total + (offset_cut(values, along, 1) + offset_cut(values, along, -1) - 2.0 * middle) / (spacings[along] ** 2)
    return total


def advance(padded, keep_velocity, keep_shear, delta, spacings, layout):
    axis_x, axis_y, axis_z = layout
    velocity, shear_x, shear_y, normal = padded[0], padded[1], padded[2], padded[3]
    mids = [offset_cut(padded[k], 0, 0) for k in range(4)]
    grad_x = central(velocity, axis_x, spacings[axis_x])
    grad_y = central(velocity, axis_y, spacings[axis_y])
    grad_z = central(velocity, axis_z, spacings[axis_z])
    diverge = central(shear_x, axis_x, spacings[axis_x]) + central(shear_y, axis_y, spacings[axis_y]) + central(normal, axis_z, spacings[axis_z])
    new_velocity = mids[0] + delta * (laplace(velocity, spacings, mids[0]) + coupling * diverge)
    new_shear_x = mids[1] + delta * (grad_x + mids[1] * grad_z - mids[1] + laplace(shear_x, spacings, mids[1]))
    new_shear_y = mids[2] + delta * (grad_y + mids[2] * grad_z - mids[2] + laplace(shear_y, spacings, mids[2]))
    new_normal = mids[3] + delta * (2.0 * (grad_x * mids[1] + grad_y * mids[2] + grad_z * mids[3]) - (mids[3] - 1.0) + laplace(normal, spacings, mids[3]))
    return jnp.stack([new_velocity * keep_velocity, new_shear_x * keep_shear, new_shear_y * keep_shear, new_normal])


def pad_all(fields):
    return jnp.pad(fields, ((0, 0), (1, 1), (1, 1), (1, 1)))


def fine_run(fields, keep_velocity, keep_shear):
    for _ in range(FINE_STEPS):
        fields = advance(pad_all(fields), keep_velocity, keep_shear, fine_dt, (1.0, 1.0, 1.0), (0, 1, 2))
    return fields


def coarse_run(fields):
    for _ in range(COARSE_STEPS):
        fields = advance(pad_all(fields), 1.0, 1.0, coarse_dt, (2.0, 16.0, 2.0), (0, 2, 1))
    return fields


def restrict(fields):
    count, xs, ys, zs = fields.shape
    blocks = fields.reshape(count, xs // 2, 2, ys // 2, 2, zs // 16, 16)
    return jnp.transpose(jnp.mean(blocks, axis=(2, 4, 6)), (0, 1, 3, 2))


def prolong(coarse, fine_shape):
    count, xs, ys, zs = fine_shape
    grid = jnp.transpose(coarse, (0, 1, 3, 2))
    wide = jnp.broadcast_to(grid[:, :, None, :, None, :, None], (count, xs // 2, 2, ys // 2, 2, zs // 16, 16))
    return wide.reshape(fine_shape)


def reference(starts, flags):
    keep_velocity = (flags != 1).astype(jnp.float32)
    keep_shear = (flags != 2).astype(jnp.float32)
    coarse_now = restrict(starts[0])
    results = []
    for slice_index in range(SLICES):
        opening = starts[slice_index]
        fine_end = fine_run(opening, keep_velocity, keep_shear)
        guess_old = coarse_run(restrict(opening))
        guess_new = coarse_run(coarse_now)
        results.append(fine_end + prolong(guess_new - guess_old, fine_end.shape))
        coarse_now = guess_new + (restrict(fine_end) - guess_old)
    return jnp.stack(results)
```

```python
import functools

import jax
import jax.numpy as jnp
from jax import lax
from jax.experimental import pallas as pl
from jax.experimental.pallas import tpu as pltpu
from jax.sharding import PartitionSpec as P

FINE_STEPS = 8
COARSE_STEPS = 2

fine_dt = 0.12
coarse_dt = 0.48

FIELDS = 4
PLANES = 4
NY = 64
NZ = 128
REACH = FINE_STEPS // PLANES
BLOCKS = 2 * REACH + 1
WINDOW = BLOCKS * PLANES
TOP = 8
CHUNK = 16
F32 = jnp.float32
HIGHEST = lax.Precision.HIGHEST
VMEM = pl.BlockSpec(memory_space=pltpu.VMEM)
ANY = pl.BlockSpec(memory_space=pl.ANY)
LIMIT = 48 * 2**20


def iota(shape, dim):
    return lax.broadcasted_iota(jnp.int32, shape, dim)


def pick_rows(shape):
    return ((iota(shape, 0) % NY) // 2 % 16 == iota(shape, 1) // 8).astype(F32)


def packed_mean(pairs):
    stacked = jnp.concatenate(pairs, axis=0)
    gather = (iota((NZ, NZ), 0) // 16 == iota((NZ, NZ), 1) % 8).astype(F32)
    sums = jnp.dot(stacked, gather, precision=HIGHEST, preferred_element_type=F32)
    sums = sums * pick_rows(sums.shape)
    rows = sums.shape[0] // 32
    return jnp.sum(sums.reshape(rows, 32, NZ), axis=1) * (1.0 / 64.0)


def restrict_kernel(starts, packed):
    pairs = [starts[0, f, 2 * x] + starts[0, f, 2 * x + 1] for f in range(FIELDS) for x in range(PLANES // 2)]
    packed[...] = packed_mean(pairs)


def fine_step(src, keep, plane, store):
    beta = 1.0 / fine_dt - 7.0
    alpha = 1.0 / fine_dt - 6.0
    for r0 in range(0, NY, CHUNK):
        lane = iota((CHUNK, NZ), 1)
        mid, lo_x, hi_x, lo_y, hi_y, lo_z, hi_z = [], [], [], [], [], [], []
        for f in range(FIELDS):
            v = src[f, plane, pl.ds(TOP + r0, CHUNK), :]
            mid.append(v)
            lo_x.append(src[f, plane - 1, pl.ds(TOP + r0, CHUNK), :])
            hi_x.append(src[f, plane + 1, pl.ds(TOP + r0, CHUNK), :])
            lo_y.append(src[f, plane, pl.ds(TOP + r0 - 1, CHUNK), :])
            hi_y.append(src[f, plane, pl.ds(TOP + r0 + 1, CHUNK), :])
            lo_z.append(jnp.where(lane == 0, 0.0, pltpu.roll(v, 1, 1)))
            hi_z.append(jnp.where(lane == NZ - 1, 0.0, pltpu.roll(v, NZ - 1, 1)))
        total = [
            ((lo_x[f] + hi_x[f]) + (lo_y[f] + hi_y[f])) + (lo_z[f] + hi_z[f]) for f in range(FIELDS)
        ]
        w, a, b, c = mid
        gx = hi_x[0] - lo_x[0]
        gy = hi_y[0] - lo_y[0]
        gz = hi_z[0] - lo_z[0]
        diverge = (hi_x[1] - lo_x[1]) + (hi_y[2] - lo_y[2]) + (hi_z[3] - lo_z[3])
        kv = keep[0, plane, pl.ds(r0, CHUNK), :]
        ks = keep[1, plane, pl.ds(r0, CHUNK), :]
        stretch = gz + beta
        new_w = kv * ((total[0] + 0.125 * diverge) + alpha * w)
        new_a = ks * ((total[1] + gx) + a * stretch)
        new_b = ks * ((total[2] + gy) + b * stretch)
        new_c = fine_dt * ((total[3] + 2.0 * (gx * a + gy * b)) + ((stretch + gz) * c + 1.0))
        for f, value in enumerate((new_w, new_a, new_b, new_c)):
            store(f, r0, value)


def fine_kernel(space_size, own, own_flags, near, near_flags, fine_end, packed, even, odd, flags, keep, sems):
    place = lax.axis_index("space")
    gathered = near.shape[0] == space_size

    def in_range(j):
        return (place + (j - REACH) >= 0) & (place + (j - REACH) < space_size)

    def source(j):
        if gathered:
            return jnp.clip(place + (j - REACH), 0, space_size - 1)
        return j

    def copies(j):
        into = even.at[:, pl.ds(j * PLANES, PLANES), pl.ds(TOP, NY), :]
        into_flags = flags.at[pl.ds(j * PLANES, PLANES)]
        if j == REACH:
            return [
                pltpu.make_async_copy(own.at[0], into, sems.at[0, j]),
                pltpu.make_async_copy(own_flags, into_flags, sems.at[1, j]),
            ]
        return [
            pltpu.make_async_copy(near.at[source(j)], into, sems.at[0, j]),
            pltpu.make_async_copy(near_flags.at[source(j)], into_flags, sems.at[1, j]),
        ]

    for j in range(BLOCKS):
        for copy in copies(j):
            copy.start()

    def clear_edges(p, carry):
        for buffer in (even, odd):
            for f in range(FIELDS):
                buffer[f, p, pl.ds(0, TOP), :] = jnp.zeros((TOP, NZ), F32)
                buffer[f, p, pl.ds(TOP + NY, TOP), :] = jnp.zeros((TOP, NZ), F32)
        return carry

    lax.fori_loop(0, WINDOW, clear_edges, 0)
    for j in range(BLOCKS):
        for copy in copies(j):
            copy.wait()
    for j in range(BLOCKS):
        if j == REACH:
            continue

        @pl.when(jnp.logical_not(in_range(j)))
        def _():
            def clear(p, carry):
                for buffer in (even, odd):
                    for f in range(FIELDS):
                        buffer[f, p, pl.ds(TOP, NY), :] = jnp.zeros((NY, NZ), F32)
                return carry

            lax.fori_loop(j * PLANES, (j + 1) * PLANES, clear, 0)

    def prepare(p, carry):
        even[0, p, pl.ds(TOP, NY), :] = even[0, p, pl.ds(TOP, NY), :] * 0.5
        kind = flags[p]
        keep[0, p] = jnp.where(kind != 1, fine_dt, 0.0).astype(F32)
        keep[1, p] = jnp.where(kind != 2, fine_dt, 0.0).astype(F32)
        return carry

    lax.fori_loop(0, WINDOW, prepare, 0)

    first = (REACH - place) * PLANES
    last = (space_size + REACH - place) * PLANES
    for t in range(FINE_STEPS - 1):
        src, dst = (even, odd) if t % 2 == 0 else (odd, even)

        def body(p, carry, src=src, dst=dst):
            def store(f, r0, value):
                dst[f, p, pl.ds(TOP + r0, CHUNK), :] = value

            fine_step(src, keep, p, store)
            return carry

        lax.fori_loop(jnp.maximum(1 + t, first), jnp.minimum(WINDOW - 1 - t, last), body, 0)

    src = even if FINE_STEPS % 2 == 1 else odd
    begin = REACH * PLANES

    def final(p, carry):
        def store(f, r0, value):
            fine_end[f, p - begin, pl.ds(r0, CHUNK), :] = value * 2.0 if f == 0 else value

        fine_step(src, keep, p, store)
        return carry

    lax.fori_loop(begin, begin + PLANES, final, 0)
    pairs = [
        fine_end[f, 2 * x] + fine_end[f, 2 * x + 1] for f in range(FIELDS) for x in range(PLANES // 2)
    ]
    packed[...] = packed_mean(pairs)


def row_shift(v, by):
    rows = v.shape[0]
    row = iota(v.shape, 0)
    rolled = pltpu.roll(v, (-by) % rows, 0)
    return jnp.where((row + by >= 0) & (row + by < rows), rolled, 0.0)


def coarse_neighbours(v):
    row = iota(v.shape, 0)
    lane = iota(v.shape, 1)
    lo_x, hi_x = row_shift(v, -2), row_shift(v, 2)
    up = pltpu.roll(v, NZ - 8, 1)
    hi_y = jnp.where(lane < NZ - 8, up, jnp.where(row % 2 == 0, row_shift(up, 1), 0.0))
    down = pltpu.roll(v, 8, 1)
    lo_y = jnp.where(lane >= 8, down, jnp.where(row % 2 == 1, row_shift(down, -1), 0.0))
    hi_z = jnp.where(lane % 8 == 7, 0.0, pltpu.roll(v, NZ - 1, 1))
    lo_z = jnp.where(lane % 8 == 0, 0.0, pltpu.roll(v, 1, 1))
    return lo_x, hi_x, lo_y, hi_y, lo_z, hi_z


def coarse_step(state):
    near = [coarse_neighbours(v) for v in state]
    w, a, b, c = state

    def lap(f):
        lo_x, hi_x, lo_y, hi_y, lo_z, hi_z = near[f]
        middle = state[f]
        return (
            0.25 * ((lo_x + hi_x) + (lo_y + hi_y)) + (1.0 / 256.0) * (lo_z + hi_z)
        ) - (1.0 + 2.0 / 256.0) * middle

    def grad(f, k):
        return (near[f][2 * k + 1] - near[f][2 * k]) * (1.0 / 32.0 if k == 2 else 0.25)

    gx, gy, gz = grad(0, 0), grad(0, 1), grad(0, 2)
    diverge = grad(1, 0) + grad(2, 1) + grad(3, 2)
    new_w = w + coarse_dt * (lap(0) + 0.5 * diverge)
    new_a = a + coarse_dt * (gx + a * gz - a + lap(1))
    new_b = b + coarse_dt * (gy + b * gz - b + lap(2))
    new_c = c + coarse_dt * (2.0 * (gx * a + gy * b + gz * c) - (c - 1.0) + lap(3))
    return new_w, new_a, new_b, new_c


def coarse_run(state):
    for _ in range(COARSE_STEPS):
        state = coarse_step(state)
    return state


def unpack(packed, grids, count):
    for m in count:
        for s in range(packed.shape[1]):
            for f in range(FIELDS):
                grids[m, f, pl.ds(4 * s, 4), :] = packed[m, s, pl.ds(4 * f, 4), :]


def guess_kernel(packed, guesses, grids):
    slices = packed.shape[0]
    unpack(packed, grids, range(1, slices))
    for m in range(1, slices):
        ended = coarse_run(tuple(grids[m, f] for f in range(FIELDS)))
        for f in range(FIELDS):
            guesses[m, f] = ended[f]


def correct_kernel(packed, guesses, fine_end, out, grids, change):
    slices = packed.shape[0]
    mine = lax.axis_index("tm")
    place = lax.axis_index("space")
    unpack(packed, grids, range(slices - 1))
    state = tuple(grids[0, f] for f in range(FIELDS))
    kept = tuple(jnp.zeros_like(v) for v in state)
    for m in range(1, slices):
        ended = coarse_run(state)
        moved = [ended[f] - guesses[m, f] for f in range(FIELDS)]
        kept = [jnp.where(mine == m, moved[f], kept[f]) for f in range(FIELDS)]
        if m < slices - 1:
            state = tuple(moved[f] + grids[m, f] for f in range(FIELDS))
    for f in range(FIELDS):
        change[f] = kept[f]
    pieces = []
    for f in range(FIELDS):
        for x in range(PLANES // 2):
            for half in range(2):
                line = change[f, pl.ds(4 * place + 2 * x + half, 1), :]
                pieces.append(jnp.broadcast_to(line, (32, NZ)))
    stacked = jnp.concatenate(pieces, axis=0)
    stacked = stacked * pick_rows(stacked.shape)
    spread = (iota((NZ, NZ), 0) % 8 == iota((NZ, NZ), 1) // 16).astype(F32)
    wide = jnp.dot(stacked, spread, precision=HIGHEST, preferred_element_type=F32)
    for f in range(FIELDS):
        for x in range(PLANES // 2):
            k = (f * 2 + x) * NY
            for i in range(2):
                out[0, f, 2 * x + i] = fine_end[f, 2 * x + i] + wide[k : k + NY]


def params():
    return pltpu.CompilerParams(vmem_limit_bytes=LIMIT)


def window(block, axis, size):
    if size <= 8:
        return lax.all_gather(block, axis)
    parts = []
    for j in range(-REACH, REACH + 1):
        if j == 0:
            parts.append(block)
            continue
        route = [(i, i - j) for i in range(size) if 0 <= i - j < size]
        parts.append(lax.ppermute(block, axis, route))
    return jnp.stack(parts)


def local(slices, space_size, starts, flags):
    near = window(starts[0], "space", space_size)
    near_flags = window(flags, "space", space_size)
    packed_shape = jax.ShapeDtypeStruct((FIELDS * 4, NZ), F32)
    begin = pl.pallas_call(
        restrict_kernel, out_shape=packed_shape, in_specs=[VMEM], out_specs=VMEM, compiler_params=params(),
        name="restrict_starts",
    )(starts)
    begin_all = lax.all_gather(begin, ("tm", "space")).reshape(slices, space_size, FIELDS * 4, NZ)

    fine_end, packed = pl.pallas_call(
        functools.partial(fine_kernel, space_size),
        out_shape=(jax.ShapeDtypeStruct((FIELDS, PLANES, NY, NZ), F32), packed_shape),
        in_specs=[ANY] * 4,
        out_specs=(VMEM, VMEM),
        scratch_shapes=[
            pltpu.VMEM((FIELDS, WINDOW, NY + 2 * TOP, NZ), F32),
            pltpu.VMEM((FIELDS, WINDOW, NY + 2 * TOP, NZ), F32),
            pltpu.VMEM((WINDOW, NY, NZ), jnp.int32),
            pltpu.VMEM((2, WINDOW, NY, NZ), F32),
            pltpu.SemaphoreType.DMA((2, BLOCKS)),
        ],
        compiler_params=params(),
        name="fine_steps",
    )(starts, flags, near, near_flags)

    end_all = lax.all_gather(packed, ("tm", "space")).reshape(slices, space_size, FIELDS * 4, NZ)

    grid_shape = (slices, FIELDS, space_size * 4, NZ)
    guesses = pl.pallas_call(
        guess_kernel,
        out_shape=jax.ShapeDtypeStruct(grid_shape, F32),
        in_specs=[VMEM],
        out_specs=VMEM,
        scratch_shapes=[pltpu.VMEM(grid_shape, F32)],
        compiler_params=params(),
        name="guess_old",
    )(begin_all)

    return pl.pallas_call(
        correct_kernel,
        out_shape=jax.ShapeDtypeStruct((1, FIELDS, PLANES, NY, NZ), F32),
        in_specs=[VMEM] * 3,
        out_specs=VMEM,
        scratch_shapes=[pltpu.VMEM(grid_shape, F32), pltpu.VMEM(grid_shape[1:], F32)],
        compiler_params=params(),
        name="correct",
    )(end_all, guesses, fine_end)


def solution(mesh):
    return jax.shard_map(
        functools.partial(local, mesh.shape["tm"], mesh.shape["space"]),
        mesh=mesh,
        in_specs=(P("tm", None, "space", None, None), P("space", None, None)),
        out_specs=P("tm", None, "space", None, None),
        check_vma=False,
    )
```

```python
import functools

import jax
import jax.numpy as jnp
from jax import lax
from jax.experimental import pallas as pl
from jax.experimental.pallas import tpu as pltpu
from jax.sharding import PartitionSpec as P

FINE_STEPS = 8
COARSE_STEPS = 2

fine_dt = 0.12
coarse_dt = 0.48

FIELDS = 4
PLANES = 4
NY = 64
NZ = 128
ROUND = 4
WINDOW = 3 * PLANES
TILES = NY // 8
PACKED = FIELDS * PLANES
F32 = jnp.float32
HIGHEST = lax.Precision.HIGHEST
VMEM = pl.BlockSpec(memory_space=pltpu.VMEM)
LIMIT = 48 * 2**20


def iota(shape, dim):
    return lax.broadcasted_iota(jnp.int32, shape, dim)


def params():
    return pltpu.CompilerParams(vmem_limit_bytes=LIMIT)


def prepare_kernel(starts, flags, sent):
    for f in range(FIELDS):
        for x in range(PLANES):
            for t in range(TILES):
                v = starts[0, f, x, pl.ds(t, 8, stride=8), :]
                sent[f * PLANES + x, t] = v * 0.5 if f == 0 else v
    for x in range(PLANES):
        for t in range(TILES):
            sent[PACKED + x, t] = flags[x, pl.ds(t, 8, stride=8), :].astype(F32)


def fine_plane(src, keep, p, store):
    beta = 1.0 / fine_dt - 7.0
    alpha = 1.0 / fine_dt - 6.0
    lane = iota((8, NZ), 1)
    low_lane, high_lane = lane == 0, lane == NZ - 1
    fields = range(FIELDS)
    lo_y = [src[f, p, 0] for f in fields]
    mid = [src[f, p, 1] for f in fields]
    for t in range(TILES):
        hi_y = [src[f, p, t + 2] for f in fields]
        lo_x = [src[f, p - 1, t + 1] for f in fields]
        hi_x = [src[f, p + 1, t + 1] for f in fields]
        lo_z = [jnp.where(low_lane, 0.0, pltpu.roll(v, 1, 1)) for v in mid]
        hi_z = [jnp.where(high_lane, 0.0, pltpu.roll(v, NZ - 1, 1)) for v in mid]
        total = [((lo_x[f] + hi_x[f]) + (lo_y[f] + hi_y[f])) + (lo_z[f] + hi_z[f]) for f in fields]
        w, a, b, c = mid
        gx = hi_x[0] - lo_x[0]
        gy = hi_y[0] - lo_y[0]
        gz = hi_z[0] - lo_z[0]
        diverge = (hi_x[1] - lo_x[1]) + (hi_y[2] - lo_y[2]) + (hi_z[3] - lo_z[3])
        kv = keep[0, p, t]
        ks = keep[1, p, t]
        stretch = gz + beta
        new_w = kv * ((total[0] + 0.125 * diverge) + alpha * w)
        new_a = ks * ((total[1] + gx) + a * stretch)
        new_b = ks * ((total[2] + gy) + b * stretch)
        new_c = fine_dt * ((total[3] + 2.0 * (gx * a + gy * b)) + ((stretch + gz) * c + 1.0))
        for f, value in enumerate((new_w, new_a, new_b, new_c)):
            store(f, t, value)
        lo_y, mid = mid, hi_y


def put_tile(buffer, f, p, t, value):
    buffer[f, p, t + 1] = value
    row = iota((8, NZ), 0)
    if t == 0:
        buffer[f, p, TILES + 1] = jnp.where(row == 7, 0.0, pltpu.roll(value, 7, 0))
    if t == TILES - 1:
        buffer[f, p, 0] = jnp.where(row == 0, 0.0, pltpu.roll(value, 1, 0))


def fine_round(space_size, place, parts, kinds, even, odd, keep, finish):
    for j, part in enumerate(parts):

        def load(x, carry, j=j, part=part):
            for f in range(FIELDS):
                for t in range(TILES):
                    put_tile(even, f, j * PLANES + x, t, part[f * PLANES + x, t])
            return carry

        lax.fori_loop(0, PLANES, load, 0)

        def convert(x, carry, j=j, kind=kinds[j]):
            v = kind[PACKED + x]
            keep[0, j * PLANES + x] = jnp.where(v != 1.0, fine_dt, 0.0).astype(F32)
            keep[1, j * PLANES + x] = jnp.where(v != 2.0, fine_dt, 0.0).astype(F32)
            return carry

        lax.fori_loop(0, PLANES, convert, 0)

    for edge, outside in ((PLANES - 1, place == 0), (2 * PLANES, place == space_size - 1)):

        @pl.when(outside)
        def _(edge=edge):
            for f in range(FIELDS):
                odd[f, edge] = jnp.zeros((TILES + 2, 8, NZ), F32)

    first = jnp.where(place == 0, PLANES, 0)
    last = jnp.where(place == space_size - 1, 2 * PLANES, WINDOW)
    for step in range(ROUND - 1):
        src, dst = (even, odd) if step % 2 == 0 else (odd, even)

        def body(p, carry, src=src, dst=dst):
            fine_plane(src, keep, p, lambda f, t, value: put_tile(dst, f, p, t, value))
            return carry

        lax.fori_loop(jnp.maximum(1 + step, first), jnp.minimum(WINDOW - 1 - step, last), body, 0)

    src = even if ROUND % 2 == 1 else odd

    def final(p, carry):
        fine_plane(src, keep, p, lambda f, t, value: finish(f, p - PLANES, t, value))
        return carry

    lax.fori_loop(PLANES, 2 * PLANES, final, 0)


def first_kernel(space_size, left, own, right, sent, even, odd, keep):
    parts = (left, own, right)

    def finish(f, x, t, value):
        sent[f * PLANES + x, t] = value

    fine_round(space_size, lax.axis_index("space"), parts, parts, even, odd, keep, finish)


def coarse_rows(pair_of, count):
    pairs = count // 2
    pieces = []
    for k in range(pairs):
        v = pair_of(k)
        for i in range(TILES // 2):
            pieces.append(v[2 * i] + v[2 * i + 1])
    stacked = jnp.concatenate(pieces, axis=0)
    gather = (iota((NZ, NZ), 0) // 16 == iota((NZ, NZ), 1) % 8).astype(F32)
    sums = jnp.dot(stacked, gather, precision=HIGHEST, preferred_element_type=F32)
    sums = sums * pick_rows(sums.shape)
    sums = sums.reshape(pairs, TILES // 2, 8, NZ)
    sums = (sums[:, 0] + sums[:, 1]) + (sums[:, 2] + sums[:, 3])
    return sums.reshape(pairs * 8, NZ)


def pick_rows(shape):
    row = iota(shape, 0)
    return (row % 8 % 4 * 4 + row // 8 % 4 == iota(shape, 1) // 8).astype(F32)


def halves(sums, rows):
    shape = (rows, sums.shape[0])
    add = (iota(shape, 0) == iota(shape, 1) // 4).astype(F32) * (1.0 / 64.0)
    return jnp.dot(add, sums, precision=HIGHEST, preferred_element_type=F32)


def row_shift(v, by):
    rows = v.shape[0]
    row = iota(v.shape, 0)
    rolled = pltpu.roll(v, (-by) % rows, 0)
    return jnp.where((row + by >= 0) & (row + by < rows), rolled, 0.0)


def coarse_neighbours(v):
    row = iota(v.shape, 0)
    lane = iota(v.shape, 1)
    lo_x, hi_x = row_shift(v, -2), row_shift(v, 2)
    up = pltpu.roll(v, NZ - 8, 1)
    hi_y = jnp.where(lane < NZ - 8, up, jnp.where(row % 2 == 0, row_shift(up, 1), 0.0))
    down = pltpu.roll(v, 8, 1)
    lo_y = jnp.where(lane >= 8, down, jnp.where(row % 2 == 1, row_shift(down, -1), 0.0))
    hi_z = jnp.where(lane % 8 == 7, 0.0, pltpu.roll(v, NZ - 1, 1))
    lo_z = jnp.where(lane % 8 == 0, 0.0, pltpu.roll(v, 1, 1))
    return lo_x, hi_x, lo_y, hi_y, lo_z, hi_z


def coarse_step(state):
    near = [coarse_neighbours(v) for v in state]
    w, a, b, c = state

    def lap(f):
        lo_x, hi_x, lo_y, hi_y, lo_z, hi_z = near[f]
        return (0.25 * ((lo_x + hi_x) + (lo_y + hi_y)) + (1.0 / 256.0) * (lo_z + hi_z)) - (1.0 + 2.0 / 256.0) * state[f]

    def grad(f, k):
        return (near[f][2 * k + 1] - near[f][2 * k]) * (1.0 / 32.0 if k == 2 else 0.25)

    gx, gy, gz = grad(0, 0), grad(0, 1), grad(0, 2)
    diverge = grad(1, 0) + grad(2, 1) + grad(3, 2)
    new_w = w + coarse_dt * (lap(0) + 0.5 * diverge)
    new_a = a + coarse_dt * (gx + a * gz - a + lap(1))
    new_b = b + coarse_dt * (gy + b * gz - b + lap(2))
    new_c = c + coarse_dt * (2.0 * (gx * a + gy * b + gz * c) - (c - 1.0) + lap(3))
    return new_w, new_a, new_b, new_c


def guess_kernel(space_size, left, own, right, guess):
    place = lax.axis_index("space")
    parts = (left, own, right)
    rows = 16
    row = iota((rows, NZ), 0)
    plane = 2 * place - 2 + row // 2
    inside = (row < WINDOW) & (plane >= 0) & (plane < 2 * space_size)
    state = []
    for f in range(FIELDS):

        def pair_of(k, f=f):
            part = parts[k // 2]
            x = f * PLANES + k % 2 * 2
            return part[x] + part[x + 1]

        grid = halves(coarse_rows(pair_of, WINDOW), rows)
        state.append(grid * 2.0 if f == 0 else grid)
    for _ in range(COARSE_STEPS):
        state = [jnp.where(inside, v, 0.0) for v in coarse_step(state)]
    for f in range(FIELDS):
        guess[pl.ds(4 * f, 4), :] = state[f][4:8]


def second_kernel(space_size, left, own, right, left_kind, own_kind, right_kind, guess, fine_end, jump, even, odd, keep):
    kinds = (left_kind, own_kind, right_kind)

    def finish(f, x, t, value):
        fine_end[f * PLANES + x, t] = value * 2.0 if f == 0 else value

    fine_round(space_size, lax.axis_index("space"), (left, own, right), kinds, even, odd, keep, finish)
    ended = halves(coarse_rows(lambda k: fine_end[2 * k] + fine_end[2 * k + 1], PACKED), PACKED)
    jumped = ended - jnp.where(lax.axis_index("tm") == 0, 0.0, guess[...])
    for k in range(jump.shape[0]):
        jump[k] = jumped


def correct_kernel(jumps, guess, fine_end, out, grids, change):
    slices, spaces = jumps.shape[:2]
    mine = lax.axis_index("tm")
    place = lax.axis_index("space")
    for m in range(slices - 1):
        for s in range(spaces):
            for f in range(FIELDS):
                grids[m, f, pl.ds(4 * s, 4), :] = jumps[m, s, pl.ds(4 * f, 4), :]
    state = [grids[0, f] for f in range(FIELDS)]
    kept = state
    for m in range(1, slices):
        ended = state
        for _ in range(COARSE_STEPS):
            ended = coarse_step(ended)
        kept = [jnp.where(mine == m, ended[f], kept[f]) for f in range(FIELDS)]
        if m < slices - 1:
            state = [ended[f] + grids[m, f] for f in range(FIELDS)]
    for f in range(FIELDS):
        change[f] = kept[f]
    row = iota((8, NZ), 0)
    pieces = []
    for f in range(FIELDS):
        for x in range(PLANES // 2):
            k = 2 * x
            lines = [
                change[f, pl.ds(4 * place + k + half, 1), :] - guess[pl.ds(4 * f + k + half, 1), :] for half in range(2)
            ]
            tile = jnp.where(row < 4, lines[0], lines[1])
            tile = jnp.where(mine == 0, 0.0, tile)
            pieces += [tile] * (TILES // 2)
    stacked = jnp.concatenate(pieces, axis=0)
    stacked = stacked * pick_rows(stacked.shape)
    spread = (iota((NZ, NZ), 0) % 8 == iota((NZ, NZ), 1) // 16).astype(F32)
    wide = jnp.dot(stacked, spread, precision=HIGHEST, preferred_element_type=F32)
    for f in range(FIELDS):
        for x in range(PLANES):
            for t in range(TILES):
                k = ((f * 2 + x // 2) * (TILES // 2) + t // 2) * 8
                out[0, f, x, pl.ds(t, 8, stride=8), :] = fine_end[f * PLANES + x, t] + wide[k : k + 8]


def neighbours(block, size):
    upward = [(i, i + 1) for i in range(size - 1)]
    downward = [(target, source) for source, target in upward]
    return lax.ppermute(block, "space", upward), lax.ppermute(block, "space", downward)


def shaped(*shape):
    return jax.ShapeDtypeStruct(shape, F32)


def local(slices, space_size, starts, flags):
    fine_scratch = [
        pltpu.VMEM((FIELDS, WINDOW, TILES + 2, 8, NZ), F32),
        pltpu.VMEM((FIELDS, WINDOW, TILES + 2, 8, NZ), F32),
        pltpu.VMEM((2, WINDOW, TILES, 8, NZ), F32),
    ]
    opening = pl.pallas_call(
        prepare_kernel,
        out_shape=shaped(PACKED + PLANES, TILES, 8, NZ),
        in_specs=[VMEM] * 2,
        out_specs=VMEM,
        compiler_params=params(),
        name="prepare",
    )(starts, flags)
    left, right = neighbours(opening, space_size)
    middle = pl.pallas_call(
        functools.partial(first_kernel, space_size),
        out_shape=shaped(PACKED, TILES, 8, NZ),
        in_specs=[VMEM] * 3,
        out_specs=VMEM,
        scratch_shapes=fine_scratch,
        compiler_params=params(),
        name="first_round",
    )(left, opening, right)
    middle_left, middle_right = neighbours(middle, space_size)
    guess = pl.pallas_call(
        functools.partial(guess_kernel, space_size),
        out_shape=shaped(PACKED, NZ),
        in_specs=[VMEM] * 3,
        out_specs=VMEM,
        compiler_params=params(),
        name="guess_old",
    )(left, opening, right)
    fine_end, jump = pl.pallas_call(
        functools.partial(second_kernel, space_size),
        out_shape=(shaped(PACKED, TILES, 8, NZ), shaped(slices * space_size, PACKED, NZ)),
        in_specs=[VMEM] * 7,
        out_specs=(VMEM, VMEM),
        scratch_shapes=fine_scratch,
        compiler_params=params(),
        name="second_round",
    )(middle_left, middle, middle_right, left, opening, right, guess)
    jumps = lax.all_to_all(jump, ("tm", "space"), 0, 0)
    jumps = jumps.reshape(slices, space_size, PACKED, NZ)
    return pl.pallas_call(
        correct_kernel,
        out_shape=shaped(1, FIELDS, PLANES, NY, NZ),
        in_specs=[VMEM] * 3,
        out_specs=VMEM,
        scratch_shapes=[
            pltpu.VMEM((slices, FIELDS, space_size * 4, NZ), F32),
            pltpu.VMEM((FIELDS, space_size * 4, NZ), F32),
        ],
        compiler_params=params(),
        name="correct",
    )(jumps, guess, fine_end)


def solution(mesh):
    return jax.shard_map(
        functools.partial(local, mesh.shape["tm"], mesh.shape["space"]),
        mesh=mesh,
        in_specs=(P("tm", None, "space", None, None), P("space", None, None)),
        out_specs=P("tm", None, "space", None, None),
        check_vma=False,
    )
```

```python
import functools

import jax
import jax.numpy as jnp
from jax import lax
from jax.experimental import pallas as pl
from jax.experimental.pallas import tpu as pltpu
from jax.sharding import PartitionSpec as P

FINE_STEPS = 8
COARSE_STEPS = 2

fine_dt = 0.12
coarse_dt = 0.48

FIELDS = 4
PLANES = 4
NY = 64
NZ = 128
ROUND = 4
WINDOW = 3 * PLANES
TILES = NY // 8
GROUP = 4
PACKED = FIELDS * PLANES
F32 = jnp.float32
HIGHEST = lax.Precision.HIGHEST
VMEM = pl.BlockSpec(memory_space=pltpu.VMEM)
LIMIT = 48 * 2**20


def iota(shape, dim):
    return lax.broadcasted_iota(jnp.int32, shape, dim)


def params():
    return pltpu.CompilerParams(vmem_limit_bytes=LIMIT)


def prepare_kernel(starts, flags, sent):
    for f in range(FIELDS):
        for x in range(PLANES):
            for t in range(TILES):
                v = starts[0, f, x, pl.ds(t, 8, stride=8), :]
                sent[f * PLANES + x, t] = v * 0.5 if f == 0 else v
    for x in range(PLANES):
        for t in range(TILES):
            sent[PACKED + x, t] = flags[x, pl.ds(t, 8, stride=8), :].astype(F32)


def fine_tile(mid, lo_x, hi_x, lo_y, hi_y, kv, ks, low_lane, high_lane):
    beta = 1.0 / fine_dt - 7.0
    alpha = 1.0 / fine_dt - 6.0
    lo_z = [jnp.where(low_lane, 0.0, pltpu.roll(v, 1, 1)) for v in mid]
    hi_z = [jnp.where(high_lane, 0.0, pltpu.roll(v, NZ - 1, 1)) for v in mid]
    total = [((lo_x[f] + hi_x[f]) + (lo_y[f] + hi_y[f])) + (lo_z[f] + hi_z[f]) for f in range(FIELDS)]
    w, a, b, c = mid
    gx = hi_x[0] - lo_x[0]
    gy = hi_y[0] - lo_y[0]
    gz = hi_z[0] - lo_z[0]
    diverge = (hi_x[1] - lo_x[1]) + (hi_y[2] - lo_y[2]) + (hi_z[3] - lo_z[3])
    stretch = gz + beta
    new_w = kv * ((total[0] + 0.125 * diverge) + alpha * w)
    new_a = ks * ((total[1] + gx) + a * stretch)
    new_b = ks * ((total[2] + gy) + b * stretch)
    new_c = fine_dt * ((total[3] + 2.0 * (gx * a + gy * b)) + ((stretch + gz) * c + 1.0))
    return new_w, new_a, new_b, new_c


def fine_plane(src, keep, p, store):
    lane = iota((8, NZ), 1)
    low_lane, high_lane = lane == 0, lane == NZ - 1
    fields = range(FIELDS)
    for begin in range(0, TILES, GROUP):
        tiles = range(begin, begin + GROUP)
        column = [[src[f, p, t] for f in fields] for t in range(begin, begin + GROUP + 2)]
        lo_x = [[src[f, p - 1, t + 1] for f in fields] for t in tiles]
        hi_x = [[src[f, p + 1, t + 1] for f in fields] for t in tiles]
        kept = [(keep[0, p, t], keep[1, p, t]) for t in tiles]
        fresh = [
            fine_tile(column[i + 1], lo_x[i], hi_x[i], column[i], column[i + 2], *kept[i], low_lane, high_lane)
            for i in range(GROUP)
        ]
        for i, t in enumerate(tiles):
            for f in fields:
                store(f, t, fresh[i][f])


def put_tile(buffer, f, p, t, value):
    buffer[f, p, t + 1] = value
    row = iota((8, NZ), 0)
    if t == 0:
        buffer[f, p, TILES + 1] = jnp.where(row == 7, 0.0, pltpu.roll(value, 7, 0))
    if t == TILES - 1:
        buffer[f, p, 0] = jnp.where(row == 0, 0.0, pltpu.roll(value, 1, 0))


def fine_round(space_size, place, parts, kinds, even, odd, keep, finish):
    for j, part in enumerate(parts):

        def load(x, carry, j=j, part=part):
            for f in range(FIELDS):
                for t in range(TILES):
                    put_tile(even, f, j * PLANES + x, t, part[f * PLANES + x, t])
            return carry

        lax.fori_loop(0, PLANES, load, 0)

        def convert(x, carry, j=j, kind=kinds[j]):
            v = kind[PACKED + x]
            keep[0, j * PLANES + x] = jnp.where(v != 1.0, fine_dt, 0.0).astype(F32)
            keep[1, j * PLANES + x] = jnp.where(v != 2.0, fine_dt, 0.0).astype(F32)
            return carry

        lax.fori_loop(0, PLANES, convert, 0)

    for edge, outside in ((PLANES - 1, place == 0), (2 * PLANES, place == space_size - 1)):

        @pl.when(outside)
        def _(edge=edge):
            for f in range(FIELDS):
                odd[f, edge] = jnp.zeros((TILES + 2, 8, NZ), F32)

    first = jnp.where(place == 0, PLANES, 0)
    last = jnp.where(place == space_size - 1, 2 * PLANES, WINDOW)
    for step in range(ROUND - 1):
        src, dst = (even, odd) if step % 2 == 0 else (odd, even)

        def body(p, carry, src=src, dst=dst):
            fine_plane(src, keep, p, lambda f, t, value: put_tile(dst, f, p, t, value))
            return carry

        lax.fori_loop(jnp.maximum(1 + step, first), jnp.minimum(WINDOW - 1 - step, last), body, 0)

    src = even if ROUND % 2 == 1 else odd

    def final(p, carry):
        fine_plane(src, keep, p, lambda f, t, value: finish(f, p - PLANES, t, value))
        return carry

    lax.fori_loop(PLANES, 2 * PLANES, final, 0)


def first_kernel(space_size, left, own, right, sent, even, odd, keep):
    parts = (left, own, right)

    def finish(f, x, t, value):
        sent[f * PLANES + x, t] = value

    fine_round(space_size, lax.axis_index("space"), parts, parts, even, odd, keep, finish)


def coarse_rows(pair_of, count):
    pairs = count // 2
    pieces = []
    for k in range(pairs):
        v = pair_of(k)
        for i in range(TILES // 2):
            pieces.append(v[2 * i] + v[2 * i + 1])
    stacked = jnp.concatenate(pieces, axis=0)
    gather = (iota((NZ, NZ), 0) // 16 == iota((NZ, NZ), 1) % 8).astype(F32)
    sums = jnp.dot(stacked, gather, precision=HIGHEST, preferred_element_type=F32)
    sums = sums * pick_rows(sums.shape)
    sums = sums.reshape(pairs, TILES // 2, 8, NZ)
    sums = (sums[:, 0] + sums[:, 1]) + (sums[:, 2] + sums[:, 3])
    return sums.reshape(pairs * 8, NZ)


def pick_rows(shape):
    row = iota(shape, 0)
    return (row % 8 % 4 * 4 + row // 8 % 4 == iota(shape, 1) // 8).astype(F32)


def halves(sums, rows):
    shape = (rows, sums.shape[0])
    add = (iota(shape, 0) == iota(shape, 1) // 4).astype(F32) * (1.0 / 64.0)
    return jnp.dot(add, sums, precision=HIGHEST, preferred_element_type=F32)


def row_shift(v, by):
    rows = v.shape[0]
    row = iota(v.shape, 0)
    rolled = pltpu.roll(v, (-by) % rows, 0)
    return jnp.where((row + by >= 0) & (row + by < rows), rolled, 0.0)


def coarse_neighbours(v):
    row = iota(v.shape, 0)
    lane = iota(v.shape, 1)
    lo_x, hi_x = row_shift(v, -2), row_shift(v, 2)
    up = pltpu.roll(v, NZ - 8, 1)
    hi_y = jnp.where(lane < NZ - 8, up, jnp.where(row % 2 == 0, row_shift(up, 1), 0.0))
    down = pltpu.roll(v, 8, 1)
    lo_y = jnp.where(lane >= 8, down, jnp.where(row % 2 == 1, row_shift(down, -1), 0.0))
    hi_z = jnp.where(lane % 8 == 7, 0.0, pltpu.roll(v, NZ - 1, 1))
    lo_z = jnp.where(lane % 8 == 0, 0.0, pltpu.roll(v, 1, 1))
    return lo_x, hi_x, lo_y, hi_y, lo_z, hi_z


def coarse_step(state):
    near = [coarse_neighbours(v) for v in state]
    w, a, b, c = state

    def lap(f):
        lo_x, hi_x, lo_y, hi_y, lo_z, hi_z = near[f]
        return (0.25 * ((lo_x + hi_x) + (lo_y + hi_y)) + (1.0 / 256.0) * (lo_z + hi_z)) - (1.0 + 2.0 / 256.0) * state[f]

    def grad(f, k):
        return (near[f][2 * k + 1] - near[f][2 * k]) * (1.0 / 32.0 if k == 2 else 0.25)

    gx, gy, gz = grad(0, 0), grad(0, 1), grad(0, 2)
    diverge = grad(1, 0) + grad(2, 1) + grad(3, 2)
    new_w = w + coarse_dt * (lap(0) + 0.5 * diverge)
    new_a = a + coarse_dt * (gx + a * gz - a + lap(1))
    new_b = b + coarse_dt * (gy + b * gz - b + lap(2))
    new_c = c + coarse_dt * (2.0 * (gx * a + gy * b + gz * c) - (c - 1.0) + lap(3))
    return new_w, new_a, new_b, new_c


def guess_kernel(space_size, left, own, right, guess):
    place = lax.axis_index("space")
    parts = (left, own, right)
    rows = 16
    row = iota((rows, NZ), 0)
    plane = 2 * place - 2 + row // 2
    inside = (row < WINDOW) & (plane >= 0) & (plane < 2 * space_size)
    state = []
    for f in range(FIELDS):

        def pair_of(k, f=f):
            part = parts[k // 2]
            x = f * PLANES + k % 2 * 2
            return part[x] + part[x + 1]

        grid = halves(coarse_rows(pair_of, WINDOW), rows)
        state.append(grid * 2.0 if f == 0 else grid)
    for _ in range(COARSE_STEPS):
        state = [jnp.where(inside, v, 0.0) for v in coarse_step(state)]
    for f in range(FIELDS):
        guess[pl.ds(4 * f, 4), :] = state[f][4:8]


def second_kernel(space_size, left, own, right, left_kind, own_kind, right_kind, guess, fine_end, jump, even, odd, keep):
    kinds = (left_kind, own_kind, right_kind)

    def finish(f, x, t, value):
        fine_end[f * PLANES + x, t] = value * 2.0 if f == 0 else value

    fine_round(space_size, lax.axis_index("space"), (left, own, right), kinds, even, odd, keep, finish)
    ended = halves(coarse_rows(lambda k: fine_end[2 * k] + fine_end[2 * k + 1], PACKED), PACKED)
    jumped = ended - jnp.where(lax.axis_index("tm") == 0, 0.0, guess[...])
    for k in range(jump.shape[0]):
        jump[k] = jumped


def repeat_kernel(jumps, repeated):
    for k in range(repeated.shape[0]):
        repeated[k] = jumps[pl.ds(0, repeated.shape[1])]


def correct_kernel(jumps, guess, fine_end, out, grids, change):
    spaces, slices = jumps.shape[0], jumps.shape[1] + 1
    mine = lax.axis_index("tm")
    place = lax.axis_index("space")
    for m in range(slices - 1):
        for s in range(spaces):
            for f in range(FIELDS):
                grids[m, f, pl.ds(4 * s, 4), :] = jumps[s, m, pl.ds(4 * f, 4), :]
    state = [grids[0, f] for f in range(FIELDS)]
    kept = state
    for m in range(1, slices):
        ended = state
        for _ in range(COARSE_STEPS):
            ended = coarse_step(ended)
        kept = [jnp.where(mine == m, ended[f], kept[f]) for f in range(FIELDS)]
        if m < slices - 1:
            state = [ended[f] + grids[m, f] for f in range(FIELDS)]
    for f in range(FIELDS):
        change[f] = kept[f]
    row = iota((8, NZ), 0)
    pieces = []
    for f in range(FIELDS):
        for x in range(PLANES // 2):
            k = 2 * x
            lines = [
                change[f, pl.ds(4 * place + k + half, 1), :] - guess[pl.ds(4 * f + k + half, 1), :] for half in range(2)
            ]
            tile = jnp.where(row < 4, lines[0], lines[1])
            tile = jnp.where(mine == 0, 0.0, tile)
            pieces += [tile] * (TILES // 2)
    stacked = jnp.concatenate(pieces, axis=0)
    stacked = stacked * pick_rows(stacked.shape)
    spread = (iota((NZ, NZ), 0) % 8 == iota((NZ, NZ), 1) // 16).astype(F32)
    wide = jnp.dot(stacked, spread, precision=HIGHEST, preferred_element_type=F32)
    for f in range(FIELDS):
        for x in range(PLANES):
            for t in range(TILES):
                k = ((f * 2 + x // 2) * (TILES // 2) + t // 2) * 8
                out[0, f, x, pl.ds(t, 8, stride=8), :] = fine_end[f * PLANES + x, t] + wide[k : k + 8]


def neighbours(block, size):
    upward = [(i, i + 1) for i in range(size - 1)]
    downward = [(target, source) for source, target in upward]
    return lax.ppermute(block, "space", upward), lax.ppermute(block, "space", downward)


def shaped(*shape):
    return jax.ShapeDtypeStruct(shape, F32)


def local(slices, space_size, starts, flags):
    fine_scratch = [
        pltpu.VMEM((FIELDS, WINDOW, TILES + 2, 8, NZ), F32),
        pltpu.VMEM((FIELDS, WINDOW, TILES + 2, 8, NZ), F32),
        pltpu.VMEM((2, WINDOW, TILES, 8, NZ), F32),
    ]
    opening = pl.pallas_call(
        prepare_kernel,
        out_shape=shaped(PACKED + PLANES, TILES, 8, NZ),
        in_specs=[VMEM] * 2,
        out_specs=VMEM,
        compiler_params=params(),
        name="prepare",
    )(starts, flags)
    left, right = neighbours(opening, space_size)
    middle = pl.pallas_call(
        functools.partial(first_kernel, space_size),
        out_shape=shaped(PACKED, TILES, 8, NZ),
        in_specs=[VMEM] * 3,
        out_specs=VMEM,
        scratch_shapes=fine_scratch,
        compiler_params=params(),
        name="first_round",
    )(left, opening, right)
    middle_left, middle_right = neighbours(middle, space_size)
    guess = pl.pallas_call(
        functools.partial(guess_kernel, space_size),
        out_shape=shaped(PACKED, NZ),
        in_specs=[VMEM] * 3,
        out_specs=VMEM,
        compiler_params=params(),
        name="guess_old",
    )(left, opening, right)
    fine_end, jump = pl.pallas_call(
        functools.partial(second_kernel, space_size),
        out_shape=(shaped(PACKED, TILES, 8, NZ), shaped(slices, PACKED, NZ)),
        in_specs=[VMEM] * 7,
        out_specs=(VMEM, VMEM),
        scratch_shapes=fine_scratch,
        compiler_params=params(),
        name="second_round",
    )(middle_left, middle, middle_right, left, opening, right, guess)
    earlier = lax.all_to_all(jump, "tm", 0, 0)
    earlier = pl.pallas_call(
        repeat_kernel,
        out_shape=shaped(space_size, slices - 1, PACKED, NZ),
        in_specs=[VMEM],
        out_specs=VMEM,
        compiler_params=params(),
        name="repeat",
    )(earlier)
    jumps = lax.all_to_all(earlier, "space", 0, 0)
    return pl.pallas_call(
        correct_kernel,
        out_shape=shaped(1, FIELDS, PLANES, NY, NZ),
        in_specs=[VMEM] * 3,
        out_specs=VMEM,
        scratch_shapes=[
            pltpu.VMEM((slices, FIELDS, space_size * 4, NZ), F32),
            pltpu.VMEM((FIELDS, space_size * 4, NZ), F32),
        ],
        compiler_params=params(),
        name="correct",
    )(jumps, guess, fine_end)


def solution(mesh):
    return jax.shard_map(
        functools.partial(local, mesh.shape["tm"], mesh.shape["space"]),
        mesh=mesh,
        in_specs=(P("tm", None, "space", None, None), P("space", None, None)),
        out_specs=P("tm", None, "space", None, None),
        check_vma=False,
    )
```

```python
import functools

import jax
import jax.numpy as jnp
from jax import lax
from jax.experimental import pallas as pl
from jax.experimental.pallas import tpu as pltpu
from jax.sharding import PartitionSpec as P

FINE_STEPS = 8
COARSE_STEPS = 2

fine_dt = 0.12
coarse_dt = 0.48

FIELDS = 4
PLANES = 4
NY = 64
NZ = 128
ROUND = 4
WINDOW = 3 * PLANES
TILES = NY // 8
GROUP = 4
PACKED = FIELDS * PLANES
F32 = jnp.float32
HIGHEST = lax.Precision.HIGHEST
VMEM = pl.BlockSpec(memory_space=pltpu.VMEM)
LIMIT = 48 * 2**20


def iota(shape, dim):
    return lax.broadcasted_iota(jnp.int32, shape, dim)


def params():
    return pltpu.CompilerParams(vmem_limit_bytes=LIMIT)


def prepare_kernel(starts, flags, tiles, kinds):
    own = natural(starts)
    for f in range(FIELDS):
        for x in range(PLANES):
            for t in range(TILES):
                tiles[f * PLANES + x, t] = own(f, x, t)
    for x in range(PLANES):
        for t in range(TILES):
            kinds[x, pl.ds(8 * t, 8), :] = flags[x, pl.ds(t, 8, stride=8), :]


def fine_tile(mid, lo_x, hi_x, lo_y, hi_y, kv, ks, kc, low_lane, high_lane):
    beta = 1.0 / fine_dt - 7.0
    alpha = 1.0 / fine_dt - 6.0
    lo_z = [jnp.where(low_lane, 0.0, pltpu.roll(v, 1, 1)) for v in mid]
    hi_z = [jnp.where(high_lane, 0.0, pltpu.roll(v, NZ - 1, 1)) for v in mid]
    total = [((lo_x[f] + hi_x[f]) + (lo_y[f] + hi_y[f])) + (lo_z[f] + hi_z[f]) for f in range(FIELDS)]
    w, a, b, c = mid
    gx = hi_x[0] - lo_x[0]
    gy = hi_y[0] - lo_y[0]
    gz = hi_z[0] - lo_z[0]
    diverge = (hi_x[1] - lo_x[1]) + (hi_y[2] - lo_y[2]) + (hi_z[3] - lo_z[3])
    stretch = gz + beta
    new_w = kv * ((total[0] + 0.125 * diverge) + alpha * w)
    new_a = ks * ((total[1] + gx) + a * stretch)
    new_b = ks * ((total[2] + gy) + b * stretch)
    new_c = kc * ((total[3] + 2.0 * (gx * a + gy * b)) + ((stretch + gz) * c + 1.0))
    return new_w, new_a, new_b, new_c


def fine_plane(src, keep, p, inside, store):
    lane = iota((8, NZ), 1)
    low_lane, high_lane = lane == 0, lane == NZ - 1
    fields = range(FIELDS)
    kc = jnp.where(inside(p), fine_dt, 0.0).astype(F32)
    for begin in range(0, TILES, GROUP):
        tiles = range(begin, begin + GROUP)
        column = [[src[f, p, t] for f in fields] for t in range(begin, begin + GROUP + 2)]
        lo_x = [[src[f, p - 1, t + 1] for f in fields] for t in tiles]
        hi_x = [[src[f, p + 1, t + 1] for f in fields] for t in tiles]
        kept = [(keep[0, p, t], keep[1, p, t]) for t in tiles]
        fresh = [
            fine_tile(column[i + 1], lo_x[i], hi_x[i], column[i], column[i + 2], *kept[i], kc, low_lane, high_lane)
            for i in range(GROUP)
        ]
        for i, t in enumerate(tiles):
            for f in fields:
                store(f, t, fresh[i][f])


def put_tile(buffer, f, p, t, value):
    buffer[f, p, t + 1] = value
    row = iota((8, NZ), 0)
    if t == 0:
        buffer[f, p, TILES + 1] = jnp.where(row == 7, 0.0, pltpu.roll(value, 7, 0))
    if t == TILES - 1:
        buffer[f, p, 0] = jnp.where(row == 0, 0.0, pltpu.roll(value, 1, 0))


def fine_round(space_size, parts, kinds, even, odd, keep, planes_at_once, finish):
    place = lax.axis_index("space")

    def inside(p):
        x = (place - 1) * PLANES + p
        return (x >= 0) & (x < space_size * PLANES)

    for j in range(3):

        def load(x, carry, j=j):
            p = j * PLANES + x
            for f in range(FIELDS):
                for t in range(TILES):
                    put_tile(even, f, p, t, parts[j](f, x, t))
            scale = jnp.where(inside(p), fine_dt, 0.0).astype(F32)
            for t in range(TILES):
                kind = kinds[j][x, pl.ds(8 * t, 8), :] if j == 1 else kinds[j][x, pl.ds(t, 8, stride=8), :]
                keep[0, p, t] = jnp.where(kind != 1, scale, 0.0)
                keep[1, p, t] = jnp.where(kind != 2, scale, 0.0)
            return carry

        lax.fori_loop(0, PLANES, load, 0)

    for step in range(ROUND):
        src, dst = (even, odd) if step % 2 == 0 else (odd, even)
        count = WINDOW - 2 * (step + 1)
        many = planes_at_once(count)

        def body(i, carry, src=src, dst=dst, first=step + 1, many=many):
            for k in range(many):
                p = first + i * many + k
                if first == ROUND:
                    store = lambda f, t, value: finish(f, p - PLANES, t, value)
                else:
                    store = lambda f, t, value: put_tile(dst, f, p, t, value)
                fine_plane(src, keep, p, inside, store)
            return carry

        lax.fori_loop(0, count // many, body, 0)


def natural(part):
    def tile(f, x, t):
        v = part[0, f, x, pl.ds(t, 8, stride=8), :]
        return v * 0.5 if f == 0 else v

    return tile


def tiled(part):
    return lambda f, x, t: part[f * PLANES + x, t]


def first_kernel(space_size, left, own, right, left_kind, own_kind, right_kind, ended, even, odd, keep):
    def finish(f, x, t, value):
        ended[f * PLANES + x, t] = value

    parts = [natural(left), tiled(own), natural(right)]
    fine_round(space_size, parts, (left_kind, own_kind, right_kind), even, odd, keep, lambda count: 2, finish)


def coarse_rows(pair_of, count):
    pairs = count // 2
    pieces = []
    for k in range(pairs):
        for i in range(TILES // 2):
            pieces.append(pair_of(k, 2 * i) + pair_of(k, 2 * i + 1))
    stacked = jnp.concatenate(pieces, axis=0)
    gather = (iota((NZ, NZ), 0) // 16 == iota((NZ, NZ), 1) % 8).astype(F32)
    sums = jnp.dot(stacked, gather, precision=HIGHEST, preferred_element_type=F32)
    sums = sums * pick_rows(sums.shape)
    sums = sums.reshape(pairs, TILES // 2, 8, NZ)
    sums = (sums[:, 0] + sums[:, 1]) + (sums[:, 2] + sums[:, 3])
    return sums.reshape(pairs * 8, NZ)


def pick_rows(shape):
    row = iota(shape, 0)
    return (row % 8 % 4 * 4 + row // 8 % 4 == iota(shape, 1) // 8).astype(F32)


def halves(sums, rows):
    shape = (rows, sums.shape[0])
    add = (iota(shape, 0) == iota(shape, 1) // 4).astype(F32) * (1.0 / 64.0)
    return jnp.dot(add, sums, precision=HIGHEST, preferred_element_type=F32)


def row_shift(v, by):
    rows = v.shape[0]
    row = iota(v.shape, 0)
    rolled = pltpu.roll(v, (-by) % rows, 0)
    return jnp.where((row + by >= 0) & (row + by < rows), rolled, 0.0)


def coarse_neighbours(v):
    row = iota(v.shape, 0)
    lane = iota(v.shape, 1)
    lo_x, hi_x = row_shift(v, -2), row_shift(v, 2)
    up = pltpu.roll(v, NZ - 8, 1)
    hi_y = jnp.where(lane < NZ - 8, up, jnp.where(row % 2 == 0, row_shift(up, 1), 0.0))
    down = pltpu.roll(v, 8, 1)
    lo_y = jnp.where(lane >= 8, down, jnp.where(row % 2 == 1, row_shift(down, -1), 0.0))
    hi_z = jnp.where(lane % 8 == 7, 0.0, pltpu.roll(v, NZ - 1, 1))
    lo_z = jnp.where(lane % 8 == 0, 0.0, pltpu.roll(v, 1, 1))
    return lo_x, hi_x, lo_y, hi_y, lo_z, hi_z


def coarse_step(state):
    near = [coarse_neighbours(v) for v in state]
    w, a, b, c = state

    def lap(f):
        lo_x, hi_x, lo_y, hi_y, lo_z, hi_z = near[f]
        return (0.25 * ((lo_x + hi_x) + (lo_y + hi_y)) + (1.0 / 256.0) * (lo_z + hi_z)) - (1.0 + 2.0 / 256.0) * state[f]

    def grad(f, k):
        return (near[f][2 * k + 1] - near[f][2 * k]) * (1.0 / 32.0 if k == 2 else 0.25)

    gx, gy, gz = grad(0, 0), grad(0, 1), grad(0, 2)
    diverge = grad(1, 0) + grad(2, 1) + grad(3, 2)
    new_w = w + coarse_dt * (lap(0) + 0.5 * diverge)
    new_a = a + coarse_dt * (gx + a * gz - a + lap(1))
    new_b = b + coarse_dt * (gy + b * gz - b + lap(2))
    new_c = c + coarse_dt * (2.0 * (gx * a + gy * b + gz * c) - (c - 1.0) + lap(3))
    return new_w, new_a, new_b, new_c


def guess_kernel(space_size, left, own, right, guess):
    place = lax.axis_index("space")
    parts = [natural(left), tiled(own), natural(right)]
    rows = 16
    row = iota((rows, NZ), 0)
    plane = 2 * place - 2 + row // 2
    inside = (row < WINDOW) & (plane >= 0) & (plane < 2 * space_size)
    state = []
    for f in range(FIELDS):

        def pair_of(k, t, f=f):
            return parts[k // 2](f, k % 2 * 2, t) + parts[k // 2](f, k % 2 * 2 + 1, t)

        grid = halves(coarse_rows(pair_of, WINDOW), rows)
        state.append(grid * 2.0 if f == 0 else grid)
    for _ in range(COARSE_STEPS):
        state = [jnp.where(inside, v, 0.0) for v in coarse_step(state)]
    for f in range(FIELDS):
        guess[pl.ds(4 * f, 4), :] = state[f][4:8]


def second_kernel(space_size, left, own, right, left_kind, own_kind, right_kind, guess, fine_end, jump, even, odd, keep):
    kinds = (left_kind, own_kind, right_kind)
    parts = [tiled(part) for part in (left, own, right)]

    def finish(f, x, t, value):
        fine_end[f * PLANES + x, t] = value * 2.0 if f == 0 else value

    fine_round(space_size, parts, kinds, even, odd, keep, lambda count: count // 2, finish)
    ended = halves(coarse_rows(lambda k, t: fine_end[2 * k, t] + fine_end[2 * k + 1, t], PACKED), PACKED)
    jumped = ended - jnp.where(lax.axis_index("tm") == 0, 0.0, guess[...])
    for k in range(jump.shape[0]):
        jump[k] = jumped


def correct_kernel(jumps, guess, fine_end, out, grids, change):
    slices, spaces = jumps.shape[:2]
    mine = lax.axis_index("tm")
    place = lax.axis_index("space")
    for m in range(slices - 1):
        for s in range(spaces):
            for f in range(FIELDS):
                grids[m, f, pl.ds(4 * s, 4), :] = jumps[m, s, pl.ds(4 * f, 4), :]
    state = [grids[0, f] for f in range(FIELDS)]
    kept = state
    for m in range(1, slices):
        ended = state
        for _ in range(COARSE_STEPS):
            ended = coarse_step(ended)
        kept = [jnp.where(mine == m, ended[f], kept[f]) for f in range(FIELDS)]
        if m < slices - 1:
            state = [ended[f] + grids[m, f] for f in range(FIELDS)]
    for f in range(FIELDS):
        change[f] = kept[f]
    row = iota((8, NZ), 0)
    pieces = []
    for f in range(FIELDS):
        for x in range(PLANES // 2):
            k = 2 * x
            lines = [
                change[f, pl.ds(4 * place + k + half, 1), :] - guess[pl.ds(4 * f + k + half, 1), :] for half in range(2)
            ]
            tile = jnp.where(row < 4, lines[0], lines[1])
            tile = jnp.where(mine == 0, 0.0, tile)
            pieces += [tile] * (TILES // 2)
    stacked = jnp.concatenate(pieces, axis=0)
    stacked = stacked * pick_rows(stacked.shape)
    spread = (iota((NZ, NZ), 0) % 8 == iota((NZ, NZ), 1) // 16).astype(F32)
    wide = jnp.dot(stacked, spread, precision=HIGHEST, preferred_element_type=F32)
    for f in range(FIELDS):
        for x in range(PLANES):
            for t in range(TILES):
                k = ((f * 2 + x // 2) * (TILES // 2) + t // 2) * 8
                out[0, f, x, pl.ds(t, 8, stride=8), :] = fine_end[f * PLANES + x, t] + wide[k : k + 8]


def neighbours(block, size):
    upward = [(i, i + 1) for i in range(size - 1)]
    downward = [(target, source) for source, target in upward]
    return lax.ppermute(block, "space", upward), lax.ppermute(block, "space", downward)


def shaped(*shape):
    return jax.ShapeDtypeStruct(shape, F32)


def local(slices, space_size, starts, flags):
    fine_scratch = [
        pltpu.VMEM((FIELDS, WINDOW, TILES + 2, 8, NZ), F32),
        pltpu.VMEM((FIELDS, WINDOW, TILES + 2, 8, NZ), F32),
        pltpu.VMEM((2, WINDOW, TILES, 8, NZ), F32),
    ]
    left, right = neighbours(starts, space_size)
    left_kind, right_kind = neighbours(flags, space_size)
    own, own_kind = pl.pallas_call(
        prepare_kernel,
        out_shape=(shaped(PACKED, TILES, 8, NZ), jax.ShapeDtypeStruct(flags.shape, flags.dtype)),
        in_specs=[VMEM] * 2,
        out_specs=(VMEM, VMEM),
        compiler_params=params(),
        name="prepare",
    )(starts, flags)
    middle = pl.pallas_call(
        functools.partial(first_kernel, space_size),
        out_shape=shaped(PACKED, TILES, 8, NZ),
        in_specs=[VMEM] * 6,
        out_specs=VMEM,
        scratch_shapes=fine_scratch,
        compiler_params=params(),
        name="first_round",
    )(left, own, right, left_kind, own_kind, right_kind)
    middle_left, middle_right = neighbours(middle, space_size)
    guess = pl.pallas_call(
        functools.partial(guess_kernel, space_size),
        out_shape=shaped(PACKED, NZ),
        in_specs=[VMEM] * 3,
        out_specs=VMEM,
        compiler_params=params(),
        name="guess_old",
    )(left, own, right)
    fine_end, jump = pl.pallas_call(
        functools.partial(second_kernel, space_size),
        out_shape=(shaped(PACKED, TILES, 8, NZ), shaped(slices * space_size, PACKED, NZ)),
        in_specs=[VMEM] * 7,
        out_specs=(VMEM, VMEM),
        scratch_shapes=fine_scratch,
        compiler_params=params(),
        name="second_round",
    )(middle_left, middle, middle_right, left_kind, own_kind, right_kind, guess)
    jumps = lax.all_to_all(jump, ("tm", "space"), 0, 0)
    jumps = jumps.reshape(slices, space_size, PACKED, NZ)
    return pl.pallas_call(
        correct_kernel,
        out_shape=shaped(1, FIELDS, PLANES, NY, NZ),
        in_specs=[VMEM] * 3,
        out_specs=VMEM,
        scratch_shapes=[
            pltpu.VMEM((slices, FIELDS, space_size * 4, NZ), F32),
            pltpu.VMEM((FIELDS, space_size * 4, NZ), F32),
        ],
        compiler_params=params(),
        name="correct",
    )(jumps, guess, fine_end)


def solution(mesh):
    return jax.shard_map(
        functools.partial(local, mesh.shape["tm"], mesh.shape["space"]),
        mesh=mesh,
        in_specs=(P("tm", None, "space", None, None), P("space", None, None)),
        out_specs=P("tm", None, "space", None, None),
        check_vma=False,
    )
```

```python
import functools

import jax
import jax.numpy as jnp
from jax import lax
from jax.experimental import pallas as pl
from jax.experimental.pallas import tpu as pltpu
from jax.sharding import PartitionSpec as P

FINE_STEPS = 8
COARSE_STEPS = 2

fine_dt = 0.12
coarse_dt = 0.48

FIELDS = 4
PLANES = 4
NY = 64
NZ = 128
ROUND = 4
WINDOW = 3 * PLANES
TILES = NY // 8
GROUP = 4
PACKED = FIELDS * PLANES
F32 = jnp.float32
HIGHEST = lax.Precision.HIGHEST
VMEM = pl.BlockSpec(memory_space=pltpu.VMEM)
LIMIT = 48 * 2**20


def iota(shape, dim):
    return lax.broadcasted_iota(jnp.int32, shape, dim)


def params():
    return pltpu.CompilerParams(vmem_limit_bytes=LIMIT)


def prepare_kernel(starts, flags, message_one, message_two, fields, kinds, sems):
    copies = [pltpu.make_async_copy(starts, fields, sems.at[0]), pltpu.make_async_copy(flags, kinds, sems.at[1])]
    for copy in copies:
        copy.start()
    for copy in copies:
        copy.wait()
    for f in range(FIELDS):
        message = message_one if f < 2 else message_two
        for x in range(PLANES):
            for t in range(TILES):
                v = fields[0, f, x, pl.ds(t, 8, stride=8), :]
                message[f % 2 * PLANES + x, t] = v * 0.5 if f == 0 else v
    for x in range(PLANES):
        message = message_one if x < 2 else message_two
        for t in range(TILES):
            message[2 * PLANES + x % 2, t] = kinds[x, pl.ds(t, 8, stride=8), :].astype(F32)


def fine_tile(mid, lo_x, hi_x, lo_y, hi_y, kv, ks, kc, low_lane, high_lane):
    beta = 1.0 / fine_dt - 7.0
    alpha = 1.0 / fine_dt - 6.0
    lo_z = [jnp.where(low_lane, 0.0, pltpu.roll(v, 1, 1)) for v in mid]
    hi_z = [jnp.where(high_lane, 0.0, pltpu.roll(v, NZ - 1, 1)) for v in mid]
    total = [((lo_x[f] + hi_x[f]) + (lo_y[f] + hi_y[f])) + (lo_z[f] + hi_z[f]) for f in range(FIELDS)]
    w, a, b, c = mid
    gx = hi_x[0] - lo_x[0]
    gy = hi_y[0] - lo_y[0]
    gz = hi_z[0] - lo_z[0]
    diverge = (hi_x[1] - lo_x[1]) + (hi_y[2] - lo_y[2]) + (hi_z[3] - lo_z[3])
    stretch = gz + beta
    new_w = kv * ((total[0] + 0.125 * diverge) + alpha * w)
    new_a = ks * ((total[1] + gx) + a * stretch)
    new_b = ks * ((total[2] + gy) + b * stretch)
    new_c = kc * ((total[3] + 2.0 * (gx * a + gy * b)) + ((stretch + gz) * c + 1.0))
    return new_w, new_a, new_b, new_c


def fine_plane(src, keep, p, valid, store):
    lane = iota((8, NZ), 1)
    low_lane, high_lane = lane == 0, lane == NZ - 1
    fields = range(FIELDS)
    kc = jnp.where(valid, fine_dt, 0.0).astype(F32)
    for begin in range(0, TILES, GROUP):
        tiles = range(begin, begin + GROUP)
        column = [[src[f, p, t] for f in fields] for t in range(begin, begin + GROUP + 2)]
        lo_x = [[src[f, p - 1, t + 1] for f in fields] for t in tiles]
        hi_x = [[src[f, p + 1, t + 1] for f in fields] for t in tiles]
        kept = [(keep[0, p, t], keep[1, p, t]) for t in tiles]
        fresh = [
            fine_tile(column[i + 1], lo_x[i], hi_x[i], column[i], column[i + 2], *kept[i], kc, low_lane, high_lane)
            for i in range(GROUP)
        ]
        for i, t in enumerate(tiles):
            for f in fields:
                store(f, t, fresh[i][f])


def put_tile(buffer, f, p, t, value):
    buffer[f, p, t + 1] = value
    row = iota((8, NZ), 0)
    if t == 0:
        buffer[f, p, TILES + 1] = jnp.where(row == 7, 0.0, pltpu.roll(value, 7, 0))
    if t == TILES - 1:
        buffer[f, p, 0] = jnp.where(row == 0, 0.0, pltpu.roll(value, 1, 0))


class Slabs:

    def __init__(self, space_size, own, first, second):
        place = lax.axis_index("space")
        self.own = own
        self.first = {0: first[0], 2: first[1]}
        self.second = second
        self.low = place < turn(space_size)
        self.there = {0: place > 0, 2: place < space_size - 1}

    def row(self, j, half, k, t):
        if j == 1:
            return self.own[half][k, t]
        if half == 0:
            return self.first[j][k, t]
        x, y = self.second[0][k, t], self.second[1][k, t]
        v = jnp.where(self.low, x, y) if j == 0 else jnp.where(self.low, y, x)
        return jnp.where(self.there[j], v, 0.0)

    def field(self, j, f, x, t):
        return self.row(j, f // 2, f % 2 * PLANES + x, t)

    def kind(self, j, x, t):
        return self.row(j, x // 2, 2 * PLANES + x % 2, t)


def inside(space_size, p):
    x = (lax.axis_index("space") - 1) * PLANES + p
    return (x >= 0) & (x < space_size * PLANES)


def fine_round(space_size, slabs, even, odd, keep, finish):
    for j in range(3):
        for x in range(PLANES):
            for f in range(FIELDS):
                for t in range(TILES):
                    put_tile(even, f, j * PLANES + x, t, slabs.field(j, f, x, t))

    for step in range(ROUND):
        src, dst = (even, odd) if step % 2 == 0 else (odd, even)
        many = PLANES + ROUND // 2 - 1 - step

        def body(i, carry, src=src, dst=dst, step=step, many=many):
            for k in range(many):
                p = step + 1 + i * many + k
                if step == ROUND - 1:
                    store = lambda f, t, value: finish(f, p - PLANES, t, value)
                else:
                    store = lambda f, t, value: put_tile(dst, f, p, t, value)
                fine_plane(src, keep, p, inside(space_size, p), store)
            return carry

        lax.fori_loop(0, 2, body, 0)


def first_kernel(space_size, own_one, own_two, up, down, x, y, ended_one, ended_two, keep, even, odd):
    slabs = Slabs(space_size, (own_one, own_two), (up, down), (x, y))
    for j in range(3):
        for k in range(PLANES):
            p = j * PLANES + k
            scale = jnp.where(inside(space_size, p), fine_dt, 0.0).astype(F32)
            for t in range(TILES):
                kind = slabs.kind(j, k, t)
                keep[0, p, t] = jnp.where(kind != 1.0, scale, 0.0)
                keep[1, p, t] = jnp.where(kind != 2.0, scale, 0.0)

    def finish(f, x, t, value):
        ended = ended_one if f < 2 else ended_two
        ended[f % 2 * PLANES + x, t] = value

    fine_round(space_size, slabs, even, odd, keep, finish)


def coarse_rows(pair_of, count):
    pairs = count // 2
    pieces = []
    for k in range(pairs):
        for i in range(TILES // 2):
            pieces.append(pair_of(k, 2 * i) + pair_of(k, 2 * i + 1))
    stacked = jnp.concatenate(pieces, axis=0)
    gather = (iota((NZ, NZ), 0) // 16 == iota((NZ, NZ), 1) % 8).astype(F32)
    sums = jnp.dot(stacked, gather, precision=HIGHEST, preferred_element_type=F32)
    sums = sums * pick_rows(sums.shape)
    sums = sums.reshape(pairs, TILES // 2, 8, NZ)
    sums = (sums[:, 0] + sums[:, 1]) + (sums[:, 2] + sums[:, 3])
    return sums.reshape(pairs * 8, NZ)


def pick_rows(shape):
    row = iota(shape, 0)
    return (row % 8 % 4 * 4 + row // 8 % 4 == iota(shape, 1) // 8).astype(F32)


def halves(sums, rows):
    shape = (rows, sums.shape[0])
    add = (iota(shape, 0) == iota(shape, 1) // 4).astype(F32) * (1.0 / 64.0)
    return jnp.dot(add, sums, precision=HIGHEST, preferred_element_type=F32)


def row_shift(v, by):
    rows = v.shape[0]
    row = iota(v.shape, 0)
    rolled = pltpu.roll(v, (-by) % rows, 0)
    return jnp.where((row + by >= 0) & (row + by < rows), rolled, 0.0)


def coarse_neighbours(v):
    row = iota(v.shape, 0)
    lane = iota(v.shape, 1)
    lo_x, hi_x = row_shift(v, -2), row_shift(v, 2)
    up = pltpu.roll(v, NZ - 8, 1)
    hi_y = jnp.where(lane < NZ - 8, up, jnp.where(row % 2 == 0, row_shift(up, 1), 0.0))
    down = pltpu.roll(v, 8, 1)
    lo_y = jnp.where(lane >= 8, down, jnp.where(row % 2 == 1, row_shift(down, -1), 0.0))
    hi_z = jnp.where(lane % 8 == 7, 0.0, pltpu.roll(v, NZ - 1, 1))
    lo_z = jnp.where(lane % 8 == 0, 0.0, pltpu.roll(v, 1, 1))
    return lo_x, hi_x, lo_y, hi_y, lo_z, hi_z


def coarse_step(state):
    near = [coarse_neighbours(v) for v in state]
    w, a, b, c = state

    def lap(f):
        lo_x, hi_x, lo_y, hi_y, lo_z, hi_z = near[f]
        return (0.25 * ((lo_x + hi_x) + (lo_y + hi_y)) + (1.0 / 256.0) * (lo_z + hi_z)) - (1.0 + 2.0 / 256.0) * state[f]

    def grad(f, k):
        return (near[f][2 * k + 1] - near[f][2 * k]) * (1.0 / 32.0 if k == 2 else 0.25)

    gx, gy, gz = grad(0, 0), grad(0, 1), grad(0, 2)
    diverge = grad(1, 0) + grad(2, 1) + grad(3, 2)
    new_w = w + coarse_dt * (lap(0) + 0.5 * diverge)
    new_a = a + coarse_dt * (gx + a * gz - a + lap(1))
    new_b = b + coarse_dt * (gy + b * gz - b + lap(2))
    new_c = c + coarse_dt * (2.0 * (gx * a + gy * b + gz * c) - (c - 1.0) + lap(3))
    return new_w, new_a, new_b, new_c


def guess_kernel(space_size, own_one, own_two, up, down, x, y, guess):
    place = lax.axis_index("space")
    slabs = Slabs(space_size, (own_one, own_two), (up, down), (x, y))
    rows = 16
    row = iota((rows, NZ), 0)
    plane = 2 * place - 2 + row // 2
    valid = (row < WINDOW) & (plane >= 0) & (plane < 2 * space_size)
    state = []
    for f in range(FIELDS):

        def pair_of(k, t, f=f):
            return slabs.field(k // 2, f, k % 2 * 2, t) + slabs.field(k // 2, f, k % 2 * 2 + 1, t)

        grid = halves(coarse_rows(pair_of, WINDOW), rows)
        state.append(grid * 2.0 if f == 0 else grid)
    for _ in range(COARSE_STEPS):
        state = [jnp.where(valid, v, 0.0) for v in coarse_step(state)]
    for f in range(FIELDS):
        guess[pl.ds(4 * f, 4), :] = state[f][4:8]


def second_kernel(space_size, own_one, own_two, up, down, x, y, keep, guess, fine_end, jump, even, odd):
    slabs = Slabs(space_size, (own_one, own_two), (up, down), (x, y))

    def finish(f, x, t, value):
        fine_end[f * PLANES + x, t] = value * 2.0 if f == 0 else value

    fine_round(space_size, slabs, even, odd, keep, finish)
    ended = halves(coarse_rows(lambda k, t: fine_end[2 * k, t] + fine_end[2 * k + 1, t], PACKED), PACKED)
    jumped = ended - jnp.where(lax.axis_index("tm") == 0, 0.0, guess[...])
    for k in range(jump.shape[0]):
        jump[k] = jumped


def correct_kernel(jumps, guess, fine_end, out, grids, change):
    slices, spaces = jumps.shape[:2]
    mine = lax.axis_index("tm")
    place = lax.axis_index("space")
    for m in range(slices - 1):
        for s in range(spaces):
            for f in range(FIELDS):
                grids[m, f, pl.ds(4 * s, 4), :] = jumps[m, s, pl.ds(4 * f, 4), :]
    state = [grids[0, f] for f in range(FIELDS)]
    kept = state
    for m in range(1, slices):
        ended = state
        for _ in range(COARSE_STEPS):
            ended = coarse_step(ended)
        kept = [jnp.where(mine == m, ended[f], kept[f]) for f in range(FIELDS)]
        if m < slices - 1:
            state = [ended[f] + grids[m, f] for f in range(FIELDS)]
    for f in range(FIELDS):
        change[f] = kept[f]
    row = iota((8, NZ), 0)
    pieces = []
    for f in range(FIELDS):
        for x in range(PLANES // 2):
            k = 2 * x
            lines = [
                change[f, pl.ds(4 * place + k + half, 1), :] - guess[pl.ds(4 * f + k + half, 1), :] for half in range(2)
            ]
            tile = jnp.where(row < 4, lines[0], lines[1])
            tile = jnp.where(mine == 0, 0.0, tile)
            pieces += [tile] * (TILES // 2)
    stacked = jnp.concatenate(pieces, axis=0)
    stacked = stacked * pick_rows(stacked.shape)
    spread = (iota((NZ, NZ), 0) % 8 == iota((NZ, NZ), 1) // 16).astype(F32)
    wide = jnp.dot(stacked, spread, precision=HIGHEST, preferred_element_type=F32)
    for f in range(FIELDS):
        for x in range(PLANES):
            for t in range(TILES):
                k = ((f * 2 + x // 2) * (TILES // 2) + t // 2) * 8
                out[0, f, x, pl.ds(t, 8, stride=8), :] = fine_end[f * PLANES + x, t] + wide[k : k + 8]


def relayed(size):
    return size == 8


def turn(size):
    return size // 2 if relayed(size) else size


def exchange(one, two, size):
    upward = [(i, i + 1) for i in range(size - 1)]
    downward = [(target, source) for source, target in upward]
    if relayed(size):
        half = size // 2
        low_up, high_up = upward[: half - 1], upward[half:]
        low_down, high_down = downward[: half - 1], downward[half:]
        x = lax.ppermute(two, "space", low_up + high_down + [(half - 1, size - 1), (half, 0)])
        up, down = lax.ppermute(one, "space", upward), lax.ppermute(one, "space", downward)
        place = lax.axis_index("space")
        passed = jnp.where((place == 0) | (place == size - 1), x, two)
        y = lax.ppermute(passed, "space", low_down + high_up + [(0, half - 1), (size - 1, half)])
    else:
        x, y = lax.ppermute(two, "space", upward), lax.ppermute(two, "space", downward)
        up, down = lax.ppermute(one, "space", upward), lax.ppermute(one, "space", downward)
    return up, down, x, y


def shaped(*shape):
    return jax.ShapeDtypeStruct(shape, F32)


def local(slices, space_size, starts, flags):
    half = shaped(2 * PLANES, TILES, 8, NZ)
    message = shaped(2 * PLANES + 2, TILES, 8, NZ)
    keep_shape = shaped(2, WINDOW, TILES, 8, NZ)
    buffers = [pltpu.VMEM((FIELDS, WINDOW, TILES + 2, 8, NZ), F32)] * 2
    opening = pl.pallas_call(
        prepare_kernel,
        out_shape=(message, message),
        in_specs=[pl.BlockSpec(memory_space=pltpu.HBM)] * 2,
        out_specs=(VMEM, VMEM),
        scratch_shapes=[
            pltpu.VMEM(starts.shape, F32),
            pltpu.VMEM(flags.shape, flags.dtype),
            pltpu.SemaphoreType.DMA((2,)),
        ],
        compiler_params=params(),
        name="prepare",
    )(starts, flags)
    opening_near = exchange(*opening, space_size)
    *middle, keep = pl.pallas_call(
        functools.partial(first_kernel, space_size),
        out_shape=(half, half, keep_shape),
        in_specs=[VMEM] * 6,
        out_specs=(VMEM,) * 3,
        scratch_shapes=buffers,
        compiler_params=params(),
        name="first_round",
    )(*opening, *opening_near)
    middle_near = exchange(*middle, space_size)
    guess = pl.pallas_call(
        functools.partial(guess_kernel, space_size),
        out_shape=shaped(PACKED, NZ),
        in_specs=[VMEM] * 6,
        out_specs=VMEM,
        compiler_params=params(),
        name="guess_old",
    )(*opening, *opening_near)
    fine_end, jump = pl.pallas_call(
        functools.partial(second_kernel, space_size),
        out_shape=(shaped(PACKED, TILES, 8, NZ), shaped(slices * space_size, PACKED, NZ)),
        in_specs=[VMEM] * 8,
        out_specs=(VMEM, VMEM),
        scratch_shapes=buffers,
        compiler_params=params(),
        name="second_round",
    )(*middle, *middle_near, keep, guess)
    jumps = lax.all_to_all(jump, ("tm", "space"), 0, 0)
    jumps = jumps.reshape(slices, space_size, PACKED, NZ)
    return pl.pallas_call(
        correct_kernel,
        out_shape=shaped(1, FIELDS, PLANES, NY, NZ),
        in_specs=[VMEM] * 3,
        out_specs=VMEM,
        scratch_shapes=[
            pltpu.VMEM((slices, FIELDS, space_size * 4, NZ), F32),
            pltpu.VMEM((FIELDS, space_size * 4, NZ), F32),
        ],
        compiler_params=params(),
        name="correct",
    )(jumps, guess, fine_end)


def solution(mesh):
    return jax.shard_map(
        functools.partial(local, mesh.shape["tm"], mesh.shape["space"]),
        mesh=mesh,
        in_specs=(P("tm", None, "space", None, None), P("space", None, None)),
        out_specs=P("tm", None, "space", None, None),
        check_vma=False,
    )
```

```python
import functools

import jax
import jax.numpy as jnp
from jax import lax
from jax.experimental import pallas as pl
from jax.experimental.pallas import tpu as pltpu
from jax.sharding import PartitionSpec as P

FINE_STEPS = 8
COARSE_STEPS = 2

fine_dt = 0.12
coarse_dt = 0.48

FIELDS = 4
PLANES = 4
NY = 64
NZ = 128
ROUND = 4
WINDOW = 3 * PLANES
TILES = NY // 8
GROUP = 4
PACKED = FIELDS * PLANES
F32 = jnp.float32
HIGHEST = lax.Precision.HIGHEST
VMEM = pl.BlockSpec(memory_space=pltpu.VMEM)
LIMIT = 48 * 2**20


def iota(shape, dim):
    return lax.broadcasted_iota(jnp.int32, shape, dim)


def params():
    return pltpu.CompilerParams(vmem_limit_bytes=LIMIT)


def prepare_kernel(starts, flags, message_one, message_two, fields, kinds, sems):
    copies = [pltpu.make_async_copy(starts, fields, sems.at[0]), pltpu.make_async_copy(flags, kinds, sems.at[1])]
    for copy in copies:
        copy.start()
    for copy in copies:
        copy.wait()
    for f in range(FIELDS):
        message = message_one if f < 2 else message_two
        for x in range(PLANES):
            for t in range(TILES):
                v = fields[0, f, x, pl.ds(t, 8, stride=8), :]
                message[f % 2 * PLANES + x, t] = v * 0.5 if f == 0 else v
    for x in range(PLANES):
        message = message_one if x < 2 else message_two
        for t in range(TILES):
            message[2 * PLANES + x % 2, t] = kinds[x, pl.ds(t, 8, stride=8), :].astype(F32)


def fine_tile(mid, lo_x, hi_x, lo_y, hi_y, kv, ks, kc, low_lane, high_lane):
    beta = 1.0 / fine_dt - 7.0
    alpha = 1.0 / fine_dt - 6.0
    lo_z = [jnp.where(low_lane, 0.0, pltpu.roll(v, 1, 1)) for v in mid]
    hi_z = [jnp.where(high_lane, 0.0, pltpu.roll(v, NZ - 1, 1)) for v in mid]
    total = [((lo_x[f] + hi_x[f]) + (lo_y[f] + hi_y[f])) + (lo_z[f] + hi_z[f]) for f in range(FIELDS)]
    w, a, b, c = mid
    gx = hi_x[0] - lo_x[0]
    gy = hi_y[0] - lo_y[0]
    gz = hi_z[0] - lo_z[0]
    diverge = (hi_x[1] - lo_x[1]) + (hi_y[2] - lo_y[2]) + (hi_z[3] - lo_z[3])
    stretch = gz + beta
    new_w = kv * ((total[0] + 0.125 * diverge) + alpha * w)
    new_a = ks * ((total[1] + gx) + a * stretch)
    new_b = ks * ((total[2] + gy) + b * stretch)
    new_c = kc * ((total[3] + 2.0 * (gx * a + gy * b)) + ((stretch + gz) * c + 1.0))
    return new_w, new_a, new_b, new_c


def fine_plane(src, keep, p, valid, store):
    lane = iota((8, NZ), 1)
    low_lane, high_lane = lane == 0, lane == NZ - 1
    fields = range(FIELDS)
    kc = jnp.where(valid, fine_dt, 0.0).astype(F32)
    for begin in range(0, TILES, GROUP):
        tiles = range(begin, begin + GROUP)
        column = [[src[f, p, t] for f in fields] for t in range(begin, begin + GROUP + 2)]
        lo_x = [[src[f, p - 1, t + 1] for f in fields] for t in tiles]
        hi_x = [[src[f, p + 1, t + 1] for f in fields] for t in tiles]
        kept = [(keep[0, p, t], keep[1, p, t]) for t in tiles]
        fresh = [
            fine_tile(column[i + 1], lo_x[i], hi_x[i], column[i], column[i + 2], *kept[i], kc, low_lane, high_lane)
            for i in range(GROUP)
        ]
        for i, t in enumerate(tiles):
            for f in fields:
                store(f, t, fresh[i][f])


def put_tile(buffer, f, p, t, value):
    buffer[f, p, t + 1] = value
    row = iota((8, NZ), 0)
    if t == 0:
        buffer[f, p, TILES + 1] = jnp.where(row == 7, 0.0, pltpu.roll(value, 7, 0))
    if t == TILES - 1:
        buffer[f, p, 0] = jnp.where(row == 0, 0.0, pltpu.roll(value, 1, 0))


class Slabs:

    def __init__(self, space_size, own, near):
        place = lax.axis_index("space")
        self.own = own
        self.near = (near[:2], near[2:])
        self.from_first = (place % 2 == 1, place < turn(space_size))
        self.there = {0: place > 0, 2: place < space_size - 1}

    def row(self, j, half, k, t):
        if j == 1:
            return self.own[half][k, t]
        v, other = (ref[k, t] for ref in self.near[half])
        first = self.from_first[half]
        v = jnp.where(first, v, other) if j == 0 else jnp.where(first, other, v)
        return jnp.where(self.there[j], v, 0.0)

    def field(self, j, f, x, t):
        return self.row(j, f // 2, f % 2 * PLANES + x, t)

    def kind(self, j, x, t):
        return self.row(j, x // 2, 2 * PLANES + x % 2, t)


def inside(space_size, p):
    x = (lax.axis_index("space") - 1) * PLANES + p
    return (x >= 0) & (x < space_size * PLANES)


def fine_round(space_size, slabs, even, odd, keep, finish):
    for j in range(3):
        for x in range(PLANES):
            for f in range(FIELDS):
                for t in range(TILES):
                    put_tile(even, f, j * PLANES + x, t, slabs.field(j, f, x, t))

    for step in range(ROUND):
        src, dst = (even, odd) if step % 2 == 0 else (odd, even)
        many = PLANES + ROUND // 2 - 1 - step

        def body(i, carry, src=src, dst=dst, step=step, many=many):
            for k in range(many):
                p = step + 1 + i * many + k
                if step == ROUND - 1:
                    store = lambda f, t, value: finish(f, p - PLANES, t, value)
                else:
                    store = lambda f, t, value: put_tile(dst, f, p, t, value)
                fine_plane(src, keep, p, inside(space_size, p), store)
            return carry

        lax.fori_loop(0, 2, body, 0)


def first_kernel(space_size, own_one, own_two, inner, outer, x, y, ended_one, ended_two, keep, even, odd):
    slabs = Slabs(space_size, (own_one, own_two), (inner, outer, x, y))
    for j in range(3):
        for k in range(PLANES):
            p = j * PLANES + k
            scale = jnp.where(inside(space_size, p), fine_dt, 0.0).astype(F32)
            for t in range(TILES):
                kind = slabs.kind(j, k, t)
                keep[0, p, t] = jnp.where(kind != 1.0, scale, 0.0)
                keep[1, p, t] = jnp.where(kind != 2.0, scale, 0.0)

    def finish(f, x, t, value):
        ended = ended_one if f < 2 else ended_two
        ended[f % 2 * PLANES + x, t] = value

    fine_round(space_size, slabs, even, odd, keep, finish)


def coarse_rows(pair_of, count):
    pairs = count // 2
    pieces = []
    for k in range(pairs):
        for i in range(TILES // 2):
            pieces.append(pair_of(k, 2 * i) + pair_of(k, 2 * i + 1))
    stacked = jnp.concatenate(pieces, axis=0)
    gather = (iota((NZ, NZ), 0) // 16 == iota((NZ, NZ), 1) % 8).astype(F32)
    sums = jnp.dot(stacked, gather, precision=HIGHEST, preferred_element_type=F32)
    sums = sums * pick_rows(sums.shape)
    sums = sums.reshape(pairs, TILES // 2, 8, NZ)
    sums = (sums[:, 0] + sums[:, 1]) + (sums[:, 2] + sums[:, 3])
    return sums.reshape(pairs * 8, NZ)


def pick_rows(shape):
    row = iota(shape, 0)
    return (row % 8 % 4 * 4 + row // 8 % 4 == iota(shape, 1) // 8).astype(F32)


def halves(sums, rows):
    shape = (rows, sums.shape[0])
    add = (iota(shape, 0) == iota(shape, 1) // 4).astype(F32) * (1.0 / 64.0)
    return jnp.dot(add, sums, precision=HIGHEST, preferred_element_type=F32)


def row_shift(v, by):
    rows = v.shape[0]
    row = iota(v.shape, 0)
    rolled = pltpu.roll(v, (-by) % rows, 0)
    return jnp.where((row + by >= 0) & (row + by < rows), rolled, 0.0)


def coarse_neighbours(v):
    row = iota(v.shape, 0)
    lane = iota(v.shape, 1)
    lo_x, hi_x = row_shift(v, -2), row_shift(v, 2)
    up = pltpu.roll(v, NZ - 8, 1)
    hi_y = jnp.where(lane < NZ - 8, up, jnp.where(row % 2 == 0, row_shift(up, 1), 0.0))
    down = pltpu.roll(v, 8, 1)
    lo_y = jnp.where(lane >= 8, down, jnp.where(row % 2 == 1, row_shift(down, -1), 0.0))
    hi_z = jnp.where(lane % 8 == 7, 0.0, pltpu.roll(v, NZ - 1, 1))
    lo_z = jnp.where(lane % 8 == 0, 0.0, pltpu.roll(v, 1, 1))
    return lo_x, hi_x, lo_y, hi_y, lo_z, hi_z


def coarse_step(state):
    near = [coarse_neighbours(v) for v in state]
    w, a, b, c = state

    def lap(f):
        lo_x, hi_x, lo_y, hi_y, lo_z, hi_z = near[f]
        return (0.25 * ((lo_x + hi_x) + (lo_y + hi_y)) + (1.0 / 256.0) * (lo_z + hi_z)) - (1.0 + 2.0 / 256.0) * state[f]

    def grad(f, k):
        return (near[f][2 * k + 1] - near[f][2 * k]) * (1.0 / 32.0 if k == 2 else 0.25)

    gx, gy, gz = grad(0, 0), grad(0, 1), grad(0, 2)
    diverge = grad(1, 0) + grad(2, 1) + grad(3, 2)
    new_w = w + coarse_dt * (lap(0) + 0.5 * diverge)
    new_a = a + coarse_dt * (gx + a * gz - a + lap(1))
    new_b = b + coarse_dt * (gy + b * gz - b + lap(2))
    new_c = c + coarse_dt * (2.0 * (gx * a + gy * b + gz * c) - (c - 1.0) + lap(3))
    return new_w, new_a, new_b, new_c


def guess_kernel(space_size, own_one, own_two, inner, outer, x, y, guess):
    place = lax.axis_index("space")
    slabs = Slabs(space_size, (own_one, own_two), (inner, outer, x, y))
    rows = 16
    row = iota((rows, NZ), 0)
    plane = 2 * place - 2 + row // 2
    valid = (row < WINDOW) & (plane >= 0) & (plane < 2 * space_size)
    state = []
    for f in range(FIELDS):

        def pair_of(k, t, f=f):
            return slabs.field(k // 2, f, k % 2 * 2, t) + slabs.field(k // 2, f, k % 2 * 2 + 1, t)

        grid = halves(coarse_rows(pair_of, WINDOW), rows)
        state.append(grid * 2.0 if f == 0 else grid)
    for _ in range(COARSE_STEPS):
        state = [jnp.where(valid, v, 0.0) for v in coarse_step(state)]
    for f in range(FIELDS):
        guess[pl.ds(4 * f, 4), :] = state[f][4:8]


def second_kernel(space_size, own_one, own_two, inner, outer, x, y, keep, guess, fine_end, jump, even, odd):
    slabs = Slabs(space_size, (own_one, own_two), (inner, outer, x, y))

    def finish(f, x, t, value):
        fine_end[f * PLANES + x, t] = value * 2.0 if f == 0 else value

    fine_round(space_size, slabs, even, odd, keep, finish)
    ended = halves(coarse_rows(lambda k, t: fine_end[2 * k, t] + fine_end[2 * k + 1, t], PACKED), PACKED)
    jumped = ended - jnp.where(lax.axis_index("tm") == 0, 0.0, guess[...])
    jump[...] = jumped


def correct_kernel(slices, space_size, *refs):
    jumps, (guess, fine_end, out, grids) = refs[:-4], refs[-4:]
    mine = lax.axis_index("tm")
    place = lax.axis_index("space")
    rows = grids.shape[2]
    centre = 4 * slices
    plane = 2 * (place - slices) + iota((rows, NZ), 0) // 2
    valid = (plane >= 0) & (plane < 2 * space_size)
    grids[...] = jnp.zeros_like(grids)
    at = 0
    for k in range(1, slices):
        for j in range(-k, k + 1):
            for f in range(FIELDS):
                grids[k - 1, f, pl.ds(centre + 4 * j, 4), :] = jumps[at][pl.ds(4 * f, 4), :]
            at += 1
    state = None
    for k in range(slices - 1, -1, -1):
        ended = state
        if state is not None:
            for _ in range(COARSE_STEPS):
                ended = [jnp.where(valid, v, 0.0) for v in coarse_step(ended)]
        if k > 0:
            state = [jnp.where(valid, grids[k - 1, f], 0.0) for f in range(FIELDS)]
            if ended is not None:
                state = [state[f] + jnp.where(mine > k, ended[f], 0.0) for f in range(FIELDS)]
    row = iota((8, NZ), 0)
    pieces = []
    for f in range(FIELDS):
        for x in range(PLANES // 2):
            k = 2 * x
            lines = [
                ended[f][centre + k + half : centre + k + half + 1] - guess[pl.ds(4 * f + k + half, 1), :]
                for half in range(2)
            ]
            tile = jnp.where(row < 4, lines[0], lines[1])
            tile = jnp.where(mine == 0, 0.0, tile)
            pieces += [tile] * (TILES // 2)
    stacked = jnp.concatenate(pieces, axis=0)
    stacked = stacked * pick_rows(stacked.shape)
    spread = (iota((NZ, NZ), 0) % 8 == iota((NZ, NZ), 1) // 16).astype(F32)
    wide = jnp.dot(stacked, spread, precision=HIGHEST, preferred_element_type=F32)
    for f in range(FIELDS):
        for x in range(PLANES):
            for t in range(TILES):
                k = ((f * 2 + x // 2) * (TILES // 2) + t // 2) * 8
                out[0, f, x, pl.ds(t, 8, stride=8), :] = fine_end[f * PLANES + x, t] + wide[k : k + 8]


def relayed(size):
    return size == 8


def turn(size):
    return size // 2 if relayed(size) else size


def exchange(one, two, size):
    inner = [(i, i ^ 1) for i in range(size)]
    outer = [(0, 0)] + [(i, (i - 1 ^ 1) + 1) for i in range(1, size - 1)] + [(size - 1, size - 1)]
    if relayed(size):
        half = size // 2
        first = [(i, i + 1) for i in range(half - 1)] + [(half - 1, size - 1)]
        first += [(i, i - 1) for i in range(size - 1, half, -1)] + [(half, 0)]
        second = [(i, i - 1) for i in range(half - 1, 0, -1)] + [(0, half - 1)]
        second += [(i, i + 1) for i in range(half, size - 1)] + [(size - 1, half)]
    else:
        first = [(i, (i + 1) % size) for i in range(size)]
        second = [(i, (i - 1) % size) for i in range(size)]
    x = lax.ppermute(two, "space", first)
    across = lax.ppermute(one, "space", outer)
    within = lax.ppermute(one, "space", inner)
    if relayed(size):
        place = lax.axis_index("space")
        two = jnp.where((place == 0) | (place == size - 1), x, two)
    y = lax.ppermute(two, "space", second)
    return within, across, x, y


def earlier_jumps(jump, slices, space_size):
    found = []
    for k in range(1, slices):
        for j in range(-k, k + 1):
            route = []
            for m in range(slices):
                for s in range(space_size):
                    target = (m + k) % slices * space_size + (s - j) % space_size
                    route.append((m * space_size + s, target))
            found.append(lax.ppermute(jump, ("tm", "space"), route))
    return found


def shaped(*shape):
    return jax.ShapeDtypeStruct(shape, F32)


def local(slices, space_size, starts, flags):
    half = shaped(2 * PLANES, TILES, 8, NZ)
    message = shaped(2 * PLANES + 2, TILES, 8, NZ)
    keep_shape = shaped(2, WINDOW, TILES, 8, NZ)
    buffers = [pltpu.VMEM((FIELDS, WINDOW, TILES + 2, 8, NZ), F32)] * 2
    opening = pl.pallas_call(
        prepare_kernel,
        out_shape=(message, message),
        in_specs=[pl.BlockSpec(memory_space=pltpu.HBM)] * 2,
        out_specs=(VMEM, VMEM),
        scratch_shapes=[
            pltpu.VMEM(starts.shape, F32),
            pltpu.VMEM(flags.shape, flags.dtype),
            pltpu.SemaphoreType.DMA((2,)),
        ],
        compiler_params=params(),
        name="prepare",
    )(starts, flags)
    opening_near = exchange(*opening, space_size)
    *middle, keep = pl.pallas_call(
        functools.partial(first_kernel, space_size),
        out_shape=(half, half, keep_shape),
        in_specs=[VMEM] * 6,
        out_specs=(VMEM,) * 3,
        scratch_shapes=buffers,
        compiler_params=params(),
        name="first_round",
    )(*opening, *opening_near)
    middle_near = exchange(*middle, space_size)
    guess = pl.pallas_call(
        functools.partial(guess_kernel, space_size),
        out_shape=shaped(PACKED, NZ),
        in_specs=[VMEM] * 6,
        out_specs=VMEM,
        compiler_params=params(),
        name="guess_old",
    )(*opening, *opening_near)
    fine_end, jump = pl.pallas_call(
        functools.partial(second_kernel, space_size),
        out_shape=(shaped(PACKED, TILES, 8, NZ), shaped(PACKED, NZ)),
        in_specs=[VMEM] * 8,
        out_specs=(VMEM, VMEM),
        scratch_shapes=buffers,
        compiler_params=params(),
        name="second_round",
    )(*middle, *middle_near, keep, guess)
    jumps = earlier_jumps(jump, slices, space_size)
    return pl.pallas_call(
        functools.partial(correct_kernel, slices, space_size),
        out_shape=shaped(1, FIELDS, PLANES, NY, NZ),
        in_specs=[VMEM] * (len(jumps) + 2),
        out_specs=VMEM,
        scratch_shapes=[pltpu.VMEM((slices - 1, FIELDS, 8 * slices, NZ), F32)],
        compiler_params=params(),
        name="correct",
    )(*jumps, guess, fine_end)


def solution(mesh):
    return jax.shard_map(
        functools.partial(local, mesh.shape["tm"], mesh.shape["space"]),
        mesh=mesh,
        in_specs=(P("tm", None, "space", None, None), P("space", None, None)),
        out_specs=P("tm", None, "space", None, None),
        check_vma=False,
    )
```

```python
import functools

import jax
import jax.numpy as jnp
from jax import lax
from jax.experimental import pallas as pl
from jax.experimental.pallas import tpu as pltpu
from jax.sharding import PartitionSpec as P

FINE_STEPS = 8
COARSE_STEPS = 2

fine_dt = 0.12
coarse_dt = 0.48

FIELDS = 4
PLANES = 4
NY = 64
NZ = 128
ROUND = 4
WINDOW = 3 * PLANES
TILES = NY // 8
GROUP = 4
PACKED = FIELDS * PLANES
F32 = jnp.float32
HIGHEST = lax.Precision.HIGHEST
VMEM = pl.BlockSpec(memory_space=pltpu.VMEM)
LIMIT = 48 * 2**20


def iota(shape, dim):
    return lax.broadcasted_iota(jnp.int32, shape, dim)


def params():
    return pltpu.CompilerParams(vmem_limit_bytes=LIMIT)


def prepare_kernel(starts, flags, whole, message_one, message_two, fields, kinds, sems):
    copies = [pltpu.make_async_copy(starts, fields, sems.at[0]), pltpu.make_async_copy(flags, kinds, sems.at[1])]
    for copy in copies:
        copy.start()
    for copy in copies:
        copy.wait()
    messages = (message_one, message_two)
    for f in range(FIELDS):
        for x in range(PLANES):
            for t in range(TILES):
                v = fields[0, f, x, pl.ds(t, 8, stride=8), :]
                put_row(whole, messages, f // 2, f % 2 * PLANES + x, t, v * 0.5 if f == 0 else v)
    for x in range(PLANES):
        for t in range(TILES):
            v = kinds[x, pl.ds(t, 8, stride=8), :].astype(F32)
            put_row(whole, messages, x // 2, 2 * PLANES + x % 2, t, v)


def put_row(whole, messages, half, k, t, value):
    whole[half * messages[0].shape[0] + k, t] = value
    messages[half][k, t] = value


def fine_tile(mid, lo_x, hi_x, lo_y, hi_y, kv, ks, kc, low_lane, high_lane):
    beta = 1.0 / fine_dt - 7.0
    alpha = 1.0 / fine_dt - 6.0
    lo_z = [jnp.where(low_lane, 0.0, pltpu.roll(v, 1, 1)) for v in mid]
    hi_z = [jnp.where(high_lane, 0.0, pltpu.roll(v, NZ - 1, 1)) for v in mid]
    total = [((lo_x[f] + hi_x[f]) + (lo_y[f] + hi_y[f])) + (lo_z[f] + hi_z[f]) for f in range(FIELDS)]
    w, a, b, c = mid
    gx = hi_x[0] - lo_x[0]
    gy = hi_y[0] - lo_y[0]
    gz = hi_z[0] - lo_z[0]
    diverge = (hi_x[1] - lo_x[1]) + (hi_y[2] - lo_y[2]) + (hi_z[3] - lo_z[3])
    stretch = gz + beta
    new_w = kv * ((total[0] + 0.125 * diverge) + alpha * w)
    new_a = ks * ((total[1] + gx) + a * stretch)
    new_b = ks * ((total[2] + gy) + b * stretch)
    new_c = kc * ((total[3] + 2.0 * (gx * a + gy * b)) + ((stretch + gz) * c + 1.0))
    return new_w, new_a, new_b, new_c


def fine_plane(src, keep, p, valid, store):
    lane = iota((8, NZ), 1)
    low_lane, high_lane = lane == 0, lane == NZ - 1
    fields = range(FIELDS)
    kc = jnp.where(valid, fine_dt, 0.0).astype(F32)
    for begin in range(0, TILES, GROUP):
        tiles = range(begin, begin + GROUP)
        column = [[src[f, p, t] for f in fields] for t in range(begin, begin + GROUP + 2)]
        lo_x = [[src[f, p - 1, t + 1] for f in fields] for t in tiles]
        hi_x = [[src[f, p + 1, t + 1] for f in fields] for t in tiles]
        kept = [(keep[0, p, t], keep[1, p, t]) for t in tiles]
        fresh = [
            fine_tile(column[i + 1], lo_x[i], hi_x[i], column[i], column[i + 2], *kept[i], kc, low_lane, high_lane)
            for i in range(GROUP)
        ]
        for i, t in enumerate(tiles):
            for f in fields:
                store(f, t, fresh[i][f])


def put_tile(buffer, f, p, t, value):
    buffer[f, p, t + 1] = value
    row = iota((8, NZ), 0)
    if t == 0:
        buffer[f, p, TILES + 1] = jnp.where(row == 7, 0.0, pltpu.roll(value, 7, 0))
    if t == TILES - 1:
        buffer[f, p, 0] = jnp.where(row == 0, 0.0, pltpu.roll(value, 1, 0))


class Slabs:

    def __init__(self, space_size, whole, inner, outer_one, outer_two, outer_relayed):
        place = lax.axis_index("space")
        self.whole, self.inner, self.outer = whole, inner, (outer_one, outer_two)
        self.rows = whole.shape[0] // 2
        self.relayed = outer_relayed
        self.odd = place % 2 == 1
        self.by_relay = (place == space_size // 2 - 1) | (place == space_size // 2)
        self.there = {0: place > 0, 2: place < space_size - 1}

    def row(self, j, half, k, t):
        if j == 1:
            return self.whole[half * self.rows + k, t]
        inner = self.inner[half * self.rows + k, t]
        outer = self.outer[half][k, t]
        if half == 1:
            outer = jnp.where(self.by_relay, self.relayed[k, t], outer)
        v = jnp.where(self.odd, inner, outer) if j == 0 else jnp.where(self.odd, outer, inner)
        return jnp.where(self.there[j], v, 0.0)

    def field(self, j, f, x, t):
        return self.row(j, f // 2, f % 2 * PLANES + x, t)

    def kind(self, j, x, t):
        return self.row(j, x // 2, 2 * PLANES + x % 2, t)


def inside(space_size, p):
    x = (lax.axis_index("space") - 1) * PLANES + p
    return (x >= 0) & (x < space_size * PLANES)


def fine_round(space_size, slabs, even, odd, keep, finish):
    for j in range(3):
        for x in range(PLANES):
            for f in range(FIELDS):
                for t in range(TILES):
                    put_tile(even, f, j * PLANES + x, t, slabs.field(j, f, x, t))

    for step in range(ROUND):
        src, dst = (even, odd) if step % 2 == 0 else (odd, even)
        many = PLANES + ROUND // 2 - 1 - step

        def body(i, carry, src=src, dst=dst, step=step, many=many):
            for k in range(many):
                p = step + 1 + i * many + k
                if step == ROUND - 1:
                    store = lambda f, t, value: finish(f, p - PLANES, t, value)
                else:
                    store = lambda f, t, value: put_tile(dst, f, p, t, value)
                fine_plane(src, keep, p, inside(space_size, p), store)
            return carry

        lax.fori_loop(0, 2, body, 0)


def first_kernel(space_size, own, inner, outer_one, outer_two, relayed, ended, ended_one, ended_two, keep, even, odd):
    slabs = Slabs(space_size, own, inner, outer_one, outer_two, relayed)
    for j in range(3):
        for k in range(PLANES):
            p = j * PLANES + k
            scale = jnp.where(inside(space_size, p), fine_dt, 0.0).astype(F32)
            for t in range(TILES):
                kind = slabs.kind(j, k, t)
                keep[0, p, t] = jnp.where(kind != 1.0, scale, 0.0)
                keep[1, p, t] = jnp.where(kind != 2.0, scale, 0.0)

    def finish(f, x, t, value):
        put_row(ended, (ended_one, ended_two), f // 2, f % 2 * PLANES + x, t, value)

    fine_round(space_size, slabs, even, odd, keep, finish)


def coarse_rows(pair_of, count):
    pairs = count // 2
    pieces = []
    for k in range(pairs):
        for i in range(TILES // 2):
            pieces.append(pair_of(k, 2 * i) + pair_of(k, 2 * i + 1))
    stacked = jnp.concatenate(pieces, axis=0)
    gather = (iota((NZ, NZ), 0) // 16 == iota((NZ, NZ), 1) % 8).astype(F32)
    sums = jnp.dot(stacked, gather, precision=HIGHEST, preferred_element_type=F32)
    sums = sums * pick_rows(sums.shape)
    sums = sums.reshape(pairs, TILES // 2, 8, NZ)
    sums = (sums[:, 0] + sums[:, 1]) + (sums[:, 2] + sums[:, 3])
    return sums.reshape(pairs * 8, NZ)


def pick_rows(shape):
    row = iota(shape, 0)
    return (row % 8 % 4 * 4 + row // 8 % 4 == iota(shape, 1) // 8).astype(F32)


def halves(sums, rows):
    shape = (rows, sums.shape[0])
    add = (iota(shape, 0) == iota(shape, 1) // 4).astype(F32) * (1.0 / 64.0)
    return jnp.dot(add, sums, precision=HIGHEST, preferred_element_type=F32)


def row_shift(v, by):
    rows = v.shape[0]
    row = iota(v.shape, 0)
    rolled = pltpu.roll(v, (-by) % rows, 0)
    return jnp.where((row + by >= 0) & (row + by < rows), rolled, 0.0)


def coarse_neighbours(v):
    row = iota(v.shape, 0)
    lane = iota(v.shape, 1)
    lo_x, hi_x = row_shift(v, -2), row_shift(v, 2)
    up = pltpu.roll(v, NZ - 8, 1)
    hi_y = jnp.where(lane < NZ - 8, up, jnp.where(row % 2 == 0, row_shift(up, 1), 0.0))
    down = pltpu.roll(v, 8, 1)
    lo_y = jnp.where(lane >= 8, down, jnp.where(row % 2 == 1, row_shift(down, -1), 0.0))
    hi_z = jnp.where(lane % 8 == 7, 0.0, pltpu.roll(v, NZ - 1, 1))
    lo_z = jnp.where(lane % 8 == 0, 0.0, pltpu.roll(v, 1, 1))
    return lo_x, hi_x, lo_y, hi_y, lo_z, hi_z


def coarse_step(state):
    near = [coarse_neighbours(v) for v in state]
    w, a, b, c = state

    def lap(f):
        lo_x, hi_x, lo_y, hi_y, lo_z, hi_z = near[f]
        return (0.25 * ((lo_x + hi_x) + (lo_y + hi_y)) + (1.0 / 256.0) * (lo_z + hi_z)) - (1.0 + 2.0 / 256.0) * state[f]

    def grad(f, k):
        return (near[f][2 * k + 1] - near[f][2 * k]) * (1.0 / 32.0 if k == 2 else 0.25)

    gx, gy, gz = grad(0, 0), grad(0, 1), grad(0, 2)
    diverge = grad(1, 0) + grad(2, 1) + grad(3, 2)
    new_w = w + coarse_dt * (lap(0) + 0.5 * diverge)
    new_a = a + coarse_dt * (gx + a * gz - a + lap(1))
    new_b = b + coarse_dt * (gy + b * gz - b + lap(2))
    new_c = c + coarse_dt * (2.0 * (gx * a + gy * b + gz * c) - (c - 1.0) + lap(3))
    return new_w, new_a, new_b, new_c


def guess_kernel(space_size, own, inner, outer_one, outer_two, relayed, guess):
    place = lax.axis_index("space")
    slabs = Slabs(space_size, own, inner, outer_one, outer_two, relayed)
    rows = 16
    row = iota((rows, NZ), 0)
    plane = 2 * place - 2 + row // 2
    valid = (row < WINDOW) & (plane >= 0) & (plane < 2 * space_size)
    state = []
    for f in range(FIELDS):

        def pair_of(k, t, f=f):
            return slabs.field(k // 2, f, k % 2 * 2, t) + slabs.field(k // 2, f, k % 2 * 2 + 1, t)

        grid = halves(coarse_rows(pair_of, WINDOW), rows)
        state.append(grid * 2.0 if f == 0 else grid)
    for _ in range(COARSE_STEPS):
        state = [jnp.where(valid, v, 0.0) for v in coarse_step(state)]
    for f in range(FIELDS):
        guess[pl.ds(4 * f, 4), :] = state[f][4:8]


def second_kernel(space_size, own, inner, outer_one, outer_two, relayed, keep, guess, fine_end, jump, even, odd):
    slabs = Slabs(space_size, own, inner, outer_one, outer_two, relayed)

    def finish(f, x, t, value):
        fine_end[f * PLANES + x, t] = value * 2.0 if f == 0 else value

    fine_round(space_size, slabs, even, odd, keep, finish)
    ended = halves(coarse_rows(lambda k, t: fine_end[2 * k, t] + fine_end[2 * k + 1, t], PACKED), PACKED)
    jumped = ended - jnp.where(lax.axis_index("tm") == 0, 0.0, guess[...])
    for k in range(jump.shape[0]):
        jump[k] = jumped


def correct_kernel(jumps, guess, fine_end, out, grids):
    slices, space_size = jumps.shape[:2]
    mine = lax.axis_index("tm")
    place = lax.axis_index("space")
    rows = grids.shape[2]
    centre = 4 * slices
    plane = 2 * (place - slices) + iota((rows, NZ), 0) // 2
    valid = (plane >= 0) & (plane < 2 * space_size)
    grids[...] = jnp.zeros_like(grids)
    for k in range(1, slices):
        m = jnp.maximum(mine - k, 0)
        for j in range(-k, k + 1):
            s = jnp.clip(place + j, 0, space_size - 1)
            for f in range(FIELDS):
                grids[k - 1, f, pl.ds(centre + 4 * j, 4), :] = jumps[m, s, pl.ds(4 * f, 4), :]
    state = None
    for k in range(slices - 1, -1, -1):
        ended = state
        if state is not None:
            for _ in range(COARSE_STEPS):
                ended = [jnp.where(valid, v, 0.0) for v in coarse_step(ended)]
        if k > 0:
            state = [jnp.where(valid, grids[k - 1, f], 0.0) for f in range(FIELDS)]
            if ended is not None:
                state = [state[f] + jnp.where(mine > k, ended[f], 0.0) for f in range(FIELDS)]
    row = iota((8, NZ), 0)
    pieces = []
    for f in range(FIELDS):
        for x in range(PLANES // 2):
            k = 2 * x
            lines = [
                ended[f][centre + k + half : centre + k + half + 1] - guess[pl.ds(4 * f + k + half, 1), :]
                for half in range(2)
            ]
            tile = jnp.where(row < 4, lines[0], lines[1])
            tile = jnp.where(mine == 0, 0.0, tile)
            pieces += [tile] * (TILES // 2)
    stacked = jnp.concatenate(pieces, axis=0)
    stacked = stacked * pick_rows(stacked.shape)
    spread = (iota((NZ, NZ), 0) % 8 == iota((NZ, NZ), 1) // 16).astype(F32)
    wide = jnp.dot(stacked, spread, precision=HIGHEST, preferred_element_type=F32)
    for f in range(FIELDS):
        for x in range(PLANES):
            for t in range(TILES):
                k = ((f * 2 + x // 2) * (TILES // 2) + t // 2) * 8
                out[0, f, x, pl.ds(t, 8, stride=8), :] = fine_end[f * PLANES + x, t] + wide[k : k + 8]


def exchange(whole, one, two, size):
    ends = [(0, 0), (size - 1, size - 1)]
    across = [(i, (i - 1 ^ 1) + 1) for i in range(1, size - 1)]
    within = [(i, i ^ 1) for i in range(size)]
    if size != 8:
        outer_two = lax.ppermute(two, "space", across + ends)
        outer_one = lax.ppermute(one, "space", across + ends)
        inner = lax.ppermute(whole, "space", within)
        return inner, outer_one, outer_two, outer_two
    straight = [pair for pair in across if pair[0] not in (3, 4)]
    outer_two = lax.ppermute(two, "space", straight + [(3, 7), (7, 3), (4, 0), (0, 4)])
    outer_one = lax.ppermute(one, "space", across + ends)
    inner = lax.ppermute(whole, "space", within)
    stay = [(source, source) for source, target in straight]
    relayed = lax.ppermute(outer_two, "space", stay + [(7, 4), (0, 3), (3, 7), (4, 0)])
    return inner, outer_one, outer_two, relayed


def shaped(*shape):
    return jax.ShapeDtypeStruct(shape, F32)


def local(slices, space_size, starts, flags):
    half = shaped(2 * PLANES, TILES, 8, NZ)
    message = shaped(2 * PLANES + 2, TILES, 8, NZ)
    keep_shape = shaped(2, WINDOW, TILES, 8, NZ)
    buffers = [pltpu.VMEM((FIELDS, WINDOW, TILES + 2, 8, NZ), F32)] * 2
    opening = pl.pallas_call(
        prepare_kernel,
        out_shape=(shaped(PACKED + PLANES, TILES, 8, NZ), message, message),
        in_specs=[pl.BlockSpec(memory_space=pltpu.HBM)] * 2,
        out_specs=(VMEM,) * 3,
        scratch_shapes=[
            pltpu.VMEM(starts.shape, F32),
            pltpu.VMEM(flags.shape, flags.dtype),
            pltpu.SemaphoreType.DMA((2,)),
        ],
        compiler_params=params(),
        name="prepare",
    )(starts, flags)
    opening_near = exchange(*opening, space_size)
    *middle, keep = pl.pallas_call(
        functools.partial(first_kernel, space_size),
        out_shape=(shaped(PACKED, TILES, 8, NZ), half, half, keep_shape),
        in_specs=[VMEM] * 5,
        out_specs=(VMEM,) * 4,
        scratch_shapes=buffers,
        compiler_params=params(),
        name="first_round",
    )(opening[0], *opening_near)
    middle_near = exchange(*middle, space_size)
    guess = pl.pallas_call(
        functools.partial(guess_kernel, space_size),
        out_shape=shaped(PACKED, NZ),
        in_specs=[VMEM] * 5,
        out_specs=VMEM,
        compiler_params=params(),
        name="guess_old",
    )(opening[0], *opening_near)
    fine_end, jump = pl.pallas_call(
        functools.partial(second_kernel, space_size),
        out_shape=(shaped(PACKED, TILES, 8, NZ), shaped(slices * space_size, PACKED, NZ)),
        in_specs=[VMEM] * 7,
        out_specs=(VMEM, VMEM),
        scratch_shapes=buffers,
        compiler_params=params(),
        name="second_round",
    )(middle[0], *middle_near, keep, guess)
    jumps = lax.all_to_all(jump, ("tm", "space"), 0, 0)
    jumps = jumps.reshape(slices, space_size, PACKED, NZ)
    return pl.pallas_call(
        correct_kernel,
        out_shape=shaped(1, FIELDS, PLANES, NY, NZ),
        in_specs=[VMEM] * 3,
        out_specs=VMEM,
        scratch_shapes=[pltpu.VMEM((slices - 1, FIELDS, 8 * slices, NZ), F32)],
        compiler_params=params(),
        name="correct",
    )(jumps, guess, fine_end)


def solution(mesh):
    return jax.shard_map(
        functools.partial(local, mesh.shape["tm"], mesh.shape["space"]),
        mesh=mesh,
        in_specs=(P("tm", None, "space", None, None), P("space", None, None)),
        out_specs=P("tm", None, "space", None, None),
        check_vma=False,
    )
```

```python
import functools

import jax
import jax.numpy as jnp
from jax import lax
from jax.experimental import pallas as pl
from jax.experimental.pallas import tpu as pltpu
from jax.sharding import PartitionSpec as P

FINE_STEPS = 8
COARSE_STEPS = 2

fine_dt = 0.12
coarse_dt = 0.48

FIELDS = 4
PLANES = 4
NY = 64
NZ = 128
ROUND = 4
WINDOW = 3 * PLANES
TILES = NY // 8
GROUP = 4
PACKED = FIELDS * PLANES
F32 = jnp.float32
HIGHEST = lax.Precision.HIGHEST
VMEM = pl.BlockSpec(memory_space=pltpu.VMEM)
LIMIT = 48 * 2**20


def iota(shape, dim):
    return lax.broadcasted_iota(jnp.int32, shape, dim)


def params():
    return pltpu.CompilerParams(vmem_limit_bytes=LIMIT)


def prepare_kernel(starts, flags, message_one, message_two, fields, kinds, sems):
    copies = [pltpu.make_async_copy(starts, fields, sems.at[0]), pltpu.make_async_copy(flags, kinds, sems.at[1])]
    for copy in copies:
        copy.start()
    for copy in copies:
        copy.wait()
    for f in range(FIELDS):
        message = message_one if f < 2 else message_two
        for x in range(PLANES):
            for t in range(TILES):
                v = fields[0, f, x, pl.ds(t, 8, stride=8), :]
                message[f % 2 * PLANES + x, t] = v * 0.5 if f == 0 else v
    for x in range(PLANES):
        message = message_one if x < 2 else message_two
        for t in range(TILES):
            message[2 * PLANES + x % 2, t] = kinds[x, pl.ds(t, 8, stride=8), :].astype(F32)


def fine_tile(mid, lo_x, hi_x, lo_y, hi_y, kv, ks, kc, low_lane, high_lane):
    beta = 1.0 / fine_dt - 7.0
    alpha = 1.0 / fine_dt - 6.0
    lo_z = [jnp.where(low_lane, 0.0, pltpu.roll(v, 1, 1)) for v in mid]
    hi_z = [jnp.where(high_lane, 0.0, pltpu.roll(v, NZ - 1, 1)) for v in mid]
    total = [((lo_x[f] + hi_x[f]) + (lo_y[f] + hi_y[f])) + (lo_z[f] + hi_z[f]) for f in range(FIELDS)]
    w, a, b, c = mid
    gx = hi_x[0] - lo_x[0]
    gy = hi_y[0] - lo_y[0]
    gz = hi_z[0] - lo_z[0]
    diverge = (hi_x[1] - lo_x[1]) + (hi_y[2] - lo_y[2]) + (hi_z[3] - lo_z[3])
    stretch = gz + beta
    new_w = kv * ((total[0] + 0.125 * diverge) + alpha * w)
    new_a = ks * ((total[1] + gx) + a * stretch)
    new_b = ks * ((total[2] + gy) + b * stretch)
    new_c = kc * ((total[3] + 2.0 * (gx * a + gy * b)) + ((stretch + gz) * c + 1.0))
    return new_w, new_a, new_b, new_c


def fine_plane(src, keep, p, valid, store):
    lane = iota((8, NZ), 1)
    low_lane, high_lane = lane == 0, lane == NZ - 1
    fields = range(FIELDS)
    kc = jnp.where(valid, fine_dt, 0.0).astype(F32)
    for begin in range(0, TILES, GROUP):
        tiles = range(begin, begin + GROUP)
        column = [[src[f, p, t] for f in fields] for t in range(begin, begin + GROUP + 2)]
        lo_x = [[src[f, p - 1, t + 1] for f in fields] for t in tiles]
        hi_x = [[src[f, p + 1, t + 1] for f in fields] for t in tiles]
        kept = [(keep[0, p, t], keep[1, p, t]) for t in tiles]
        fresh = [
            fine_tile(column[i + 1], lo_x[i], hi_x[i], column[i], column[i + 2], *kept[i], kc, low_lane, high_lane)
            for i in range(GROUP)
        ]
        for i, t in enumerate(tiles):
            for f in fields:
                store(f, t, fresh[i][f])


def put_tile(buffer, f, p, t, value):
    buffer[f, p, t + 1] = value
    row = iota((8, NZ), 0)
    if t == 0:
        buffer[f, p, TILES + 1] = jnp.where(row == 7, 0.0, pltpu.roll(value, 7, 0))
    if t == TILES - 1:
        buffer[f, p, 0] = jnp.where(row == 0, 0.0, pltpu.roll(value, 1, 0))


class Slabs:

    def __init__(self, space_size, own, near):
        place = lax.axis_index("space")
        self.own = own
        self.near = (near[:2], near[2:])
        self.from_first = (place % 2 == 1, place < turn(space_size))
        self.there = {0: place > 0, 2: place < space_size - 1}

    def row(self, j, half, k, t):
        if j == 1:
            return self.own[half][k, t]
        v, other = (ref[k, t] for ref in self.near[half])
        first = self.from_first[half]
        v = jnp.where(first, v, other) if j == 0 else jnp.where(first, other, v)
        return jnp.where(self.there[j], v, 0.0)

    def field(self, j, f, x, t):
        return self.row(j, f // 2, f % 2 * PLANES + x, t)

    def kind(self, j, x, t):
        return self.row(j, x // 2, 2 * PLANES + x % 2, t)


def inside(space_size, p):
    x = (lax.axis_index("space") - 1) * PLANES + p
    return (x >= 0) & (x < space_size * PLANES)


def fine_round(space_size, slabs, even, odd, keep, finish):
    for j in range(3):
        for x in range(PLANES):
            for f in range(FIELDS):
                for t in range(TILES):
                    put_tile(even, f, j * PLANES + x, t, slabs.field(j, f, x, t))

    for step in range(ROUND):
        src, dst = (even, odd) if step % 2 == 0 else (odd, even)
        many = PLANES + ROUND // 2 - 1 - step

        def body(i, carry, src=src, dst=dst, step=step, many=many):
            for k in range(many):
                p = step + 1 + i * many + k
                if step == ROUND - 1:
                    store = lambda f, t, value: finish(f, p - PLANES, t, value)
                else:
                    store = lambda f, t, value: put_tile(dst, f, p, t, value)
                fine_plane(src, keep, p, inside(space_size, p), store)
            return carry

        lax.fori_loop(0, 2, body, 0)


def first_kernel(space_size, own_one, own_two, inner, outer, x, y, ended_one, ended_two, keep, even, odd):
    slabs = Slabs(space_size, (own_one, own_two), (inner, outer, x, y))
    for j in range(3):
        for k in range(PLANES):
            p = j * PLANES + k
            scale = jnp.where(inside(space_size, p), fine_dt, 0.0).astype(F32)
            for t in range(TILES):
                kind = slabs.kind(j, k, t)
                keep[0, p, t] = jnp.where(kind != 1.0, scale, 0.0)
                keep[1, p, t] = jnp.where(kind != 2.0, scale, 0.0)

    def finish(f, x, t, value):
        ended = ended_one if f < 2 else ended_two
        ended[f % 2 * PLANES + x, t] = value

    fine_round(space_size, slabs, even, odd, keep, finish)


def coarse_rows(pair_of, count):
    pairs = count // 2
    pieces = []
    for k in range(pairs):
        for i in range(TILES // 2):
            pieces.append(pair_of(k, 2 * i) + pair_of(k, 2 * i + 1))
    stacked = jnp.concatenate(pieces, axis=0)
    gather = (iota((NZ, NZ), 0) // 16 == iota((NZ, NZ), 1) % 8).astype(F32)
    sums = jnp.dot(stacked, gather, precision=HIGHEST, preferred_element_type=F32)
    sums = sums * pick_rows(sums.shape)
    sums = sums.reshape(pairs, TILES // 2, 8, NZ)
    sums = (sums[:, 0] + sums[:, 1]) + (sums[:, 2] + sums[:, 3])
    return sums.reshape(pairs * 8, NZ)


def pick_rows(shape):
    row = iota(shape, 0)
    return (row % 8 % 4 * 4 + row // 8 % 4 == iota(shape, 1) // 8).astype(F32)


def halves(sums, rows):
    shape = (rows, sums.shape[0])
    add = (iota(shape, 0) == iota(shape, 1) // 4).astype(F32) * (1.0 / 64.0)
    return jnp.dot(add, sums, precision=HIGHEST, preferred_element_type=F32)


def row_shift(v, by):
    rows = v.shape[0]
    row = iota(v.shape, 0)
    rolled = pltpu.roll(v, (-by) % rows, 0)
    return jnp.where((row + by >= 0) & (row + by < rows), rolled, 0.0)


def coarse_neighbours(v):
    row = iota(v.shape, 0)
    lane = iota(v.shape, 1)
    lo_x, hi_x = row_shift(v, -2), row_shift(v, 2)
    up = pltpu.roll(v, NZ - 8, 1)
    hi_y = jnp.where(lane < NZ - 8, up, jnp.where(row % 2 == 0, row_shift(up, 1), 0.0))
    down = pltpu.roll(v, 8, 1)
    lo_y = jnp.where(lane >= 8, down, jnp.where(row % 2 == 1, row_shift(down, -1), 0.0))
    hi_z = jnp.where(lane % 8 == 7, 0.0, pltpu.roll(v, NZ - 1, 1))
    lo_z = jnp.where(lane % 8 == 0, 0.0, pltpu.roll(v, 1, 1))
    return lo_x, hi_x, lo_y, hi_y, lo_z, hi_z


def coarse_step(state):
    near = [coarse_neighbours(v) for v in state]
    w, a, b, c = state

    def lap(f):
        lo_x, hi_x, lo_y, hi_y, lo_z, hi_z = near[f]
        return (0.25 * ((lo_x + hi_x) + (lo_y + hi_y)) + (1.0 / 256.0) * (lo_z + hi_z)) - (1.0 + 2.0 / 256.0) * state[f]

    def grad(f, k):
        return (near[f][2 * k + 1] - near[f][2 * k]) * (1.0 / 32.0 if k == 2 else 0.25)

    gx, gy, gz = grad(0, 0), grad(0, 1), grad(0, 2)
    diverge = grad(1, 0) + grad(2, 1) + grad(3, 2)
    new_w = w + coarse_dt * (lap(0) + 0.5 * diverge)
    new_a = a + coarse_dt * (gx + a * gz - a + lap(1))
    new_b = b + coarse_dt * (gy + b * gz - b + lap(2))
    new_c = c + coarse_dt * (2.0 * (gx * a + gy * b + gz * c) - (c - 1.0) + lap(3))
    return new_w, new_a, new_b, new_c


def guess_kernel(space_size, own_one, own_two, inner, outer, x, y, guess):
    place = lax.axis_index("space")
    slabs = Slabs(space_size, (own_one, own_two), (inner, outer, x, y))
    rows = 16
    row = iota((rows, NZ), 0)
    plane = 2 * place - 2 + row // 2
    valid = (row < WINDOW) & (plane >= 0) & (plane < 2 * space_size)
    state = []
    for f in range(FIELDS):

        def pair_of(k, t, f=f):
            return slabs.field(k // 2, f, k % 2 * 2, t) + slabs.field(k // 2, f, k % 2 * 2 + 1, t)

        grid = halves(coarse_rows(pair_of, WINDOW), rows)
        state.append(grid * 2.0 if f == 0 else grid)
    for _ in range(COARSE_STEPS):
        state = [jnp.where(valid, v, 0.0) for v in coarse_step(state)]
    for f in range(FIELDS):
        guess[pl.ds(4 * f, 4), :] = state[f][4:8]


def second_kernel(space_size, own_one, own_two, inner, outer, x, y, keep, guess, fine_end, jump, even, odd):
    slabs = Slabs(space_size, (own_one, own_two), (inner, outer, x, y))

    def finish(f, x, t, value):
        fine_end[f * PLANES + x, t] = value * 2.0 if f == 0 else value

    fine_round(space_size, slabs, even, odd, keep, finish)
    ended = halves(coarse_rows(lambda k, t: fine_end[2 * k, t] + fine_end[2 * k + 1, t], PACKED), PACKED)
    jumped = ended - jnp.where(lax.axis_index("tm") == 0, 0.0, guess[...])
    for k in range(jump.shape[0]):
        jump[k] = jumped


def correct_kernel(jumps, others, guess, fine_end, out, grids):
    slices, space_size = jumps.shape[0] + 1, jumps.shape[1] * 2
    mine = lax.axis_index("tm")
    place = lax.axis_index("space")
    rows = grids.shape[2]
    centre = 4 * slices
    plane = 2 * (place - slices) + iota((rows, NZ), 0) // 2
    valid = (plane >= 0) & (plane < 2 * space_size)
    grids[...] = jnp.zeros_like(grids)
    for k in range(1, slices):
        m = jnp.maximum(mine - k, 0)
        for j in range(-k, k + 1):
            s = jnp.clip(place + j, 0, space_size - 1)
            source = jumps if j % 2 == 0 else others
            for f in range(FIELDS):
                grids[k - 1, f, pl.ds(centre + 4 * j, 4), :] = source[m, s // 2, pl.ds(4 * f, 4), :]
    state = None
    for k in range(slices - 1, -1, -1):
        ended = state
        if state is not None:
            for _ in range(COARSE_STEPS):
                ended = [jnp.where(valid, v, 0.0) for v in coarse_step(ended)]
        if k > 0:
            state = [jnp.where(valid, grids[k - 1, f], 0.0) for f in range(FIELDS)]
            if ended is not None:
                state = [state[f] + jnp.where(mine > k, ended[f], 0.0) for f in range(FIELDS)]
    row = iota((8, NZ), 0)
    pieces = []
    for f in range(FIELDS):
        for x in range(PLANES // 2):
            k = 2 * x
            lines = [
                ended[f][centre + k + half : centre + k + half + 1] - guess[pl.ds(4 * f + k + half, 1), :]
                for half in range(2)
            ]
            tile = jnp.where(row < 4, lines[0], lines[1])
            tile = jnp.where(mine == 0, 0.0, tile)
            pieces += [tile] * (TILES // 2)
    stacked = jnp.concatenate(pieces, axis=0)
    stacked = stacked * pick_rows(stacked.shape)
    spread = (iota((NZ, NZ), 0) % 8 == iota((NZ, NZ), 1) // 16).astype(F32)
    wide = jnp.dot(stacked, spread, precision=HIGHEST, preferred_element_type=F32)
    for f in range(FIELDS):
        for x in range(PLANES):
            for t in range(TILES):
                k = ((f * 2 + x // 2) * (TILES // 2) + t // 2) * 8
                out[0, f, x, pl.ds(t, 8, stride=8), :] = fine_end[f * PLANES + x, t] + wide[k : k + 8]


def relayed(size):
    return size == 8


def turn(size):
    return size // 2 if relayed(size) else size


def exchange(one, two, size):
    inner = [(i, i ^ 1) for i in range(size)]
    outer = [(0, 0)] + [(i, (i - 1 ^ 1) + 1) for i in range(1, size - 1)] + [(size - 1, size - 1)]
    if relayed(size):
        half = size // 2
        first = [(i, i + 1) for i in range(half - 1)] + [(half - 1, size - 1)]
        first += [(i, i - 1) for i in range(size - 1, half, -1)] + [(half, 0)]
        second = [(i, i - 1) for i in range(half - 1, 0, -1)] + [(0, half - 1)]
        second += [(i, i + 1) for i in range(half, size - 1)] + [(size - 1, half)]
    else:
        first = [(i, (i + 1) % size) for i in range(size)]
        second = [(i, (i - 1) % size) for i in range(size)]
    x = lax.ppermute(two, "space", first)
    across = lax.ppermute(one, "space", outer)
    within = lax.ppermute(one, "space", inner)
    if relayed(size):
        place = lax.axis_index("space")
        two = jnp.where((place == 0) | (place == size - 1), x, two)
    y = lax.ppermute(two, "space", second)
    return within, across, x, y


def shaped(*shape):
    return jax.ShapeDtypeStruct(shape, F32)


def local(slices, space_size, starts, flags):
    half = shaped(2 * PLANES, TILES, 8, NZ)
    message = shaped(2 * PLANES + 2, TILES, 8, NZ)
    keep_shape = shaped(2, WINDOW, TILES, 8, NZ)
    buffers = [pltpu.VMEM((FIELDS, WINDOW, TILES + 2, 8, NZ), F32)] * 2
    opening = pl.pallas_call(
        prepare_kernel,
        out_shape=(message, message),
        in_specs=[pl.BlockSpec(memory_space=pltpu.HBM)] * 2,
        out_specs=(VMEM,) * 2,
        scratch_shapes=[
            pltpu.VMEM(starts.shape, F32),
            pltpu.VMEM(flags.shape, flags.dtype),
            pltpu.SemaphoreType.DMA((2,)),
        ],
        compiler_params=params(),
        name="prepare",
    )(starts, flags)
    opening_near = exchange(*opening, space_size)
    *middle, keep = pl.pallas_call(
        functools.partial(first_kernel, space_size),
        out_shape=(half, half, keep_shape),
        in_specs=[VMEM] * 6,
        out_specs=(VMEM,) * 3,
        scratch_shapes=buffers,
        compiler_params=params(),
        name="first_round",
    )(*opening, *opening_near)
    middle_near = exchange(*middle, space_size)
    guess = pl.pallas_call(
        functools.partial(guess_kernel, space_size),
        out_shape=shaped(PACKED, NZ),
        in_specs=[VMEM] * 6,
        out_specs=VMEM,
        compiler_params=params(),
        name="guess_old",
    )(*opening, *opening_near)
    fine_end, jump = pl.pallas_call(
        functools.partial(second_kernel, space_size),
        out_shape=(shaped(PACKED, TILES, 8, NZ), shaped(slices * space_size // 2, PACKED, NZ)),
        in_specs=[VMEM] * 8,
        out_specs=(VMEM, VMEM),
        scratch_shapes=buffers,
        compiler_params=params(),
        name="second_round",
    )(*middle, *middle_near, keep, guess)
    members = [range(core, slices * space_size, 2) for core in range(2)]
    jumps = lax.all_to_all(jump, ("tm", "space"), 0, 0, axis_index_groups=[list(group) for group in members])
    jumps = jumps.reshape(slices, space_size // 2, PACKED, NZ)[: slices - 1]
    others = lax.ppermute(jumps, "space", [(i, i ^ 1) for i in range(space_size)])
    return pl.pallas_call(
        correct_kernel,
        out_shape=shaped(1, FIELDS, PLANES, NY, NZ),
        in_specs=[VMEM] * 4,
        out_specs=VMEM,
        scratch_shapes=[pltpu.VMEM((slices - 1, FIELDS, 8 * slices, NZ), F32)],
        compiler_params=params(),
        name="correct",
    )(jumps, others, guess, fine_end)


def solution(mesh):
    return jax.shard_map(
        functools.partial(local, mesh.shape["tm"], mesh.shape["space"]),
        mesh=mesh,
        in_specs=(P("tm", None, "space", None, None), P("space", None, None)),
        out_specs=P("tm", None, "space", None, None),
        check_vma=False,
    )
```

```python
import functools

import jax
import jax.numpy as jnp
from jax import lax
from jax.experimental import pallas as pl
from jax.experimental.pallas import tpu as pltpu
from jax.sharding import PartitionSpec as P

FINE_STEPS = 8
COARSE_STEPS = 2

fine_dt = 0.12
coarse_dt = 0.48

FIELDS = 4
PLANES = 4
NY = 64
NZ = 128
ROUND = 4
WINDOW = 3 * PLANES
TILES = NY // 8
GROUP = 4
PACKED = FIELDS * PLANES
F32 = jnp.float32
HIGHEST = lax.Precision.HIGHEST
VMEM = pl.BlockSpec(memory_space=pltpu.VMEM)
LIMIT = 48 * 2**20


def iota(shape, dim):
    return lax.broadcasted_iota(jnp.int32, shape, dim)


def params():
    return pltpu.CompilerParams(vmem_limit_bytes=LIMIT)


def prepare_kernel(space_size, starts, flags, one, two_x, two_y, fields, kinds, sems):
    low = lax.axis_index("space") < turn(space_size)
    copies = [pltpu.make_async_copy(starts, fields, sems.at[0]), pltpu.make_async_copy(flags, kinds, sems.at[1])]
    for copy in copies:
        copy.start()
    for copy in copies:
        copy.wait()
    for t in range(TILES):
        for f in range(FIELDS):
            for x in range(PLANES):
                v = fields[0, f, x, pl.ds(t, 8, stride=8), :]
                for message in (one,) if f < 2 else (two_x, two_y):
                    message[f % 2 * PLANES + x, t] = v * 0.5 if f == 0 else v
        kind = [kinds[x, pl.ds(t, 8, stride=8), :].astype(F32) for x in range(PLANES)]
        one[2 * PLANES, t], one[2 * PLANES + 1, t] = kind[1], kind[2]
        two_x[2 * PLANES, t] = jnp.where(low, kind[3], kind[0])
        two_y[2 * PLANES, t] = jnp.where(low, kind[0], kind[3])


def fine_tile(mid, lo_x, hi_x, lo_y, hi_y, kv, ks, kc, low_lane, high_lane):
    beta = 1.0 / fine_dt - 7.0
    alpha = 1.0 / fine_dt - 6.0
    lo_z = [jnp.where(low_lane, 0.0, pltpu.roll(v, 1, 1)) for v in mid]
    hi_z = [jnp.where(high_lane, 0.0, pltpu.roll(v, NZ - 1, 1)) for v in mid]
    total = [((lo_x[f] + hi_x[f]) + (lo_y[f] + hi_y[f])) + (lo_z[f] + hi_z[f]) for f in range(FIELDS)]
    w, a, b, c = mid
    gx = hi_x[0] - lo_x[0]
    gy = hi_y[0] - lo_y[0]
    gz = hi_z[0] - lo_z[0]
    diverge = (hi_x[1] - lo_x[1]) + (hi_y[2] - lo_y[2]) + (hi_z[3] - lo_z[3])
    stretch = gz + beta
    new_w = kv * ((total[0] + 0.125 * diverge) + alpha * w)
    new_a = ks * ((total[1] + gx) + a * stretch)
    new_b = ks * ((total[2] + gy) + b * stretch)
    new_c = kc * ((total[3] + 2.0 * (gx * a + gy * b)) + ((stretch + gz) * c + 1.0))
    return new_w, new_a, new_b, new_c


def fine_plane(src, keep, p, valid, store):
    lane = iota((8, NZ), 1)
    low_lane, high_lane = lane == 0, lane == NZ - 1
    fields = range(FIELDS)
    kc = jnp.where(valid, fine_dt, 0.0).astype(F32)
    for begin in range(0, TILES, GROUP):
        tiles = range(begin, begin + GROUP)
        column = [[src[f, p, t] for f in fields] for t in range(begin, begin + GROUP + 2)]
        lo_x = [[src[f, p - 1, t + 1] for f in fields] for t in tiles]
        hi_x = [[src[f, p + 1, t + 1] for f in fields] for t in tiles]
        kept = [(keep[0, p, t], keep[1, p, t]) for t in tiles]
        fresh = [
            fine_tile(column[i + 1], lo_x[i], hi_x[i], column[i], column[i + 2], *kept[i], kc, low_lane, high_lane)
            for i in range(GROUP)
        ]
        for i, t in enumerate(tiles):
            for f in fields:
                store(f, t, fresh[i][f])


def put_tile(buffer, f, p, t, value):
    buffer[f, p, t + 1] = value
    row = iota((8, NZ), 0)
    if t == 0:
        buffer[f, p, TILES + 1] = jnp.where(row == 7, 0.0, pltpu.roll(value, 7, 0))
    if t == TILES - 1:
        buffer[f, p, 0] = jnp.where(row == 0, 0.0, pltpu.roll(value, 1, 0))


class Slabs:

    def __init__(self, space_size, own, near):
        place = lax.axis_index("space")
        self.own = own
        self.near = (near[:2], near[2:])
        self.low = place < turn(space_size)
        self.from_first = (place % 2 == 1, self.low)
        self.there = {0: place > 0, 2: place < space_size - 1}

    def row(self, j, half, k, t):
        if j == 1:
            return self.own[half][k, t]
        v, other = (ref[k, t] for ref in self.near[half])
        first = self.from_first[half]
        v = jnp.where(first, v, other) if j == 0 else jnp.where(first, other, v)
        return jnp.where(self.there[j], v, 0.0)

    def field(self, j, f, x, t):
        return self.row(j, f // 2, f % 2 * PLANES + x, t)

    def kind(self, j, x, t):
        return self.row(j, 0, 2 * PLANES + x - 1, t) if x in (1, 2) else self.row(j, 1, 2 * PLANES, t)


def inside(space_size, p):
    x = (lax.axis_index("space") - 1) * PLANES + p
    return (x >= 0) & (x < space_size * PLANES)


def fine_round(space_size, slabs, even, odd, keep, finish):
    for j in range(3):
        for x in range(PLANES):
            for f in range(FIELDS):
                for t in range(TILES):
                    put_tile(even, f, j * PLANES + x, t, slabs.field(j, f, x, t))

    for step in range(ROUND):
        src, dst = (even, odd) if step % 2 == 0 else (odd, even)
        many = PLANES + ROUND // 2 - 1 - step

        def body(i, carry, src=src, dst=dst, step=step, many=many):
            for k in range(many):
                p = step + 1 + i * many + k
                if step == ROUND - 1:
                    store = lambda f, t, value: finish(f, p - PLANES, t, value)
                else:
                    store = lambda f, t, value: put_tile(dst, f, p, t, value)
                fine_plane(src, keep, p, inside(space_size, p), store)
            return carry

        lax.fori_loop(0, 2, body, 0)


def first_kernel(space_size, own_one, own_two, own_other, inner, outer, x, y, ended_one, ended_two, keep, even, odd):
    slabs = Slabs(space_size, (own_one, own_two), (inner, outer, x, y))
    for p in range(1, WINDOW - 1):
        j, k = p // PLANES, p % PLANES
        scale = jnp.where(inside(space_size, p), fine_dt, 0.0).astype(F32)
        for t in range(TILES):
            kind = slabs.kind(j, k, t)
            if j == 1 and k in (0, PLANES - 1):
                other = own_other[2 * PLANES, t]
                kind = jnp.where(slabs.low == (k == 0), other, kind)
            keep[0, p, t] = jnp.where(kind != 1.0, scale, 0.0)
            keep[1, p, t] = jnp.where(kind != 2.0, scale, 0.0)

    def finish(f, x, t, value):
        ended = ended_one if f < 2 else ended_two
        ended[f % 2 * PLANES + x, t] = value

    fine_round(space_size, slabs, even, odd, keep, finish)


def chosen(values, picks):
    parts, rest = [], values
    for _ in range(3):
        part = rest.astype(jnp.bfloat16)
        parts.append(part)
        rest = rest - part.astype(F32)
    stacked = jnp.concatenate(parts, axis=1)
    picks = jnp.concatenate([picks.astype(jnp.bfloat16)] * 3, axis=0)
    return jnp.dot(stacked, picks, preferred_element_type=F32)


def coarse_rows(pair_of, count):
    pairs = count // 2
    pieces = []
    for k in range(pairs):
        for i in range(TILES // 2):
            pieces.append(pair_of(k, 2 * i) + pair_of(k, 2 * i + 1))
    stacked = jnp.concatenate(pieces, axis=0)
    gather = (iota((NZ, NZ), 0) // 16 == iota((NZ, NZ), 1) % 8).astype(F32)
    sums = chosen(stacked, gather)
    sums = sums * pick_rows(sums.shape)
    sums = sums.reshape(pairs, TILES // 2, 8, NZ)
    sums = (sums[:, 0] + sums[:, 1]) + (sums[:, 2] + sums[:, 3])
    return sums.reshape(pairs * 8, NZ)


def pick_rows(shape):
    row = iota(shape, 0)
    return (row % 8 % 4 * 4 + row // 8 % 4 == iota(shape, 1) // 8).astype(F32)


def halves(sums, rows):
    shape = (rows, sums.shape[0])
    add = (iota(shape, 0) == iota(shape, 1) // 4).astype(F32) * (1.0 / 64.0)
    return jnp.dot(add, sums, precision=HIGHEST, preferred_element_type=F32)


def row_shift(v, by):
    rows = v.shape[0]
    row = iota(v.shape, 0)
    rolled = pltpu.roll(v, (-by) % rows, 0)
    return jnp.where((row + by >= 0) & (row + by < rows), rolled, 0.0)


def coarse_neighbours(v):
    row = iota(v.shape, 0)
    lane = iota(v.shape, 1)
    lo_x, hi_x = row_shift(v, -2), row_shift(v, 2)
    up = pltpu.roll(v, NZ - 8, 1)
    hi_y = jnp.where(lane < NZ - 8, up, jnp.where(row % 2 == 0, row_shift(up, 1), 0.0))
    down = pltpu.roll(v, 8, 1)
    lo_y = jnp.where(lane >= 8, down, jnp.where(row % 2 == 1, row_shift(down, -1), 0.0))
    hi_z = jnp.where(lane % 8 == 7, 0.0, pltpu.roll(v, NZ - 1, 1))
    lo_z = jnp.where(lane % 8 == 0, 0.0, pltpu.roll(v, 1, 1))
    return lo_x, hi_x, lo_y, hi_y, lo_z, hi_z


def coarse_step(state):
    near = [coarse_neighbours(v) for v in state]
    w, a, b, c = state

    def lap(f):
        lo_x, hi_x, lo_y, hi_y, lo_z, hi_z = near[f]
        return (0.25 * ((lo_x + hi_x) + (lo_y + hi_y)) + (1.0 / 256.0) * (lo_z + hi_z)) - (1.0 + 2.0 / 256.0) * state[f]

    def grad(f, k):
        return (near[f][2 * k + 1] - near[f][2 * k]) * (1.0 / 32.0 if k == 2 else 0.25)

    gx, gy, gz = grad(0, 0), grad(0, 1), grad(0, 2)
    diverge = grad(1, 0) + grad(2, 1) + grad(3, 2)
    new_w = w + coarse_dt * (lap(0) + 0.5 * diverge)
    new_a = a + coarse_dt * (gx + a * gz - a + lap(1))
    new_b = b + coarse_dt * (gy + b * gz - b + lap(2))
    new_c = c + coarse_dt * (2.0 * (gx * a + gy * b + gz * c) - (c - 1.0) + lap(3))
    return new_w, new_a, new_b, new_c


def guess_kernel(space_size, own_one, own_two, inner, outer, x, y, guess):
    place = lax.axis_index("space")
    slabs = Slabs(space_size, (own_one, own_two), (inner, outer, x, y))
    rows = 16
    row = iota((rows, NZ), 0)
    plane = 2 * place - 2 + row // 2
    valid = (row < WINDOW) & (plane >= 0) & (plane < 2 * space_size)
    state = []
    for f in range(FIELDS):

        def pair_of(k, t, f=f):
            return slabs.field(k // 2, f, k % 2 * 2, t) + slabs.field(k // 2, f, k % 2 * 2 + 1, t)

        grid = halves(coarse_rows(pair_of, WINDOW), rows)
        state.append(grid * 2.0 if f == 0 else grid)
    for _ in range(COARSE_STEPS):
        state = [jnp.where(valid, v, 0.0) for v in coarse_step(state)]
    for f in range(FIELDS):
        guess[pl.ds(4 * f, 4), :] = state[f][4:8]


def second_kernel(space_size, own_one, own_two, inner, outer, x, y, keep, guess, fine_end, jump, even, odd):
    slabs = Slabs(space_size, (own_one, own_two), (inner, outer, x, y))

    def finish(f, x, t, value):
        fine_end[f * PLANES + x, t] = value * 2.0 if f == 0 else value

    fine_round(space_size, slabs, even, odd, keep, finish)
    ended = halves(coarse_rows(lambda k, t: fine_end[2 * k, t] + fine_end[2 * k + 1, t], PACKED), PACKED)
    jumped = ended - jnp.where(lax.axis_index("tm") == 0, 0.0, guess[...])
    for k in range(jump.shape[0]):
        jump[k] = jumped


def correct_kernel(jumps, others, guess, fine_end, out, grids, result, sems):
    slices, space_size = jumps.shape[0] + 1, jumps.shape[1] * 2
    mine = lax.axis_index("tm")
    place = lax.axis_index("space")
    rows = grids.shape[2]
    centre = 4 * slices
    plane = 2 * (place - slices) + iota((rows, NZ), 0) // 2
    valid = (plane >= 0) & (plane < 2 * space_size)
    grids[...] = jnp.zeros_like(grids)
    for k in range(1, slices):
        m = jnp.maximum(mine - k, 0)
        for j in range(-k, k + 1):
            s = jnp.clip(place + j, 0, space_size - 1)
            source = jumps if j % 2 == 0 else others
            for f in range(FIELDS):
                grids[k - 1, f, pl.ds(centre + 4 * j, 4), :] = source[m, s // 2, pl.ds(4 * f, 4), :]
    state = None
    for k in range(slices - 1, -1, -1):
        ended = state
        if state is not None:
            for _ in range(COARSE_STEPS):
                ended = [jnp.where(valid, v, 0.0) for v in coarse_step(ended)]
        if k > 0:
            state = [jnp.where(valid, grids[k - 1, f], 0.0) for f in range(FIELDS)]
            if ended is not None:
                state = [state[f] + jnp.where(mine > k, ended[f], 0.0) for f in range(FIELDS)]
    row = iota((8, NZ), 0)
    pieces = []
    for f in range(FIELDS):
        for x in range(PLANES // 2):
            k = 2 * x
            lines = [
                ended[f][centre + k + half : centre + k + half + 1] - guess[pl.ds(4 * f + k + half, 1), :]
                for half in range(2)
            ]
            tile = jnp.where(row < 4, lines[0], lines[1])
            tile = jnp.where(mine == 0, 0.0, tile)
            pieces += [tile] * (TILES // 2)
    stacked = jnp.concatenate(pieces, axis=0)
    stacked = stacked * pick_rows(stacked.shape)
    spread = (iota((NZ, NZ), 0) % 8 == iota((NZ, NZ), 1) // 16).astype(F32)
    wide = chosen(stacked, spread)
    for f in range(FIELDS):
        for x in range(PLANES):
            for t in range(TILES):
                k = ((f * 2 + x // 2) * (TILES // 2) + t // 2) * 8
                result[f, x, pl.ds(t, 8, stride=8), :] = fine_end[f * PLANES + x, t] + wide[k : k + 8]
        pltpu.make_async_copy(result.at[f], out.at[0, f], sems.at[f]).start()
    for f in range(FIELDS):
        pltpu.make_async_copy(result.at[f], out.at[0, f], sems.at[f]).wait()


def relayed(size):
    return size == 8


def turn(size):
    return size // 2 if relayed(size) else size


def exchange(one, two_x, two_y, size):
    inner = [(i, i ^ 1) for i in range(size)]
    outer = [(0, 0)] + [(i, (i - 1 ^ 1) + 1) for i in range(1, size - 1)] + [(size - 1, size - 1)]
    if relayed(size):
        half = size // 2
        first = [(i, i + 1) for i in range(half - 1)] + [(half - 1, size - 1)]
        first += [(i, i - 1) for i in range(size - 1, half, -1)] + [(half, 0)]
        second = [(i, i - 1) for i in range(half - 1, 0, -1)] + [(0, half - 1)]
        second += [(i, i + 1) for i in range(half, size - 1)] + [(size - 1, half)]
    else:
        first = [(i, (i + 1) % size) for i in range(size)]
        second = [(i, (i - 1) % size) for i in range(size)]
    x = lax.ppermute(two_x, "space", first)
    across = lax.ppermute(one, "space", outer)
    within = lax.ppermute(one, "space", inner)
    if relayed(size):
        place = lax.axis_index("space")
        two_y = jnp.where((place == 0) | (place == size - 1), x, two_y)
    y = lax.ppermute(two_y, "space", second)
    return within, across, x, y


def shaped(*shape):
    return jax.ShapeDtypeStruct(shape, F32)


def local(slices, space_size, starts, flags):
    half = shaped(2 * PLANES, TILES, 8, NZ)
    message_one, message_two = shaped(2 * PLANES + 2, TILES, 8, NZ), shaped(2 * PLANES + 1, TILES, 8, NZ)
    keep_shape = shaped(2, WINDOW, TILES, 8, NZ)
    buffers = [pltpu.VMEM((FIELDS, WINDOW, TILES + 2, 8, NZ), F32)] * 2
    opening = pl.pallas_call(
        functools.partial(prepare_kernel, space_size),
        out_shape=(message_one, message_two, message_two),
        in_specs=[pl.BlockSpec(memory_space=pltpu.HBM)] * 2,
        out_specs=(VMEM,) * 3,
        scratch_shapes=[
            pltpu.VMEM(starts.shape, F32),
            pltpu.VMEM(flags.shape, flags.dtype),
            pltpu.SemaphoreType.DMA((2,)),
        ],
        compiler_params=params(),
        name="prepare",
    )(starts, flags)
    opening_near = exchange(*opening, space_size)
    *middle, keep = pl.pallas_call(
        functools.partial(first_kernel, space_size),
        out_shape=(half, half, keep_shape),
        in_specs=[VMEM] * 7,
        out_specs=(VMEM,) * 3,
        scratch_shapes=buffers,
        compiler_params=params(),
        name="first_round",
    )(*opening, *opening_near)
    middle_near = exchange(middle[0], middle[1], middle[1], space_size)
    guess = pl.pallas_call(
        functools.partial(guess_kernel, space_size),
        out_shape=shaped(PACKED, NZ),
        in_specs=[VMEM] * 6,
        out_specs=VMEM,
        compiler_params=params(),
        name="guess_old",
    )(*opening[:2], *opening_near)
    fine_end, jump = pl.pallas_call(
        functools.partial(second_kernel, space_size),
        out_shape=(shaped(PACKED, TILES, 8, NZ), shaped(slices * space_size // 2, PACKED, NZ)),
        in_specs=[VMEM] * 8,
        out_specs=(VMEM, VMEM),
        scratch_shapes=buffers,
        compiler_params=params(),
        name="second_round",
    )(*middle, *middle_near, keep, guess)
    members = [range(core, slices * space_size, 2) for core in range(2)]
    jumps = lax.all_to_all(jump, ("tm", "space"), 0, 0, axis_index_groups=[list(group) for group in members])
    jumps = jumps.reshape(slices, space_size // 2, PACKED, NZ)[: slices - 1]
    others = lax.ppermute(jumps, "space", [(i, i ^ 1) for i in range(space_size)])
    return pl.pallas_call(
        correct_kernel,
        out_shape=shaped(1, FIELDS, PLANES, NY, NZ),
        in_specs=[VMEM] * 4,
        out_specs=pl.BlockSpec(memory_space=pltpu.HBM),
        scratch_shapes=[
            pltpu.VMEM((slices - 1, FIELDS, 8 * slices, NZ), F32),
            pltpu.VMEM((FIELDS, PLANES, NY, NZ), F32),
            pltpu.SemaphoreType.DMA((FIELDS,)),
        ],
        compiler_params=params(),
        name="correct",
    )(jumps, others, guess, fine_end)


def solution(mesh):
    return jax.shard_map(
        functools.partial(local, mesh.shape["tm"], mesh.shape["space"]),
        mesh=mesh,
        in_specs=(P("tm", None, "space", None, None), P("space", None, None)),
        out_specs=P("tm", None, "space", None, None),
        check_vma=False,
    )
```

```python
import functools

import jax
import jax.numpy as jnp
from jax import lax
from jax.experimental import pallas as pl
from jax.experimental.pallas import tpu as pltpu
from jax.sharding import PartitionSpec as P

FINE_STEPS = 8
COARSE_STEPS = 2

fine_dt = 0.12
coarse_dt = 0.48

FIELDS = 4
PLANES = 4
NY = 64
NZ = 128
ROUND = 4
WINDOW = 3 * PLANES
TILES = NY // 8
GROUP = 4
PACKED = FIELDS * PLANES
F32 = jnp.float32
HIGHEST = lax.Precision.HIGHEST
VMEM = pl.BlockSpec(memory_space=pltpu.VMEM)
LIMIT = 48 * 2**20


def iota(shape, dim):
    return lax.broadcasted_iota(jnp.int32, shape, dim)


def params():
    return pltpu.CompilerParams(vmem_limit_bytes=LIMIT)


def prepare_kernel(space_size, starts, flags, one, two_x, two_y, fields, kinds, sems):
    low = lax.axis_index("space") < turn(space_size)
    copies = [pltpu.make_async_copy(starts, fields, sems.at[0]), pltpu.make_async_copy(flags, kinds, sems.at[1])]
    for copy in copies:
        copy.start()
    for copy in copies:
        copy.wait()
    for t in range(TILES):
        for f in range(FIELDS):
            for x in range(PLANES):
                v = fields[0, f, x, pl.ds(t, 8, stride=8), :]
                for message in (one,) if f < 2 else (two_x, two_y):
                    message[f % 2 * PLANES + x, t] = v * 0.5 if f == 0 else v
        kind = [kinds[x, pl.ds(t, 8, stride=8), :].astype(F32) for x in range(PLANES)]
        one[2 * PLANES, t], one[2 * PLANES + 1, t] = kind[1], kind[2]
        two_x[2 * PLANES, t] = jnp.where(low, kind[3], kind[0])
        two_y[2 * PLANES, t] = jnp.where(low, kind[0], kind[3])


def fine_tile(mid, lo_x, hi_x, lo_y, hi_y, kv, ks, kc, low_lane, high_lane):
    beta = 1.0 / fine_dt - 7.0
    alpha = 1.0 / fine_dt - 6.0
    lo_z = [jnp.where(low_lane, 0.0, pltpu.roll(v, 1, 1)) for v in mid]
    hi_z = [jnp.where(high_lane, 0.0, pltpu.roll(v, NZ - 1, 1)) for v in mid]
    total = [((lo_x[f] + hi_x[f]) + (lo_y[f] + hi_y[f])) + (lo_z[f] + hi_z[f]) for f in range(FIELDS)]
    w, a, b, c = mid
    gx = hi_x[0] - lo_x[0]
    gy = hi_y[0] - lo_y[0]
    gz = hi_z[0] - lo_z[0]
    diverge = (hi_x[1] - lo_x[1]) + (hi_y[2] - lo_y[2]) + (hi_z[3] - lo_z[3])
    stretch = gz + beta
    new_w = kv * ((total[0] + 0.125 * diverge) + alpha * w)
    new_a = ks * ((total[1] + gx) + a * stretch)
    new_b = ks * ((total[2] + gy) + b * stretch)
    new_c = kc * ((total[3] + 2.0 * (gx * a + gy * b)) + ((stretch + gz) * c + 1.0))
    return new_w, new_a, new_b, new_c


def fine_plane(src, keep, p, valid, store):
    lane = iota((8, NZ), 1)
    low_lane, high_lane = lane == 0, lane == NZ - 1
    fields = range(FIELDS)
    kc = jnp.where(valid, fine_dt, 0.0).astype(F32)
    for begin in range(0, TILES, GROUP):
        tiles = range(begin, begin + GROUP)
        column = [[src[f, p, t] for f in fields] for t in range(begin, begin + GROUP + 2)]
        lo_x = [[src[f, p - 1, t + 1] for f in fields] for t in tiles]
        hi_x = [[src[f, p + 1, t + 1] for f in fields] for t in tiles]
        kept = [(keep[0, p, t], keep[1, p, t]) for t in tiles]
        fresh = [
            fine_tile(column[i + 1], lo_x[i], hi_x[i], column[i], column[i + 2], *kept[i], kc, low_lane, high_lane)
            for i in range(GROUP)
        ]
        for i, t in enumerate(tiles):
            for f in fields:
                store(f, t, fresh[i][f])


def put_tile(buffer, f, p, t, value):
    buffer[f, p, t + 1] = value
    row = iota((8, NZ), 0)
    if t == 0:
        buffer[f, p, TILES + 1] = jnp.where(row == 7, 0.0, pltpu.roll(value, 7, 0))
    if t == TILES - 1:
        buffer[f, p, 0] = jnp.where(row == 0, 0.0, pltpu.roll(value, 1, 0))


class Slabs:

    def __init__(self, space_size, own, near):
        place = lax.axis_index("space")
        self.own = own
        self.near = (near[:2], near[2:])
        self.low = place < turn(space_size)
        self.from_first = (place % 2 == 1, self.low)
        self.there = {0: place > 0, 2: place < space_size - 1}

    def row(self, j, half, k, t):
        if j == 1:
            return self.own[half][k, t]
        v, other = (ref[k, t] for ref in self.near[half])
        first = self.from_first[half]
        v = jnp.where(first, v, other) if j == 0 else jnp.where(first, other, v)
        return jnp.where(self.there[j], v, 0.0)

    def field(self, j, f, x, t):
        return self.row(j, f // 2, f % 2 * PLANES + x, t)

    def kind(self, j, x, t):
        return self.row(j, 0, 2 * PLANES + x - 1, t) if x in (1, 2) else self.row(j, 1, 2 * PLANES, t)


def inside(space_size, p):
    x = (lax.axis_index("space") - 1) * PLANES + p
    return (x >= 0) & (x < space_size * PLANES)


def fine_round(space_size, slabs, even, odd, keep, finish):
    for j in range(3):
        for x in range(PLANES):
            for f in range(FIELDS):
                for t in range(TILES):
                    put_tile(even, f, j * PLANES + x, t, slabs.field(j, f, x, t))

    for step in range(ROUND):
        src, dst = (even, odd) if step % 2 == 0 else (odd, even)
        many = PLANES + ROUND // 2 - 1 - step

        def body(i, carry, src=src, dst=dst, step=step, many=many):
            for k in range(many):
                p = step + 1 + i * many + k
                if step == ROUND - 1:
                    store = lambda f, t, value: finish(f, p - PLANES, t, value)
                else:
                    store = lambda f, t, value: put_tile(dst, f, p, t, value)
                fine_plane(src, keep, p, inside(space_size, p), store)
            return carry

        lax.fori_loop(0, 2, body, 0)


def first_kernel(space_size, own_one, own_two, own_other, inner, outer, x, y, ended_one, ended_two, keep, even, odd):
    slabs = Slabs(space_size, (own_one, own_two), (inner, outer, x, y))
    for p in range(1, WINDOW - 1):
        j, k = p // PLANES, p % PLANES
        scale = jnp.where(inside(space_size, p), fine_dt, 0.0).astype(F32)
        for t in range(TILES):
            kind = slabs.kind(j, k, t)
            if j == 1 and k in (0, PLANES - 1):
                other = own_other[2 * PLANES, t]
                kind = jnp.where(slabs.low == (k == 0), other, kind)
            keep[0, p, t] = jnp.where(kind != 1.0, scale, 0.0)
            keep[1, p, t] = jnp.where(kind != 2.0, scale, 0.0)

    def finish(f, x, t, value):
        ended = ended_one if f < 2 else ended_two
        ended[f % 2 * PLANES + x, t] = value

    fine_round(space_size, slabs, even, odd, keep, finish)


def chosen(values, picks):
    parts, rest = [], values
    for _ in range(3):
        part = rest.astype(jnp.bfloat16)
        parts.append(part)
        rest = rest - part.astype(F32)
    stacked = jnp.concatenate(parts, axis=1)
    picks = jnp.concatenate([picks.astype(jnp.bfloat16)] * 3, axis=0)
    return jnp.dot(stacked, picks, preferred_element_type=F32)


def coarse_rows(pair_of, count):
    pairs = count // 2
    pieces = []
    for k in range(pairs):
        for i in range(TILES // 2):
            pieces.append(pair_of(k, 2 * i) + pair_of(k, 2 * i + 1))
    stacked = jnp.concatenate(pieces, axis=0)
    gather = (iota((NZ, NZ), 0) // 16 == iota((NZ, NZ), 1) % 8).astype(F32)
    sums = chosen(stacked, gather)
    sums = sums * pick_rows(sums.shape)
    sums = sums.reshape(pairs, TILES // 2, 8, NZ)
    sums = (sums[:, 0] + sums[:, 1]) + (sums[:, 2] + sums[:, 3])
    return sums.reshape(pairs * 8, NZ)


def pick_rows(shape):
    row = iota(shape, 0)
    return (row % 8 % 4 * 4 + row // 8 % 4 == iota(shape, 1) // 8).astype(F32)


def halves(sums, rows):
    shape = (rows, sums.shape[0])
    add = (iota(shape, 0) == iota(shape, 1) // 4).astype(F32) * (1.0 / 64.0)
    return jnp.dot(add, sums, precision=HIGHEST, preferred_element_type=F32)


def row_shift(v, by):
    rows = v.shape[0]
    row = iota(v.shape, 0)
    rolled = pltpu.roll(v, (-by) % rows, 0)
    return jnp.where((row + by >= 0) & (row + by < rows), rolled, 0.0)


def coarse_neighbours(v):
    row = iota(v.shape, 0)
    lane = iota(v.shape, 1)
    lo_x, hi_x = row_shift(v, -2), row_shift(v, 2)
    up = pltpu.roll(v, NZ - 8, 1)
    hi_y = jnp.where(lane < NZ - 8, up, jnp.where(row % 2 == 0, row_shift(up, 1), 0.0))
    down = pltpu.roll(v, 8, 1)
    lo_y = jnp.where(lane >= 8, down, jnp.where(row % 2 == 1, row_shift(down, -1), 0.0))
    hi_z = jnp.where(lane % 8 == 7, 0.0, pltpu.roll(v, NZ - 1, 1))
    lo_z = jnp.where(lane % 8 == 0, 0.0, pltpu.roll(v, 1, 1))
    return lo_x, hi_x, lo_y, hi_y, lo_z, hi_z


def coarse_step(state):
    near = [coarse_neighbours(v) for v in state]
    w, a, b, c = state

    def lap(f):
        lo_x, hi_x, lo_y, hi_y, lo_z, hi_z = near[f]
        return (0.25 * ((lo_x + hi_x) + (lo_y + hi_y)) + (1.0 / 256.0) * (lo_z + hi_z)) - (1.0 + 2.0 / 256.0) * state[f]

    def grad(f, k):
        return (near[f][2 * k + 1] - near[f][2 * k]) * (1.0 / 32.0 if k == 2 else 0.25)

    gx, gy, gz = grad(0, 0), grad(0, 1), grad(0, 2)
    diverge = grad(1, 0) + grad(2, 1) + grad(3, 2)
    new_w = w + coarse_dt * (lap(0) + 0.5 * diverge)
    new_a = a + coarse_dt * (gx + a * gz - a + lap(1))
    new_b = b + coarse_dt * (gy + b * gz - b + lap(2))
    new_c = c + coarse_dt * (2.0 * (gx * a + gy * b + gz * c) - (c - 1.0) + lap(3))
    return new_w, new_a, new_b, new_c


def guess_kernel(space_size, own_one, own_two, inner, outer, x, y, guess):
    place = lax.axis_index("space")
    slabs = Slabs(space_size, (own_one, own_two), (inner, outer, x, y))
    rows = 16
    row = iota((rows, NZ), 0)
    plane = 2 * place - 2 + row // 2
    valid = (row < WINDOW) & (plane >= 0) & (plane < 2 * space_size)
    state = []
    for f in range(FIELDS):

        def pair_of(k, t, f=f):
            return slabs.field(k // 2, f, k % 2 * 2, t) + slabs.field(k // 2, f, k % 2 * 2 + 1, t)

        grid = halves(coarse_rows(pair_of, WINDOW), rows)
        state.append(grid * 2.0 if f == 0 else grid)
    for _ in range(COARSE_STEPS):
        state = [jnp.where(valid, v, 0.0) for v in coarse_step(state)]
    for f in range(FIELDS):
        guess[pl.ds(4 * f, 4), :] = state[f][4:8]


def second_kernel(space_size, own_one, own_two, inner, outer, x, y, keep, guess, fine_end, jump, even, odd):
    slabs = Slabs(space_size, (own_one, own_two), (inner, outer, x, y))

    def finish(f, x, t, value):
        fine_end[f * PLANES + x, t] = value * 2.0 if f == 0 else value

    fine_round(space_size, slabs, even, odd, keep, finish)
    ended = halves(coarse_rows(lambda k, t: fine_end[2 * k, t] + fine_end[2 * k + 1, t], PACKED), PACKED)
    jumped = ended - jnp.where(lax.axis_index("tm") == 0, 0.0, guess[...])
    for k in range(jump.shape[0]):
        jump[k] = jumped


def correct_kernel(jumps, guess, fine_end, out, grids, result, sems):
    slices, space_size = jumps.shape[:2]
    mine = lax.axis_index("tm")
    place = lax.axis_index("space")
    rows = grids.shape[2]
    centre = 4 * slices
    plane = 2 * (place - slices) + iota((rows, NZ), 0) // 2
    valid = (plane >= 0) & (plane < 2 * space_size)
    grids[...] = jnp.zeros_like(grids)
    for k in range(1, slices):
        m = jnp.maximum(mine - k, 0)
        for j in range(-k, k + 1):
            s = jnp.clip(place + j, 0, space_size - 1)
            for f in range(FIELDS):
                grids[k - 1, f, pl.ds(centre + 4 * j, 4), :] = jumps[m, s, pl.ds(4 * f, 4), :]
    state = None
    for k in range(slices - 1, -1, -1):
        ended = state
        if state is not None:
            for _ in range(COARSE_STEPS):
                ended = [jnp.where(valid, v, 0.0) for v in coarse_step(ended)]
        if k > 0:
            state = [jnp.where(valid, grids[k - 1, f], 0.0) for f in range(FIELDS)]
            if ended is not None:
                state = [state[f] + jnp.where(mine > k, ended[f], 0.0) for f in range(FIELDS)]
    row = iota((8, NZ), 0)
    pieces = []
    for f in range(FIELDS):
        for x in range(PLANES // 2):
            k = 2 * x
            lines = [
                ended[f][centre + k + half : centre + k + half + 1] - guess[pl.ds(4 * f + k + half, 1), :]
                for half in range(2)
            ]
            tile = jnp.where(row < 4, lines[0], lines[1])
            tile = jnp.where(mine == 0, 0.0, tile)
            pieces += [tile] * (TILES // 2)
    stacked = jnp.concatenate(pieces, axis=0)
    stacked = stacked * pick_rows(stacked.shape)
    spread = (iota((NZ, NZ), 0) % 8 == iota((NZ, NZ), 1) // 16).astype(F32)
    wide = chosen(stacked, spread)
    for f in range(FIELDS):
        for x in range(PLANES):
            for t in range(TILES):
                k = ((f * 2 + x // 2) * (TILES // 2) + t // 2) * 8
                result[f, x, pl.ds(t, 8, stride=8), :] = fine_end[f * PLANES + x, t] + wide[k : k + 8]
        pltpu.make_async_copy(result.at[f], out.at[0, f], sems.at[f]).start()
    for f in range(FIELDS):
        pltpu.make_async_copy(result.at[f], out.at[0, f], sems.at[f]).wait()


def relayed(size):
    return size == 8


def turn(size):
    return size // 2 if relayed(size) else size


def exchange(one, two_x, two_y, size):
    inner = [(i, i ^ 1) for i in range(size)]
    outer = [(0, 0)] + [(i, (i - 1 ^ 1) + 1) for i in range(1, size - 1)] + [(size - 1, size - 1)]
    if relayed(size):
        half = size // 2
        first = [(i, i + 1) for i in range(half - 1)] + [(half - 1, size - 1)]
        first += [(i, i - 1) for i in range(size - 1, half, -1)] + [(half, 0)]
        second = [(i, i - 1) for i in range(half - 1, 0, -1)] + [(0, half - 1)]
        second += [(i, i + 1) for i in range(half, size - 1)] + [(size - 1, half)]
    else:
        first = [(i, (i + 1) % size) for i in range(size)]
        second = [(i, (i - 1) % size) for i in range(size)]
    x = lax.ppermute(two_x, "space", first)
    across = lax.ppermute(one, "space", outer)
    within = lax.ppermute(one, "space", inner)
    if relayed(size):
        place = lax.axis_index("space")
        two_y = jnp.where((place == 0) | (place == size - 1), x, two_y)
    y = lax.ppermute(two_y, "space", second)
    return within, across, x, y


def shaped(*shape):
    return jax.ShapeDtypeStruct(shape, F32)


def local(slices, space_size, starts, flags):
    half = shaped(2 * PLANES, TILES, 8, NZ)
    message_one, message_two = shaped(2 * PLANES + 2, TILES, 8, NZ), shaped(2 * PLANES + 1, TILES, 8, NZ)
    keep_shape = shaped(2, WINDOW, TILES, 8, NZ)
    buffers = [pltpu.VMEM((FIELDS, WINDOW, TILES + 2, 8, NZ), F32)] * 2
    opening = pl.pallas_call(
        functools.partial(prepare_kernel, space_size),
        out_shape=(message_one, message_two, message_two),
        in_specs=[pl.BlockSpec(memory_space=pltpu.HBM)] * 2,
        out_specs=(VMEM,) * 3,
        scratch_shapes=[
            pltpu.VMEM(starts.shape, F32),
            pltpu.VMEM(flags.shape, flags.dtype),
            pltpu.SemaphoreType.DMA((2,)),
        ],
        compiler_params=params(),
        name="prepare",
    )(starts, flags)
    opening_near = exchange(*opening, space_size)
    *middle, keep = pl.pallas_call(
        functools.partial(first_kernel, space_size),
        out_shape=(half, half, keep_shape),
        in_specs=[VMEM] * 7,
        out_specs=(VMEM,) * 3,
        scratch_shapes=buffers,
        compiler_params=params(),
        name="first_round",
    )(*opening, *opening_near)
    middle_near = exchange(middle[0], middle[1], middle[1], space_size)
    guess = pl.pallas_call(
        functools.partial(guess_kernel, space_size),
        out_shape=shaped(PACKED, NZ),
        in_specs=[VMEM] * 6,
        out_specs=VMEM,
        compiler_params=params(),
        name="guess_old",
    )(*opening[:2], *opening_near)
    fine_end, jump = pl.pallas_call(
        functools.partial(second_kernel, space_size),
        out_shape=(shaped(PACKED, TILES, 8, NZ), shaped(slices * space_size, PACKED, NZ)),
        in_specs=[VMEM] * 8,
        out_specs=(VMEM, VMEM),
        scratch_shapes=buffers,
        compiler_params=params(),
        name="second_round",
    )(*middle, *middle_near, keep, guess)
    jumps = lax.all_to_all(jump, ("tm", "space"), 0, 0)
    jumps = jumps.reshape(slices, space_size, PACKED, NZ)
    return pl.pallas_call(
        correct_kernel,
        out_shape=shaped(1, FIELDS, PLANES, NY, NZ),
        in_specs=[VMEM] * 3,
        out_specs=pl.BlockSpec(memory_space=pltpu.HBM),
        scratch_shapes=[
            pltpu.VMEM((slices - 1, FIELDS, 8 * slices, NZ), F32),
            pltpu.VMEM((FIELDS, PLANES, NY, NZ), F32),
            pltpu.SemaphoreType.DMA((FIELDS,)),
        ],
        compiler_params=params(),
        name="correct",
    )(jumps, guess, fine_end)


def solution(mesh):
    return jax.shard_map(
        functools.partial(local, mesh.shape["tm"], mesh.shape["space"]),
        mesh=mesh,
        in_specs=(P("tm", None, "space", None, None), P("space", None, None)),
        out_specs=P("tm", None, "space", None, None),
        check_vma=False,
    )
```

```python
import functools

import jax
import jax.numpy as jnp
from jax import lax
from jax.experimental import pallas as pl
from jax.experimental.pallas import tpu as pltpu
from jax.sharding import PartitionSpec as P

FINE_STEPS = 8
COARSE_STEPS = 2

fine_dt = 0.12
coarse_dt = 0.48

FIELDS = 4
PLANES = 4
NY = 64
NZ = 128
ROUND = 4
WINDOW = 3 * PLANES
TILES = NY // 8
GROUP = 4
PACKED = FIELDS * PLANES
F32 = jnp.float32
HIGHEST = lax.Precision.HIGHEST
VMEM = pl.BlockSpec(memory_space=pltpu.VMEM)
LIMIT = 48 * 2**20


def iota(shape, dim):
    return lax.broadcasted_iota(jnp.int32, shape, dim)


def params():
    return pltpu.CompilerParams(vmem_limit_bytes=LIMIT)


def prepare_kernel(space_size, starts, flags, one, two_x, two_y, fields, kinds, sems):
    low = lax.axis_index("space") < turn(space_size)
    copies = [pltpu.make_async_copy(starts, fields, sems.at[0]), pltpu.make_async_copy(flags, kinds, sems.at[1])]
    for copy in copies:
        copy.start()
    for copy in copies:
        copy.wait()
    for t in range(TILES):
        for f in range(FIELDS):
            for x in range(PLANES):
                v = fields[0, f, x, pl.ds(t, 8, stride=8), :]
                for message in (one,) if f < 2 else (two_x, two_y):
                    message[f % 2 * PLANES + x, t] = v * 0.5 if f == 0 else v
        kind = [kinds[x, pl.ds(t, 8, stride=8), :].astype(F32) for x in range(PLANES)]
        one[2 * PLANES, t], one[2 * PLANES + 1, t] = kind[1], kind[2]
        two_x[2 * PLANES, t] = jnp.where(low, kind[3], kind[0])
        two_y[2 * PLANES, t] = jnp.where(low, kind[0], kind[3])


def fine_tile(mid, lo_x, hi_x, lo_y, hi_y, kv, ks, kc, low_lane, high_lane):
    beta = 1.0 / fine_dt - 7.0
    alpha = 1.0 / fine_dt - 6.0
    lo_z = [jnp.where(low_lane, 0.0, pltpu.roll(v, 1, 1)) for v in mid]
    hi_z = [jnp.where(high_lane, 0.0, pltpu.roll(v, NZ - 1, 1)) for v in mid]
    total = [((lo_x[f] + hi_x[f]) + (lo_y[f] + hi_y[f])) + (lo_z[f] + hi_z[f]) for f in range(FIELDS)]
    w, a, b, c = mid
    gx = hi_x[0] - lo_x[0]
    gy = hi_y[0] - lo_y[0]
    gz = hi_z[0] - lo_z[0]
    diverge = (hi_x[1] - lo_x[1]) + (hi_y[2] - lo_y[2]) + (hi_z[3] - lo_z[3])
    stretch = gz + beta
    new_w = kv * ((total[0] + 0.125 * diverge) + alpha * w)
    new_a = ks * ((total[1] + gx) + a * stretch)
    new_b = ks * ((total[2] + gy) + b * stretch)
    new_c = kc * ((total[3] + 2.0 * (gx * a + gy * b)) + ((stretch + gz) * c + 1.0))
    return new_w, new_a, new_b, new_c


def fine_plane(src, keep, p, valid, store):
    lane = iota((8, NZ), 1)
    low_lane, high_lane = lane == 0, lane == NZ - 1
    fields = range(FIELDS)
    kc = jnp.where(valid, fine_dt, 0.0).astype(F32)
    for begin in range(0, TILES, GROUP):
        tiles = range(begin, begin + GROUP)
        column = [[src[f, p, t] for f in fields] for t in range(begin, begin + GROUP + 2)]
        lo_x = [[src[f, p - 1, t + 1] for f in fields] for t in tiles]
        hi_x = [[src[f, p + 1, t + 1] for f in fields] for t in tiles]
        kept = [(keep[0, p, t], keep[1, p, t]) for t in tiles]
        fresh = [
            fine_tile(column[i + 1], lo_x[i], hi_x[i], column[i], column[i + 2], *kept[i], kc, low_lane, high_lane)
            for i in range(GROUP)
        ]
        for i, t in enumerate(tiles):
            for f in fields:
                store(f, t, fresh[i][f])


def put_tile(buffer, f, p, t, value):
    buffer[f, p, t + 1] = value
    row = iota((8, NZ), 0)
    if t == 0:
        buffer[f, p, TILES + 1] = jnp.where(row == 7, 0.0, pltpu.roll(value, 7, 0))
    if t == TILES - 1:
        buffer[f, p, 0] = jnp.where(row == 0, 0.0, pltpu.roll(value, 1, 0))


class Slabs:

    def __init__(self, space_size, own, near):
        place = lax.axis_index("space")
        self.own = own
        self.near = (near[:2], near[2:])
        self.low = place < turn(space_size)
        self.from_first = (place % 2 == 1, self.low)
        self.there = {0: place > 0, 2: place < space_size - 1}

    def row(self, j, half, k, t):
        if j == 1:
            return self.own[half][k, t]
        v, other = (ref[k, t] for ref in self.near[half])
        first = self.from_first[half]
        v = jnp.where(first, v, other) if j == 0 else jnp.where(first, other, v)
        return jnp.where(self.there[j], v, 0.0)

    def field(self, j, f, x, t):
        return self.row(j, f // 2, f % 2 * PLANES + x, t)

    def kind(self, j, x, t):
        return self.row(j, 0, 2 * PLANES + x - 1, t) if x in (1, 2) else self.row(j, 1, 2 * PLANES, t)


def inside(space_size, p):
    x = (lax.axis_index("space") - 1) * PLANES + p
    return (x >= 0) & (x < space_size * PLANES)


def fine_round(space_size, slabs, even, odd, keep, finish):
    for j in range(3):
        for x in range(PLANES):
            for f in range(FIELDS):
                for t in range(TILES):
                    put_tile(even, f, j * PLANES + x, t, slabs.field(j, f, x, t))

    for step in range(ROUND):
        src, dst = (even, odd) if step % 2 == 0 else (odd, even)
        for p in range(step + 1, WINDOW - 1 - step):
            if step == ROUND - 1:
                store = lambda f, t, value: finish(f, p - PLANES, t, value)
            else:
                store = lambda f, t, value: put_tile(dst, f, p, t, value)
            fine_plane(src, keep, p, inside(space_size, p), store)


def first_kernel(space_size, own_one, own_two, own_other, inner, outer, x, y, ended_one, ended_two, keep, even, odd):
    slabs = Slabs(space_size, (own_one, own_two), (inner, outer, x, y))
    for p in range(1, WINDOW - 1):
        j, k = p // PLANES, p % PLANES
        scale = jnp.where(inside(space_size, p), fine_dt, 0.0).astype(F32)
        for t in range(TILES):
            kind = slabs.kind(j, k, t)
            if j == 1 and k in (0, PLANES - 1):
                other = own_other[2 * PLANES, t]
                kind = jnp.where(slabs.low == (k == 0), other, kind)
            keep[0, p, t] = jnp.where(kind != 1.0, scale, 0.0)
            keep[1, p, t] = jnp.where(kind != 2.0, scale, 0.0)

    def finish(f, x, t, value):
        ended = ended_one if f < 2 else ended_two
        ended[f % 2 * PLANES + x, t] = value

    fine_round(space_size, slabs, even, odd, keep, finish)


def chosen(values, picks):
    parts, rest = [], values
    for _ in range(3):
        part = rest.astype(jnp.bfloat16)
        parts.append(part)
        rest = rest - part.astype(F32)
    stacked = jnp.concatenate(parts, axis=1)
    picks = jnp.concatenate([picks.astype(jnp.bfloat16)] * 3, axis=0)
    return jnp.dot(stacked, picks, preferred_element_type=F32)


def coarse_rows(pair_of, count):
    pairs = count // 2
    pieces = []
    for k in range(pairs):
        for i in range(TILES // 2):
            pieces.append(pair_of(k, 2 * i) + pair_of(k, 2 * i + 1))
    stacked = jnp.concatenate(pieces, axis=0)
    gather = (iota((NZ, NZ), 0) // 16 == iota((NZ, NZ), 1) % 8).astype(F32)
    sums = chosen(stacked, gather)
    sums = sums * pick_rows(sums.shape)
    sums = sums.reshape(pairs, TILES // 2, 8, NZ)
    sums = (sums[:, 0] + sums[:, 1]) + (sums[:, 2] + sums[:, 3])
    return sums.reshape(pairs * 8, NZ)


def pick_rows(shape):
    row = iota(shape, 0)
    return (row % 8 % 4 * 4 + row // 8 % 4 == iota(shape, 1) // 8).astype(F32)


def halves(sums, rows):
    shape = (rows, sums.shape[0])
    add = (iota(shape, 0) == iota(shape, 1) // 4).astype(F32) * (1.0 / 64.0)
    return jnp.dot(add, sums, precision=HIGHEST, preferred_element_type=F32)


def row_shift(v, by):
    rows = v.shape[0]
    row = iota(v.shape, 0)
    rolled = pltpu.roll(v, (-by) % rows, 0)
    return jnp.where((row + by >= 0) & (row + by < rows), rolled, 0.0)


def coarse_neighbours(v):
    row = iota(v.shape, 0)
    lane = iota(v.shape, 1)
    lo_x, hi_x = row_shift(v, -2), row_shift(v, 2)
    up = pltpu.roll(v, NZ - 8, 1)
    hi_y = jnp.where(lane < NZ - 8, up, jnp.where(row % 2 == 0, row_shift(up, 1), 0.0))
    down = pltpu.roll(v, 8, 1)
    lo_y = jnp.where(lane >= 8, down, jnp.where(row % 2 == 1, row_shift(down, -1), 0.0))
    hi_z = jnp.where(lane % 8 == 7, 0.0, pltpu.roll(v, NZ - 1, 1))
    lo_z = jnp.where(lane % 8 == 0, 0.0, pltpu.roll(v, 1, 1))
    return lo_x, hi_x, lo_y, hi_y, lo_z, hi_z


def coarse_step(state):
    near = [coarse_neighbours(v) for v in state]
    w, a, b, c = state

    def lap(f):
        lo_x, hi_x, lo_y, hi_y, lo_z, hi_z = near[f]
        return (0.25 * ((lo_x + hi_x) + (lo_y + hi_y)) + (1.0 / 256.0) * (lo_z + hi_z)) - (1.0 + 2.0 / 256.0) * state[f]

    def grad(f, k):
        return (near[f][2 * k + 1] - near[f][2 * k]) * (1.0 / 32.0 if k == 2 else 0.25)

    gx, gy, gz = grad(0, 0), grad(0, 1), grad(0, 2)
    diverge = grad(1, 0) + grad(2, 1) + grad(3, 2)
    new_w = w + coarse_dt * (lap(0) + 0.5 * diverge)
    new_a = a + coarse_dt * (gx + a * gz - a + lap(1))
    new_b = b + coarse_dt * (gy + b * gz - b + lap(2))
    new_c = c + coarse_dt * (2.0 * (gx * a + gy * b + gz * c) - (c - 1.0) + lap(3))
    return new_w, new_a, new_b, new_c


def guess_kernel(space_size, own_one, own_two, inner, outer, x, y, guess):
    place = lax.axis_index("space")
    slabs = Slabs(space_size, (own_one, own_two), (inner, outer, x, y))
    rows = 16
    row = iota((rows, NZ), 0)
    plane = 2 * place - 2 + row // 2
    valid = (row < WINDOW) & (plane >= 0) & (plane < 2 * space_size)
    state = []
    for f in range(FIELDS):

        def pair_of(k, t, f=f):
            return slabs.field(k // 2, f, k % 2 * 2, t) + slabs.field(k // 2, f, k % 2 * 2 + 1, t)

        grid = halves(coarse_rows(pair_of, WINDOW), rows)
        state.append(grid * 2.0 if f == 0 else grid)
    for _ in range(COARSE_STEPS):
        state = [jnp.where(valid, v, 0.0) for v in coarse_step(state)]
    for f in range(FIELDS):
        guess[pl.ds(4 * f, 4), :] = state[f][4:8]


def second_kernel(space_size, own_one, own_two, inner, outer, x, y, keep, guess, fine_end, jump, even, odd):
    slabs = Slabs(space_size, (own_one, own_two), (inner, outer, x, y))

    def finish(f, x, t, value):
        fine_end[f * PLANES + x, t] = value * 2.0 if f == 0 else value

    fine_round(space_size, slabs, even, odd, keep, finish)
    ended = halves(coarse_rows(lambda k, t: fine_end[2 * k, t] + fine_end[2 * k + 1, t], PACKED), PACKED)
    jumped = ended - jnp.where(lax.axis_index("tm") == 0, 0.0, guess[...])
    for k in range(jump.shape[0]):
        jump[k] = jumped


def correct_kernel(jumps, others, guess, fine_end, out, grids, result, sems):
    slices, space_size = jumps.shape[0] + 1, jumps.shape[1] * 2
    mine = lax.axis_index("tm")
    place = lax.axis_index("space")
    rows = grids.shape[2]
    centre = 4 * slices
    plane = 2 * (place - slices) + iota((rows, NZ), 0) // 2
    valid = (plane >= 0) & (plane < 2 * space_size)
    grids[...] = jnp.zeros_like(grids)
    for k in range(1, slices):
        m = jnp.maximum(mine - k, 0)
        for j in range(-k, k + 1):
            s = jnp.clip(place + j, 0, space_size - 1)
            source = jumps if j % 2 == 0 else others
            for f in range(FIELDS):
                grids[k - 1, f, pl.ds(centre + 4 * j, 4), :] = source[m, s // 2, pl.ds(4 * f, 4), :]
    state = None
    for k in range(slices - 1, -1, -1):
        ended = state
        if state is not None:
            for _ in range(COARSE_STEPS):
                ended = [jnp.where(valid, v, 0.0) for v in coarse_step(ended)]
        if k > 0:
            state = [jnp.where(valid, grids[k - 1, f], 0.0) for f in range(FIELDS)]
            if ended is not None:
                state = [state[f] + jnp.where(mine > k, ended[f], 0.0) for f in range(FIELDS)]
    row = iota((8, NZ), 0)
    pieces = []
    for f in range(FIELDS):
        for x in range(PLANES // 2):
            k = 2 * x
            lines = [
                ended[f][centre + k + half : centre + k + half + 1] - guess[pl.ds(4 * f + k + half, 1), :]
                for half in range(2)
            ]
            tile = jnp.where(row < 4, lines[0], lines[1])
            tile = jnp.where(mine == 0, 0.0, tile)
            pieces += [tile] * (TILES // 2)
    stacked = jnp.concatenate(pieces, axis=0)
    stacked = stacked * pick_rows(stacked.shape)
    spread = (iota((NZ, NZ), 0) % 8 == iota((NZ, NZ), 1) // 16).astype(F32)
    wide = chosen(stacked, spread)
    for f in range(FIELDS):
        for x in range(PLANES):
            for t in range(TILES):
                k = ((f * 2 + x // 2) * (TILES // 2) + t // 2) * 8
                result[f, x, pl.ds(t, 8, stride=8), :] = fine_end[f * PLANES + x, t] + wide[k : k + 8]
        pltpu.make_async_copy(result.at[f], out.at[0, f], sems.at[f]).start()
    for f in range(FIELDS):
        pltpu.make_async_copy(result.at[f], out.at[0, f], sems.at[f]).wait()


def relayed(size):
    return size == 8


def turn(size):
    return size // 2 if relayed(size) else size


def exchange(one, two_x, two_y, size):
    inner = [(i, i ^ 1) for i in range(size)]
    outer = [(0, 0)] + [(i, (i - 1 ^ 1) + 1) for i in range(1, size - 1)] + [(size - 1, size - 1)]
    if relayed(size):
        half = size // 2
        first = [(i, i + 1) for i in range(half - 1)] + [(half - 1, size - 1)]
        first += [(i, i - 1) for i in range(size - 1, half, -1)] + [(half, 0)]
        second = [(i, i - 1) for i in range(half - 1, 0, -1)] + [(0, half - 1)]
        second += [(i, i + 1) for i in range(half, size - 1)] + [(size - 1, half)]
    else:
        first = [(i, (i + 1) % size) for i in range(size)]
        second = [(i, (i - 1) % size) for i in range(size)]
    x = lax.ppermute(two_x, "space", first)
    across = lax.ppermute(one, "space", outer)
    within = lax.ppermute(one, "space", inner)
    if relayed(size):
        place = lax.axis_index("space")
        two_y = jnp.where((place == 0) | (place == size - 1), x, two_y)
    y = lax.ppermute(two_y, "space", second)
    return within, across, x, y


def shaped(*shape):
    return jax.ShapeDtypeStruct(shape, F32)


def local(slices, space_size, starts, flags):
    half = shaped(2 * PLANES, TILES, 8, NZ)
    message_one, message_two = shaped(2 * PLANES + 2, TILES, 8, NZ), shaped(2 * PLANES + 1, TILES, 8, NZ)
    keep_shape = shaped(2, WINDOW, TILES, 8, NZ)
    buffers = [pltpu.VMEM((FIELDS, WINDOW, TILES + 2, 8, NZ), F32)] * 2
    opening = pl.pallas_call(
        functools.partial(prepare_kernel, space_size),
        out_shape=(message_one, message_two, message_two),
        in_specs=[pl.BlockSpec(memory_space=pltpu.HBM)] * 2,
        out_specs=(VMEM,) * 3,
        scratch_shapes=[
            pltpu.VMEM(starts.shape, F32),
            pltpu.VMEM(flags.shape, flags.dtype),
            pltpu.SemaphoreType.DMA((2,)),
        ],
        compiler_params=params(),
        name="prepare",
    )(starts, flags)
    opening_near = exchange(*opening, space_size)
    *middle, keep = pl.pallas_call(
        functools.partial(first_kernel, space_size),
        out_shape=(half, half, keep_shape),
        in_specs=[VMEM] * 7,
        out_specs=(VMEM,) * 3,
        scratch_shapes=buffers,
        compiler_params=params(),
        name="first_round",
    )(*opening, *opening_near)
    middle_near = exchange(middle[0], middle[1], middle[1], space_size)
    guess = pl.pallas_call(
        functools.partial(guess_kernel, space_size),
        out_shape=shaped(PACKED, NZ),
        in_specs=[VMEM] * 6,
        out_specs=VMEM,
        compiler_params=params(),
        name="guess_old",
    )(*opening[:2], *opening_near)
    fine_end, jump = pl.pallas_call(
        functools.partial(second_kernel, space_size),
        out_shape=(shaped(PACKED, TILES, 8, NZ), shaped(slices * space_size // 2, PACKED, NZ)),
        in_specs=[VMEM] * 8,
        out_specs=(VMEM, VMEM),
        scratch_shapes=buffers,
        compiler_params=params(),
        name="second_round",
    )(*middle, *middle_near, keep, guess)
    members = [range(core, slices * space_size, 2) for core in range(2)]
    jumps = lax.all_to_all(jump, ("tm", "space"), 0, 0, axis_index_groups=[list(group) for group in members])
    jumps = jumps.reshape(slices, space_size // 2, PACKED, NZ)[: slices - 1]
    others = lax.ppermute(jumps, "space", [(i, i ^ 1) for i in range(space_size)])
    return pl.pallas_call(
        correct_kernel,
        out_shape=shaped(1, FIELDS, PLANES, NY, NZ),
        in_specs=[VMEM] * 4,
        out_specs=pl.BlockSpec(memory_space=pltpu.HBM),
        scratch_shapes=[
            pltpu.VMEM((slices - 1, FIELDS, 8 * slices, NZ), F32),
            pltpu.VMEM((FIELDS, PLANES, NY, NZ), F32),
            pltpu.SemaphoreType.DMA((FIELDS,)),
        ],
        compiler_params=params(),
        name="correct",
    )(jumps, others, guess, fine_end)


def solution(mesh):
    return jax.shard_map(
        functools.partial(local, mesh.shape["tm"], mesh.shape["space"]),
        mesh=mesh,
        in_specs=(P("tm", None, "space", None, None), P("space", None, None)),
        out_specs=P("tm", None, "space", None, None),
        check_vma=False,
    )
```

```python
import functools

import jax
import jax.numpy as jnp
from jax import lax
from jax.experimental import pallas as pl
from jax.experimental.pallas import tpu as pltpu
from jax.sharding import PartitionSpec as P

FINE_STEPS = 8
COARSE_STEPS = 2

fine_dt = 0.12
coarse_dt = 0.48

FIELDS = 4
PLANES = 4
NY = 64
NZ = 128
ROUND = 4
WINDOW = 3 * PLANES
TILES = NY // 8
GROUP = 4
PACKED = FIELDS * PLANES
F32 = jnp.float32
HIGHEST = lax.Precision.HIGHEST
VMEM = pl.BlockSpec(memory_space=pltpu.VMEM)
LIMIT = 48 * 2**20


def iota(shape, dim):
    return lax.broadcasted_iota(jnp.int32, shape, dim)


def params():
    return pltpu.CompilerParams(vmem_limit_bytes=LIMIT)


def prepare_kernel(space_size, starts, flags, one, two_x, two_y, fields, kinds, sems):
    low = lax.axis_index("space") < turn(space_size)
    copies = [pltpu.make_async_copy(starts, fields, sems.at[0]), pltpu.make_async_copy(flags, kinds, sems.at[1])]
    for copy in copies:
        copy.start()
    for copy in copies:
        copy.wait()
    for t in range(TILES):
        for f in range(FIELDS):
            for x in range(PLANES):
                v = fields[0, f, x, pl.ds(t, 8, stride=8), :]
                for message in (one,) if f < 2 else (two_x, two_y):
                    message[f % 2 * PLANES + x, t] = v * 0.5 if f == 0 else v
        kind = [kinds[x, pl.ds(t, 8, stride=8), :].astype(F32) for x in range(PLANES)]
        one[2 * PLANES, t], one[2 * PLANES + 1, t] = kind[1], kind[2]
        two_x[2 * PLANES, t] = jnp.where(low, kind[3], kind[0])
        two_y[2 * PLANES, t] = jnp.where(low, kind[0], kind[3])


def fine_tile(mid, lo_x, hi_x, lo_y, hi_y, kv, ks, kc, low_lane, high_lane):
    beta = 1.0 / fine_dt - 7.0
    alpha = 1.0 / fine_dt - 6.0
    lo_z = [jnp.where(low_lane, 0.0, pltpu.roll(v, 1, 1)) for v in mid]
    hi_z = [jnp.where(high_lane, 0.0, pltpu.roll(v, NZ - 1, 1)) for v in mid]
    total = [((lo_x[f] + hi_x[f]) + (lo_y[f] + hi_y[f])) + (lo_z[f] + hi_z[f]) for f in range(FIELDS)]
    w, a, b, c = mid
    gx = hi_x[0] - lo_x[0]
    gy = hi_y[0] - lo_y[0]
    gz = hi_z[0] - lo_z[0]
    diverge = (hi_x[1] - lo_x[1]) + (hi_y[2] - lo_y[2]) + (hi_z[3] - lo_z[3])
    stretch = gz + beta
    new_w = kv * ((total[0] + 0.125 * diverge) + alpha * w)
    new_a = ks * ((total[1] + gx) + a * stretch)
    new_b = ks * ((total[2] + gy) + b * stretch)
    new_c = kc * ((total[3] + 2.0 * (gx * a + gy * b)) + ((stretch + gz) * c + 1.0))
    return new_w, new_a, new_b, new_c


def fine_plane(src, keep, p, valid, store):
    lane = iota((8, NZ), 1)
    low_lane, high_lane = lane == 0, lane == NZ - 1
    fields = range(FIELDS)
    kc = jnp.where(valid, fine_dt, 0.0).astype(F32)
    for begin in range(0, TILES, GROUP):
        tiles = range(begin, begin + GROUP)
        column = [[src(p)[f, p, t] for f in fields] for t in range(begin, begin + GROUP + 2)]
        lo_x = [[src(p - 1)[f, p - 1, t + 1] for f in fields] for t in tiles]
        hi_x = [[src(p + 1)[f, p + 1, t + 1] for f in fields] for t in tiles]
        kept = [(keep[0, p, t], keep[1, p, t]) for t in tiles]
        fresh = [
            fine_tile(column[i + 1], lo_x[i], hi_x[i], column[i], column[i + 2], *kept[i], kc, low_lane, high_lane)
            for i in range(GROUP)
        ]
        for i, t in enumerate(tiles):
            for f in fields:
                store(f, t, fresh[i][f])


def put_tile(buffer, f, p, t, value):
    buffer[f, p, t + 1] = value
    row = iota((8, NZ), 0)
    if t == 0:
        buffer[f, p, TILES + 1] = jnp.where(row == 7, 0.0, pltpu.roll(value, 7, 0))
    if t == TILES - 1:
        buffer[f, p, 0] = jnp.where(row == 0, 0.0, pltpu.roll(value, 1, 0))


class Slabs:

    def __init__(self, space_size, own, near):
        place = lax.axis_index("space")
        self.own = own
        self.near = (near[:2], near[2:])
        self.low = place < turn(space_size)
        self.from_first = (place % 2 == 1, self.low)
        self.there = {0: place > 0, 2: place < space_size - 1}

    def row(self, j, half, k, t):
        if j == 1:
            return self.own[half][k, t]
        refs = self.near[half]
        v = refs[0][k, t]
        if refs[1] is not refs[0]:
            other, first = refs[1][k, t], self.from_first[half]
            v = jnp.where(first, v, other) if j == 0 else jnp.where(first, other, v)
        return jnp.where(self.there[j], v, 0.0)

    def field(self, j, f, x, t):
        return self.row(j, f // 2, f % 2 * PLANES + x, t)

    def kind(self, j, x, t):
        return self.row(j, 0, 2 * PLANES + x - 1, t) if x in (1, 2) else self.row(j, 1, 2 * PLANES, t)


def inside(space_size, p):
    x = (lax.axis_index("space") - 1) * PLANES + p
    return (x >= 0) & (x < space_size * PLANES)


def fine_load(slabs, sides, even):
    for j in sides:
        for x in range(PLANES):
            for f in range(FIELDS):
                for t in range(TILES):
                    put_tile(even, f, j * PLANES + x, t, slabs.field(j, f, x, t))


def fine_planes(space_size, spans, even, odd, keep, finish, source=None):
    for step, span in enumerate(spans):
        src, dst = (even, odd) if step % 2 == 0 else (odd, even)

        def read(p, src=src, step=step):
            found = source(step, p) if source else None
            return src if found is None else found

        for p in span:
            if step == ROUND - 1:
                store = lambda f, t, value: finish(f, p - PLANES, t, value)
            else:
                store = lambda f, t, value: put_tile(dst, f, p, t, value)
            fine_plane(read, keep, p, inside(space_size, p), store)


def fine_round(space_size, slabs, even, odd, keep, finish):
    fine_load(slabs, range(3), even)
    spans = [range(step + 1, WINDOW - 1 - step) for step in range(ROUND)]
    fine_planes(space_size, spans, even, odd, keep, finish)


def both_ways(space_size, run):
    low = lax.axis_index("space") < turn(space_size)
    pl.when(low)(lambda: run(False))
    pl.when(jnp.logical_not(low))(lambda: run(True))


def seen(span, mirror):
    return [WINDOW - 1 - p for p in span] if mirror else list(span)


def early_kernel(space_size, own_one, own_two, inner, outer, x, keep, even, odd):
    slabs = Slabs(space_size, (own_one, own_two), (inner, outer, x, x))

    def run(mirror):
        fine_load(slabs, (2 if mirror else 0, 1), even)
        spans = [seen(range(1 + step, 2 * PLANES - 1 - step), mirror) for step in range(ROUND - 1)]
        fine_planes(space_size, spans, even, odd, keep, None)

    both_ways(space_size, run)


def late_round(space_size, slabs, early_even, early_odd, even, odd, keep, finish):
    def run(mirror):
        fine_load(slabs, (0 if mirror else 2,), even)
        spans = [seen(range(2 * PLANES - 1 - step, WINDOW - 1 - step), mirror) for step in range(ROUND)]

        def source(step, p):
            before = seen(range(2 * PLANES - step), mirror)
            return (early_even if step % 2 == 0 else early_odd) if p in before else None

        fine_planes(space_size, spans, even, odd, keep, finish, source)

    both_ways(space_size, run)


def first_kernel(space_size, own_one, own_two, own_other, inner, outer, x, y, ended_one, ended_two, keep, even, odd):
    slabs = Slabs(space_size, (own_one, own_two), (inner, outer, x, y))
    for p in range(1, WINDOW - 1):
        j, k = p // PLANES, p % PLANES
        scale = jnp.where(inside(space_size, p), fine_dt, 0.0).astype(F32)
        for t in range(TILES):
            kind = slabs.kind(j, k, t)
            if j == 1 and k in (0, PLANES - 1):
                other = own_other[2 * PLANES, t]
                kind = jnp.where(slabs.low == (k == 0), other, kind)
            keep[0, p, t] = jnp.where(kind != 1.0, scale, 0.0)
            keep[1, p, t] = jnp.where(kind != 2.0, scale, 0.0)

    def finish(f, x, t, value):
        ended = ended_one if f < 2 else ended_two
        ended[f % 2 * PLANES + x, t] = value

    fine_round(space_size, slabs, even, odd, keep, finish)


def chosen(values, picks):
    parts, rest = [], values
    for _ in range(3):
        part = rest.astype(jnp.bfloat16)
        parts.append(part)
        rest = rest - part.astype(F32)
    stacked = jnp.concatenate(parts, axis=1)
    picks = jnp.concatenate([picks.astype(jnp.bfloat16)] * 3, axis=0)
    return jnp.dot(stacked, picks, preferred_element_type=F32)


def coarse_rows(pair_of, count):
    pairs = count // 2
    pieces = []
    for k in range(pairs):
        for i in range(TILES // 2):
            pieces.append(pair_of(k, 2 * i) + pair_of(k, 2 * i + 1))
    stacked = jnp.concatenate(pieces, axis=0)
    gather = (iota((NZ, NZ), 0) // 16 == iota((NZ, NZ), 1) % 8).astype(F32)
    sums = chosen(stacked, gather)
    sums = sums * pick_rows(sums.shape)
    sums = sums.reshape(pairs, TILES // 2, 8, NZ)
    sums = (sums[:, 0] + sums[:, 1]) + (sums[:, 2] + sums[:, 3])
    return sums.reshape(pairs * 8, NZ)


def pick_rows(shape):
    row = iota(shape, 0)
    return (row % 8 % 4 * 4 + row // 8 % 4 == iota(shape, 1) // 8).astype(F32)


def halves(sums, rows):
    shape = (rows, sums.shape[0])
    add = (iota(shape, 0) == iota(shape, 1) // 4).astype(F32) * (1.0 / 64.0)
    return jnp.dot(add, sums, precision=HIGHEST, preferred_element_type=F32)


def row_shift(v, by):
    rows = v.shape[0]
    row = iota(v.shape, 0)
    rolled = pltpu.roll(v, (-by) % rows, 0)
    return jnp.where((row + by >= 0) & (row + by < rows), rolled, 0.0)


def coarse_neighbours(v):
    row = iota(v.shape, 0)
    lane = iota(v.shape, 1)
    lo_x, hi_x = row_shift(v, -2), row_shift(v, 2)
    up = pltpu.roll(v, NZ - 8, 1)
    hi_y = jnp.where(lane < NZ - 8, up, jnp.where(row % 2 == 0, row_shift(up, 1), 0.0))
    down = pltpu.roll(v, 8, 1)
    lo_y = jnp.where(lane >= 8, down, jnp.where(row % 2 == 1, row_shift(down, -1), 0.0))
    hi_z = jnp.where(lane % 8 == 7, 0.0, pltpu.roll(v, NZ - 1, 1))
    lo_z = jnp.where(lane % 8 == 0, 0.0, pltpu.roll(v, 1, 1))
    return lo_x, hi_x, lo_y, hi_y, lo_z, hi_z


def coarse_step(state):
    near = [coarse_neighbours(v) for v in state]
    w, a, b, c = state

    def lap(f):
        lo_x, hi_x, lo_y, hi_y, lo_z, hi_z = near[f]
        return (0.25 * ((lo_x + hi_x) + (lo_y + hi_y)) + (1.0 / 256.0) * (lo_z + hi_z)) - (1.0 + 2.0 / 256.0) * state[f]

    def grad(f, k):
        return (near[f][2 * k + 1] - near[f][2 * k]) * (1.0 / 32.0 if k == 2 else 0.25)

    gx, gy, gz = grad(0, 0), grad(0, 1), grad(0, 2)
    diverge = grad(1, 0) + grad(2, 1) + grad(3, 2)
    new_w = w + coarse_dt * (lap(0) + 0.5 * diverge)
    new_a = a + coarse_dt * (gx + a * gz - a + lap(1))
    new_b = b + coarse_dt * (gy + b * gz - b + lap(2))
    new_c = c + coarse_dt * (2.0 * (gx * a + gy * b + gz * c) - (c - 1.0) + lap(3))
    return new_w, new_a, new_b, new_c


def guess_kernel(space_size, own_one, own_two, inner, outer, x, y, guess):
    place = lax.axis_index("space")
    slabs = Slabs(space_size, (own_one, own_two), (inner, outer, x, y))
    rows = 16
    row = iota((rows, NZ), 0)
    plane = 2 * place - 2 + row // 2
    valid = (row < WINDOW) & (plane >= 0) & (plane < 2 * space_size)
    state = []
    for f in range(FIELDS):

        def pair_of(k, t, f=f):
            return slabs.field(k // 2, f, k % 2 * 2, t) + slabs.field(k // 2, f, k % 2 * 2 + 1, t)

        grid = halves(coarse_rows(pair_of, WINDOW), rows)
        state.append(grid * 2.0 if f == 0 else grid)
    for _ in range(COARSE_STEPS):
        state = [jnp.where(valid, v, 0.0) for v in coarse_step(state)]
    for f in range(FIELDS):
        guess[pl.ds(4 * f, 4), :] = state[f][4:8]


def second_kernel(space_size, inner, outer, y, keep, guess, early_even, early_odd, fine_end, jump, even, odd):
    slabs = Slabs(space_size, None, (inner, outer, y, y))

    def finish(f, x, t, value):
        fine_end[f * PLANES + x, t] = value * 2.0 if f == 0 else value

    late_round(space_size, slabs, early_even, early_odd, even, odd, keep, finish)
    ended = halves(coarse_rows(lambda k, t: fine_end[2 * k, t] + fine_end[2 * k + 1, t], PACKED), PACKED)
    jumped = ended - jnp.where(lax.axis_index("tm") == 0, 0.0, guess[...])
    for k in range(jump.shape[0]):
        jump[k] = jumped


def correct_kernel(jumps, others, guess, fine_end, out, grids, result, sems):
    slices, space_size = jumps.shape[0] + 1, jumps.shape[1] * 2
    mine = lax.axis_index("tm")
    place = lax.axis_index("space")
    rows = grids.shape[2]
    centre = 4 * slices
    plane = 2 * (place - slices) + iota((rows, NZ), 0) // 2
    valid = (plane >= 0) & (plane < 2 * space_size)
    grids[...] = jnp.zeros_like(grids)
    for k in range(1, slices):
        m = jnp.maximum(mine - k, 0)
        for j in range(-k, k + 1):
            s = jnp.clip(place + j, 0, space_size - 1)
            source = jumps if j % 2 == 0 else others
            for f in range(FIELDS):
                grids[k - 1, f, pl.ds(centre + 4 * j, 4), :] = source[m, s // 2, pl.ds(4 * f, 4), :]
    state = None
    for k in range(slices - 1, -1, -1):
        ended = state
        if state is not None:
            for _ in range(COARSE_STEPS):
                ended = [jnp.where(valid, v, 0.0) for v in coarse_step(ended)]
        if k > 0:
            state = [jnp.where(valid, grids[k - 1, f], 0.0) for f in range(FIELDS)]
            if ended is not None:
                state = [state[f] + jnp.where(mine > k, ended[f], 0.0) for f in range(FIELDS)]
    row = iota((8, NZ), 0)
    pieces = []
    for f in range(FIELDS):
        for x in range(PLANES // 2):
            k = 2 * x
            lines = [
                ended[f][centre + k + half : centre + k + half + 1] - guess[pl.ds(4 * f + k + half, 1), :]
                for half in range(2)
            ]
            tile = jnp.where(row < 4, lines[0], lines[1])
            tile = jnp.where(mine == 0, 0.0, tile)
            pieces += [tile] * (TILES // 2)
    stacked = jnp.concatenate(pieces, axis=0)
    stacked = stacked * pick_rows(stacked.shape)
    spread = (iota((NZ, NZ), 0) % 8 == iota((NZ, NZ), 1) // 16).astype(F32)
    wide = chosen(stacked, spread)
    for f in range(FIELDS):
        for x in range(PLANES):
            for t in range(TILES):
                k = ((f * 2 + x // 2) * (TILES // 2) + t // 2) * 8
                result[f, x, pl.ds(t, 8, stride=8), :] = fine_end[f * PLANES + x, t] + wide[k : k + 8]
        pltpu.make_async_copy(result.at[f], out.at[0, f], sems.at[f]).start()
    for f in range(FIELDS):
        pltpu.make_async_copy(result.at[f], out.at[0, f], sems.at[f]).wait()


def relayed(size):
    return size == 8


def turn(size):
    return size // 2 if relayed(size) else size


def exchange(one, two_x, two_y, size):
    inner = [(i, i ^ 1) for i in range(size)]
    outer = [(0, 0)] + [(i, (i - 1 ^ 1) + 1) for i in range(1, size - 1)] + [(size - 1, size - 1)]
    if relayed(size):
        half = size // 2
        first = [(i, i + 1) for i in range(half - 1)] + [(half - 1, size - 1)]
        first += [(i, i - 1) for i in range(size - 1, half, -1)] + [(half, 0)]
        second = [(i, i - 1) for i in range(half - 1, 0, -1)] + [(0, half - 1)]
        second += [(i, i + 1) for i in range(half, size - 1)] + [(size - 1, half)]
    else:
        first = [(i, (i + 1) % size) for i in range(size)]
        second = [(i, (i - 1) % size) for i in range(size)]
    x = lax.ppermute(two_x, "space", first)
    across = lax.ppermute(one, "space", outer)
    within = lax.ppermute(one, "space", inner)
    if relayed(size):
        place = lax.axis_index("space")
        two_y = jnp.where((place == 0) | (place == size - 1), x, two_y)
    y = lax.ppermute(two_y, "space", second)
    return within, across, x, y


def shaped(*shape):
    return jax.ShapeDtypeStruct(shape, F32)


def local(slices, space_size, starts, flags):
    half = shaped(2 * PLANES, TILES, 8, NZ)
    message_one, message_two = shaped(2 * PLANES + 2, TILES, 8, NZ), shaped(2 * PLANES + 1, TILES, 8, NZ)
    keep_shape = shaped(2, WINDOW, TILES, 8, NZ)
    buffers = [pltpu.VMEM((FIELDS, WINDOW, TILES + 2, 8, NZ), F32)] * 2
    opening = pl.pallas_call(
        functools.partial(prepare_kernel, space_size),
        out_shape=(message_one, message_two, message_two),
        in_specs=[pl.BlockSpec(memory_space=pltpu.HBM)] * 2,
        out_specs=(VMEM,) * 3,
        scratch_shapes=[
            pltpu.VMEM(starts.shape, F32),
            pltpu.VMEM(flags.shape, flags.dtype),
            pltpu.SemaphoreType.DMA((2,)),
        ],
        compiler_params=params(),
        name="prepare",
    )(starts, flags)
    opening_near = exchange(*opening, space_size)
    *middle, keep = pl.pallas_call(
        functools.partial(first_kernel, space_size),
        out_shape=(half, half, keep_shape),
        in_specs=[VMEM] * 7,
        out_specs=(VMEM,) * 3,
        scratch_shapes=buffers,
        compiler_params=params(),
        name="first_round",
    )(*opening, *opening_near)
    middle_near = exchange(middle[0], middle[1], middle[1], space_size)
    guess = pl.pallas_call(
        functools.partial(guess_kernel, space_size),
        out_shape=shaped(PACKED, NZ),
        in_specs=[VMEM] * 6,
        out_specs=VMEM,
        compiler_params=params(),
        name="guess_old",
    )(*opening[:2], *opening_near)
    inner, outer, x, y = middle_near
    buffer = shaped(FIELDS, WINDOW, TILES + 2, 8, NZ)
    early = pl.pallas_call(
        functools.partial(early_kernel, space_size),
        out_shape=(buffer, buffer),
        in_specs=[VMEM] * 6,
        out_specs=(VMEM, VMEM),
        compiler_params=params(),
        name="second_round_early",
    )(*middle, inner, outer, x, keep)
    fine_end, jump = pl.pallas_call(
        functools.partial(second_kernel, space_size),
        out_shape=(shaped(PACKED, TILES, 8, NZ), shaped(slices * space_size // 2, PACKED, NZ)),
        in_specs=[VMEM] * 7,
        out_specs=(VMEM, VMEM),
        scratch_shapes=buffers,
        compiler_params=params(),
        name="second_round",
    )(inner, outer, y, keep, guess, *early)
    members = [range(core, slices * space_size, 2) for core in range(2)]
    jumps = lax.all_to_all(jump, ("tm", "space"), 0, 0, axis_index_groups=[list(group) for group in members])
    jumps = jumps.reshape(slices, space_size // 2, PACKED, NZ)[: slices - 1]
    others = lax.ppermute(jumps, "space", [(i, i ^ 1) for i in range(space_size)])
    return pl.pallas_call(
        correct_kernel,
        out_shape=shaped(1, FIELDS, PLANES, NY, NZ),
        in_specs=[VMEM] * 4,
        out_specs=pl.BlockSpec(memory_space=pltpu.HBM),
        scratch_shapes=[
            pltpu.VMEM((slices - 1, FIELDS, 8 * slices, NZ), F32),
            pltpu.VMEM((FIELDS, PLANES, NY, NZ), F32),
            pltpu.SemaphoreType.DMA((FIELDS,)),
        ],
        compiler_params=params(),
        name="correct",
    )(jumps, others, guess, fine_end)


def solution(mesh):
    return jax.shard_map(
        functools.partial(local, mesh.shape["tm"], mesh.shape["space"]),
        mesh=mesh,
        in_specs=(P("tm", None, "space", None, None), P("space", None, None)),
        out_specs=P("tm", None, "space", None, None),
        check_vma=False,
    )
```

```python
import functools

import jax
import jax.numpy as jnp
from jax import lax
from jax.experimental import pallas as pl
from jax.experimental.pallas import tpu as pltpu
from jax.sharding import PartitionSpec as P

FINE_STEPS = 8
COARSE_STEPS = 2

fine_dt = 0.12
coarse_dt = 0.48

FIELDS = 4
PLANES = 4
NY = 64
NZ = 128
ROUND = 4
WINDOW = 3 * PLANES
TILES = NY // 8
GROUP = 4
PACKED = FIELDS * PLANES
F32 = jnp.float32
HIGHEST = lax.Precision.HIGHEST
VMEM = pl.BlockSpec(memory_space=pltpu.VMEM)
LIMIT = 48 * 2**20


def iota(shape, dim):
    return lax.broadcasted_iota(jnp.int32, shape, dim)


def params():
    return pltpu.CompilerParams(vmem_limit_bytes=LIMIT)


def prepare_kernel(space_size, starts, flags, one, two_x, two_y, fields, kinds, sems):
    low = lax.axis_index("space") < turn(space_size)
    copies = [pltpu.make_async_copy(starts, fields, sems.at[0]), pltpu.make_async_copy(flags, kinds, sems.at[1])]
    for copy in copies:
        copy.start()
    for copy in copies:
        copy.wait()
    for t in range(TILES):
        for f in range(FIELDS):
            for x in range(PLANES):
                v = fields[0, f, x, pl.ds(t, 8, stride=8), :]
                for message in (one,) if f < 2 else (two_x, two_y):
                    message[f % 2 * PLANES + x, t] = v * 0.5 if f == 0 else v
        kind = [kinds[x, pl.ds(t, 8, stride=8), :].astype(F32) for x in range(PLANES)]
        one[2 * PLANES, t], one[2 * PLANES + 1, t] = kind[1], kind[2]
        two_x[2 * PLANES, t] = jnp.where(low, kind[3], kind[0])
        two_y[2 * PLANES, t] = jnp.where(low, kind[0], kind[3])


def fine_tile(mid, lo_x, hi_x, lo_y, hi_y, kv, ks, kc, low_lane, high_lane):
    beta = 1.0 / fine_dt - 7.0
    alpha = 1.0 / fine_dt - 6.0
    lo_z = [jnp.where(low_lane, 0.0, pltpu.roll(v, 1, 1)) for v in mid]
    hi_z = [jnp.where(high_lane, 0.0, pltpu.roll(v, NZ - 1, 1)) for v in mid]
    total = [((lo_x[f] + hi_x[f]) + (lo_y[f] + hi_y[f])) + (lo_z[f] + hi_z[f]) for f in range(FIELDS)]
    w, a, b, c = mid
    gx = hi_x[0] - lo_x[0]
    gy = hi_y[0] - lo_y[0]
    gz = hi_z[0] - lo_z[0]
    diverge = (hi_x[1] - lo_x[1]) + (hi_y[2] - lo_y[2]) + (hi_z[3] - lo_z[3])
    stretch = gz + beta
    new_w = kv * ((total[0] + 0.125 * diverge) + alpha * w)
    new_a = ks * ((total[1] + gx) + a * stretch)
    new_b = ks * ((total[2] + gy) + b * stretch)
    new_c = kc * ((total[3] + 2.0 * (gx * a + gy * b)) + ((stretch + gz) * c + 1.0))
    return new_w, new_a, new_b, new_c


def fine_plane(src, keep, p, valid, store):
    lane = iota((8, NZ), 1)
    low_lane, high_lane = lane == 0, lane == NZ - 1
    fields = range(FIELDS)
    kc = jnp.where(valid, fine_dt, 0.0).astype(F32)
    for begin in range(0, TILES, GROUP):
        tiles = range(begin, begin + GROUP)
        column = [[src(p)[f, p, t] for f in fields] for t in range(begin, begin + GROUP + 2)]
        lo_x = [[src(p - 1)[f, p - 1, t + 1] for f in fields] for t in tiles]
        hi_x = [[src(p + 1)[f, p + 1, t + 1] for f in fields] for t in tiles]
        kept = [(keep[0, p, t], keep[1, p, t]) for t in tiles]
        fresh = [
            fine_tile(column[i + 1], lo_x[i], hi_x[i], column[i], column[i + 2], *kept[i], kc, low_lane, high_lane)
            for i in range(GROUP)
        ]
        for i, t in enumerate(tiles):
            for f in fields:
                store(f, t, fresh[i][f])


def put_tile(buffer, f, p, t, value):
    buffer[f, p, t + 1] = value
    row = iota((8, NZ), 0)
    if t == 0:
        buffer[f, p, TILES + 1] = jnp.where(row == 7, 0.0, pltpu.roll(value, 7, 0))
    if t == TILES - 1:
        buffer[f, p, 0] = jnp.where(row == 0, 0.0, pltpu.roll(value, 1, 0))


class Slabs:

    def __init__(self, space_size, own, near):
        place = lax.axis_index("space")
        self.own = own
        self.near = (near[:2], near[2:])
        self.low = place < turn(space_size)
        self.from_first = (place % 2 == 1, self.low)
        self.there = {0: place > 0, 2: place < space_size - 1}

    def row(self, j, half, k, t):
        if j == 1:
            return self.own[half][k, t]
        refs = self.near[half]
        v = refs[0][k, t]
        if refs[1] is not refs[0]:
            other, first = refs[1][k, t], self.from_first[half]
            v = jnp.where(first, v, other) if j == 0 else jnp.where(first, other, v)
        return jnp.where(self.there[j], v, 0.0)

    def field(self, j, f, x, t):
        return self.row(j, f // 2, f % 2 * PLANES + x, t)

    def kind(self, j, x, t):
        return self.row(j, 0, 2 * PLANES + x - 1, t) if x in (1, 2) else self.row(j, 1, 2 * PLANES, t)


def inside(space_size, p):
    x = (lax.axis_index("space") - 1) * PLANES + p
    return (x >= 0) & (x < space_size * PLANES)


def fine_load(slabs, sides, even):
    for j in sides:
        for x in range(PLANES):
            for f in range(FIELDS):
                for t in range(TILES):
                    put_tile(even, f, j * PLANES + x, t, slabs.field(j, f, x, t))


def fine_planes(space_size, spans, even, odd, keep, finish, source=None):
    for step, span in enumerate(spans):
        src, dst = (even, odd) if step % 2 == 0 else (odd, even)

        def read(p, src=src, step=step):
            found = source(step, p) if source else None
            return src if found is None else found

        for p in span:
            if step == ROUND - 1:
                store = lambda f, t, value: finish(f, p - PLANES, t, value)
            else:
                store = lambda f, t, value: put_tile(dst, f, p, t, value)
            fine_plane(read, keep, p, inside(space_size, p), store)


def both_ways(mirror, run):
    pl.when(jnp.logical_not(mirror))(lambda: run(False))
    pl.when(mirror)(lambda: run(True))


def seen(span, mirror):
    return [WINDOW - 1 - p for p in span] if mirror else list(span)


def early_kernel(space_size, own_one, own_two, inner, outer, x, keep, even, odd):
    slabs = Slabs(space_size, (own_one, own_two), (inner, outer, x, x))

    def run(mirror):
        fine_load(slabs, (2 if mirror else 0, 1), even)
        spans = [seen(range(1 + step, 2 * PLANES - 1 - step), mirror) for step in range(ROUND - 1)]
        fine_planes(space_size, spans, even, odd, keep, None)

    both_ways(jnp.logical_not(slabs.low), run)


def late_round(space_size, slabs, mirrored, early_even, early_odd, even, odd, keep, finish):
    def run(mirror):
        fine_load(slabs, (0 if mirror else 2,), even)
        spans = [seen(range(2 * PLANES - 1 - step, WINDOW - 1 - step), mirror) for step in range(ROUND)]

        def source(step, p):
            before = seen(range(2 * PLANES - step), mirror)
            return (early_even if step % 2 == 0 else early_odd) if p in before else None

        fine_planes(space_size, spans, even, odd, keep, finish, source)

    both_ways(mirrored, run)


def keep_factors(space_size, slabs, own_other, planes, keep):
    for p in planes:
        j, k = p // PLANES, p % PLANES
        scale = jnp.where(inside(space_size, p), fine_dt, 0.0).astype(F32)
        for t in range(TILES):
            kind = slabs.kind(j, k, t)
            if j == 1 and k in (0, PLANES - 1):
                other = own_other[2 * PLANES, t]
                kind = jnp.where(slabs.low == (k == 0), other, kind)
            keep[0, p, t] = jnp.where(kind != 1.0, scale, 0.0)
            keep[1, p, t] = jnp.where(kind != 2.0, scale, 0.0)


def first_early_kernel(space_size, own_one, own_two, own_other, inner, x, y, keep, even, odd):
    slabs = Slabs(space_size, (own_one, own_two), (inner, inner, x, y))

    def run(mirror):
        fine_load(slabs, (2 if mirror else 0, 1), even)
        keep_factors(space_size, slabs, own_other, seen(range(1, 2 * PLANES), mirror), keep)
        spans = [seen(range(1 + step, 2 * PLANES - 1 - step), mirror) for step in range(ROUND - 1)]
        fine_planes(space_size, spans, even, odd, keep, None)

    both_ways(lax.axis_index("space") % 2 == 0, run)


def first_kernel(space_size, outer, x, y, early_keep, early_even, early_odd, ended_one, ended_two, keep, even, odd):
    slabs = Slabs(space_size, None, (outer, outer, x, y))
    mirrored = lax.axis_index("space") % 2 == 0

    def fill(mirror):
        for p in seen(range(1, 2 * PLANES), mirror):
            for k in range(2):
                keep[k, p] = early_keep[k, p]
        keep_factors(space_size, slabs, None, seen(range(2 * PLANES, WINDOW - 1), mirror), keep)

    def finish(f, x, t, value):
        ended = ended_one if f < 2 else ended_two
        ended[f % 2 * PLANES + x, t] = value

    both_ways(mirrored, fill)
    late_round(space_size, slabs, mirrored, early_even, early_odd, even, odd, keep, finish)


def chosen(values, picks):
    parts, rest = [], values
    for _ in range(3):
        part = rest.astype(jnp.bfloat16)
        parts.append(part)
        rest = rest - part.astype(F32)
    stacked = jnp.concatenate(parts, axis=1)
    picks = jnp.concatenate([picks.astype(jnp.bfloat16)] * 3, axis=0)
    return jnp.dot(stacked, picks, preferred_element_type=F32)


def coarse_rows(pair_of, count):
    pairs = count // 2
    pieces = []
    for k in range(pairs):
        for i in range(TILES // 2):
            pieces.append(pair_of(k, 2 * i) + pair_of(k, 2 * i + 1))
    stacked = jnp.concatenate(pieces, axis=0)
    gather = (iota((NZ, NZ), 0) // 16 == iota((NZ, NZ), 1) % 8).astype(F32)
    sums = chosen(stacked, gather)
    sums = sums * pick_rows(sums.shape)
    sums = sums.reshape(pairs, TILES // 2, 8, NZ)
    sums = (sums[:, 0] + sums[:, 1]) + (sums[:, 2] + sums[:, 3])
    return sums.reshape(pairs * 8, NZ)


def pick_rows(shape):
    row = iota(shape, 0)
    return (row % 8 % 4 * 4 + row // 8 % 4 == iota(shape, 1) // 8).astype(F32)


def halves(sums, rows):
    shape = (rows, sums.shape[0])
    add = (iota(shape, 0) == iota(shape, 1) // 4).astype(F32) * (1.0 / 64.0)
    return jnp.dot(add, sums, precision=HIGHEST, preferred_element_type=F32)


def row_shift(v, by):
    rows = v.shape[0]
    row = iota(v.shape, 0)
    rolled = pltpu.roll(v, (-by) % rows, 0)
    return jnp.where((row + by >= 0) & (row + by < rows), rolled, 0.0)


def coarse_neighbours(v):
    row = iota(v.shape, 0)
    lane = iota(v.shape, 1)
    lo_x, hi_x = row_shift(v, -2), row_shift(v, 2)
    up = pltpu.roll(v, NZ - 8, 1)
    hi_y = jnp.where(lane < NZ - 8, up, jnp.where(row % 2 == 0, row_shift(up, 1), 0.0))
    down = pltpu.roll(v, 8, 1)
    lo_y = jnp.where(lane >= 8, down, jnp.where(row % 2 == 1, row_shift(down, -1), 0.0))
    hi_z = jnp.where(lane % 8 == 7, 0.0, pltpu.roll(v, NZ - 1, 1))
    lo_z = jnp.where(lane % 8 == 0, 0.0, pltpu.roll(v, 1, 1))
    return lo_x, hi_x, lo_y, hi_y, lo_z, hi_z


def coarse_step(state):
    near = [coarse_neighbours(v) for v in state]
    w, a, b, c = state

    def lap(f):
        lo_x, hi_x, lo_y, hi_y, lo_z, hi_z = near[f]
        return (0.25 * ((lo_x + hi_x) + (lo_y + hi_y)) + (1.0 / 256.0) * (lo_z + hi_z)) - (1.0 + 2.0 / 256.0) * state[f]

    def grad(f, k):
        return (near[f][2 * k + 1] - near[f][2 * k]) * (1.0 / 32.0 if k == 2 else 0.25)

    gx, gy, gz = grad(0, 0), grad(0, 1), grad(0, 2)
    diverge = grad(1, 0) + grad(2, 1) + grad(3, 2)
    new_w = w + coarse_dt * (lap(0) + 0.5 * diverge)
    new_a = a + coarse_dt * (gx + a * gz - a + lap(1))
    new_b = b + coarse_dt * (gy + b * gz - b + lap(2))
    new_c = c + coarse_dt * (2.0 * (gx * a + gy * b + gz * c) - (c - 1.0) + lap(3))
    return new_w, new_a, new_b, new_c


def guess_kernel(space_size, own_one, own_two, inner, outer, x, y, guess):
    place = lax.axis_index("space")
    slabs = Slabs(space_size, (own_one, own_two), (inner, outer, x, y))
    rows = 16
    row = iota((rows, NZ), 0)
    plane = 2 * place - 2 + row // 2
    valid = (row < WINDOW) & (plane >= 0) & (plane < 2 * space_size)
    state = []
    for f in range(FIELDS):

        def pair_of(k, t, f=f):
            return slabs.field(k // 2, f, k % 2 * 2, t) + slabs.field(k // 2, f, k % 2 * 2 + 1, t)

        grid = halves(coarse_rows(pair_of, WINDOW), rows)
        state.append(grid * 2.0 if f == 0 else grid)
    for _ in range(COARSE_STEPS):
        state = [jnp.where(valid, v, 0.0) for v in coarse_step(state)]
    for f in range(FIELDS):
        guess[pl.ds(4 * f, 4), :] = state[f][4:8]


def second_kernel(space_size, inner, outer, y, keep, guess, early_even, early_odd, fine_end, jump, even, odd):
    slabs = Slabs(space_size, None, (inner, outer, y, y))

    def finish(f, x, t, value):
        fine_end[f * PLANES + x, t] = value * 2.0 if f == 0 else value

    late_round(space_size, slabs, jnp.logical_not(slabs.low), early_even, early_odd, even, odd, keep, finish)
    ended = halves(coarse_rows(lambda k, t: fine_end[2 * k, t] + fine_end[2 * k + 1, t], PACKED), PACKED)
    jumped = ended - jnp.where(lax.axis_index("tm") == 0, 0.0, guess[...])
    for k in range(jump.shape[0]):
        jump[k] = jumped


def correct_kernel(jumps, others, guess, fine_end, out, grids, result, sems):
    slices, space_size = jumps.shape[0] + 1, jumps.shape[1] * 2
    mine = lax.axis_index("tm")
    place = lax.axis_index("space")
    rows = grids.shape[2]
    centre = 4 * slices
    plane = 2 * (place - slices) + iota((rows, NZ), 0) // 2
    valid = (plane >= 0) & (plane < 2 * space_size)
    grids[...] = jnp.zeros_like(grids)
    for k in range(1, slices):
        m = jnp.maximum(mine - k, 0)
        for j in range(-k, k + 1):
            s = jnp.clip(place + j, 0, space_size - 1)
            source = jumps if j % 2 == 0 else others
            for f in range(FIELDS):
                grids[k - 1, f, pl.ds(centre + 4 * j, 4), :] = source[m, s // 2, pl.ds(4 * f, 4), :]
    state = None
    for k in range(slices - 1, -1, -1):
        ended = state
        if state is not None:
            for _ in range(COARSE_STEPS):
                ended = [jnp.where(valid, v, 0.0) for v in coarse_step(ended)]
        if k > 0:
            state = [jnp.where(valid, grids[k - 1, f], 0.0) for f in range(FIELDS)]
            if ended is not None:
                state = [state[f] + jnp.where(mine > k, ended[f], 0.0) for f in range(FIELDS)]
    row = iota((8, NZ), 0)
    pieces = []
    for f in range(FIELDS):
        for x in range(PLANES // 2):
            k = 2 * x
            lines = [
                ended[f][centre + k + half : centre + k + half + 1] - guess[pl.ds(4 * f + k + half, 1), :]
                for half in range(2)
            ]
            tile = jnp.where(row < 4, lines[0], lines[1])
            tile = jnp.where(mine == 0, 0.0, tile)
            pieces += [tile] * (TILES // 2)
    stacked = jnp.concatenate(pieces, axis=0)
    stacked = stacked * pick_rows(stacked.shape)
    spread = (iota((NZ, NZ), 0) % 8 == iota((NZ, NZ), 1) // 16).astype(F32)
    wide = chosen(stacked, spread)
    for f in range(FIELDS):
        for x in range(PLANES):
            for t in range(TILES):
                k = ((f * 2 + x // 2) * (TILES // 2) + t // 2) * 8
                result[f, x, pl.ds(t, 8, stride=8), :] = fine_end[f * PLANES + x, t] + wide[k : k + 8]
        pltpu.make_async_copy(result.at[f], out.at[0, f], sems.at[f]).start()
    for f in range(FIELDS):
        pltpu.make_async_copy(result.at[f], out.at[0, f], sems.at[f]).wait()


def relayed(size):
    return size == 8


def turn(size):
    return size // 2 if relayed(size) else size


def exchange(one, two_x, two_y, size):
    inner = [(i, i ^ 1) for i in range(size)]
    outer = [(0, 0)] + [(i, (i - 1 ^ 1) + 1) for i in range(1, size - 1)] + [(size - 1, size - 1)]
    if relayed(size):
        half = size // 2
        first = [(i, i + 1) for i in range(half - 1)] + [(half - 1, size - 1)]
        first += [(i, i - 1) for i in range(size - 1, half, -1)] + [(half, 0)]
        second = [(i, i - 1) for i in range(half - 1, 0, -1)] + [(0, half - 1)]
        second += [(i, i + 1) for i in range(half, size - 1)] + [(size - 1, half)]
    else:
        first = [(i, (i + 1) % size) for i in range(size)]
        second = [(i, (i - 1) % size) for i in range(size)]
    x = lax.ppermute(two_x, "space", first)
    across = lax.ppermute(one, "space", outer)
    within = lax.ppermute(one, "space", inner)
    if relayed(size):
        place = lax.axis_index("space")
        two_y = jnp.where((place == 0) | (place == size - 1), x, two_y)
    y = lax.ppermute(two_y, "space", second)
    return within, across, x, y


def shaped(*shape):
    return jax.ShapeDtypeStruct(shape, F32)


def local(slices, space_size, starts, flags):
    half = shaped(2 * PLANES, TILES, 8, NZ)
    message_one, message_two = shaped(2 * PLANES + 2, TILES, 8, NZ), shaped(2 * PLANES + 1, TILES, 8, NZ)
    keep_shape = shaped(2, WINDOW, TILES, 8, NZ)
    buffers = [pltpu.VMEM((FIELDS, WINDOW, TILES + 2, 8, NZ), F32)] * 2
    opening = pl.pallas_call(
        functools.partial(prepare_kernel, space_size),
        out_shape=(message_one, message_two, message_two),
        in_specs=[pl.BlockSpec(memory_space=pltpu.HBM)] * 2,
        out_specs=(VMEM,) * 3,
        scratch_shapes=[
            pltpu.VMEM(starts.shape, F32),
            pltpu.VMEM(flags.shape, flags.dtype),
            pltpu.SemaphoreType.DMA((2,)),
        ],
        compiler_params=params(),
        name="prepare",
    )(starts, flags)
    opening_near = exchange(*opening, space_size)
    inner, outer, x, y = opening_near
    buffer = shaped(FIELDS, WINDOW, TILES + 2, 8, NZ)
    early = pl.pallas_call(
        functools.partial(first_early_kernel, space_size),
        out_shape=(keep_shape, buffer, buffer),
        in_specs=[VMEM] * 6,
        out_specs=(VMEM,) * 3,
        compiler_params=params(),
        name="first_round_early",
    )(*opening, inner, x, y)
    *middle, keep = pl.pallas_call(
        functools.partial(first_kernel, space_size),
        out_shape=(half, half, keep_shape),
        in_specs=[VMEM] * 6,
        out_specs=(VMEM,) * 3,
        scratch_shapes=buffers,
        compiler_params=params(),
        name="first_round",
    )(outer, x, y, *early)
    middle_near = exchange(middle[0], middle[1], middle[1], space_size)
    guess = pl.pallas_call(
        functools.partial(guess_kernel, space_size),
        out_shape=shaped(PACKED, NZ),
        in_specs=[VMEM] * 6,
        out_specs=VMEM,
        compiler_params=params(),
        name="guess_old",
    )(*opening[:2], *opening_near)
    inner, outer, x, y = middle_near
    early = pl.pallas_call(
        functools.partial(early_kernel, space_size),
        out_shape=(buffer, buffer),
        in_specs=[VMEM] * 6,
        out_specs=(VMEM, VMEM),
        compiler_params=params(),
        name="second_round_early",
    )(*middle, inner, outer, x, keep)
    fine_end, jump = pl.pallas_call(
        functools.partial(second_kernel, space_size),
        out_shape=(shaped(PACKED, TILES, 8, NZ), shaped(slices * space_size // 2, PACKED, NZ)),
        in_specs=[VMEM] * 7,
        out_specs=(VMEM, VMEM),
        scratch_shapes=buffers,
        compiler_params=params(),
        name="second_round",
    )(inner, outer, y, keep, guess, *early)
    members = [range(core, slices * space_size, 2) for core in range(2)]
    jumps = lax.all_to_all(jump, ("tm", "space"), 0, 0, axis_index_groups=[list(group) for group in members])
    jumps = jumps.reshape(slices, space_size // 2, PACKED, NZ)[: slices - 1]
    others = lax.ppermute(jumps, "space", [(i, i ^ 1) for i in range(space_size)])
    return pl.pallas_call(
        correct_kernel,
        out_shape=shaped(1, FIELDS, PLANES, NY, NZ),
        in_specs=[VMEM] * 4,
        out_specs=pl.BlockSpec(memory_space=pltpu.HBM),
        scratch_shapes=[
            pltpu.VMEM((slices - 1, FIELDS, 8 * slices, NZ), F32),
            pltpu.VMEM((FIELDS, PLANES, NY, NZ), F32),
            pltpu.SemaphoreType.DMA((FIELDS,)),
        ],
        compiler_params=params(),
        name="correct",
    )(jumps, others, guess, fine_end)


def solution(mesh):
    return jax.shard_map(
        functools.partial(local, mesh.shape["tm"], mesh.shape["space"]),
        mesh=mesh,
        in_specs=(P("tm", None, "space", None, None), P("space", None, None)),
        out_specs=P("tm", None, "space", None, None),
        check_vma=False,
    )
```
